32 devices in a mesh: kv: 2 (over x), pg: 16 (over z, y, core).
Axes of the slice: x: 2, y: 2, z: 4, core: 2. Of those that a mesh axis runs over, the one named last changes fastest.
Arguments:
- residual_in: bfloat16 [1024, 1536], P('pg', 'kv'), as said below
- queries: bfloat16 [64, 1536], P('pg', 'kv'), as said below
- prefill_attn: bfloat16 [960, 1536], P('pg', 'kv'), may hold values from -1.1953125 to 1.1953125
- kv_cache: bfloat16 [256, 8, 128, 128], P('pg', 'kv'), as said below
- page_table: int32 [64, 4], replicated, may hold values from 0 to 255, as said below
- lengths: int32 [64], replicated, may hold values from 2 to 512, as said below
- out_weight: bfloat16 [1536, 1536], P('kv'), may hold values from -0.75 to 0.75
- norm_gain_in: float32 [1536], P('kv'), may hold values from 0.25 to 1.75
- norm_gain_out: float32 [1536], P('kv'), may hold values from 0.25 to 1.75
- expert_ids: int32 [1024, 8], P('pg'), may hold values from 0 to 39, all different within a row; in each aligned block of 64 rows (0 to 63, 64 to 127, ...) at most 16 rows name the same one
- route_weight: float32 [1024, 8], P('pg'), may hold values from 0.05 to 1
- slot_table: int32 [40, 2], replicated, may hold values from 0 to 47, as said below
- w_gate_up: bfloat16 [48, 1536, 1024], P('pg', 'kv'), as said below
- w_down: bfloat16 [48, 512, 1536], P('pg', None, 'kv'), as said below
Outputs:
- layer_out: bfloat16 [1024, 1536], P('pg', 'kv')
The draws below stay inside these ranges and needn't reach their ends.
Inputs may be any that keep to these rules, and one draw needn't show every extreme that they name: `page_table`: every page of 0 to 255 appears exactly once in the table. `lengths`: some request has exactly 512 cached tokens. `slot_table`: row e lists the slots of expert e; each slot of 0 to 47 belongs to exactly one expert; an expert with a single slot repeats it. `w_gate_up`: slots of the same expert carry equal weights; entries lie within -0.2 and 0.2. `w_down`: slots of the same expert carry equal weights; entries lie within -0.3 and 0.3. `queries`: entries lie within -60 and 60. `kv_cache`: entries lie within -6 and 6. `residual_in`: entries lie within -50 and 50. `expert_ids`: in each aligned block of 64 rows no expert is named more than 16 times.
All inputs are finite; a program needn't handle non-finite values.
Results may differ from the reference program's by a relative error of at most 0.02.
Values may be sent and summed in bfloat16 or wider, within the bound.
No kernel may reach another device: no remote copies, remote signals or barrier semaphores. Data moves between devices by JAX's collectives and lax.ppermute only.
A program may use at most 128 MiB of HBM per device.

```python
import math
import jax
import jax.numpy as jnp
import numpy as np
from jax import lax

D = 1536
QUERY_HEADS = 24
KEY_VALUE_HEADS = 8
HEAD_SIZE = 64
EXPERT_COUNT = 40
FF = 512
TOPK = 8
PAGE_TOKENS = 128
MAXP = 4
RMAX = 2
REQ_DEV = 4
PRE_DEV = 60
ROWS_DEV = 64
DECODE_REQUESTS = 64
PRE = 960
TOKENS = 1024
CACHE_PAGES = 256
EXPERT_SLOTS = 48
CAP = 16
N_KV = 2
N_PG = 16


def page_layout(key):
    sort_order = jax.random.permutation(jax.random.fold_in(key, 11), CACHE_PAGES)
    return sort_order.reshape(DECODE_REQUESTS, MAXP).astype(jnp.int32)


def draw_page_table(key, part):
    return page_layout(key)


def draw_lengths(key, part):
    base = jax.random.randint(jax.random.fold_in(key, 12), (DECODE_REQUESTS,), 2, MAXP * PAGE_TOKENS + 1)
    longest = jax.random.randint(jax.random.fold_in(key, 13), (), 0, DECODE_REQUESTS)
    return base.at[longest].set(MAXP * PAGE_TOKENS).astype(jnp.int32)


def cache_values(key):
    array_shape = (CACHE_PAGES, KEY_VALUE_HEADS, PAGE_TOKENS, 2 * HEAD_SIZE)
    cache = jnp.clip(jax.random.normal(jax.random.fold_in(key, 21), array_shape, jnp.float32), -6.0, 6.0)
    return cache


def draw_kv_cache(key, part):
    return cache_values(key).astype(jnp.bfloat16)


def draw_queries(key, part):
    array_shape = (DECODE_REQUESTS, QUERY_HEADS * HEAD_SIZE)
    return (2.0 * jnp.clip(jax.random.normal(jax.random.fold_in(key, 22), array_shape, jnp.float32), -6.0, 6.0)).astype(jnp.bfloat16)


def draw_residual_in(key, part):
    row_scale = jnp.exp(jax.random.uniform(jax.random.fold_in(key, 41), (TOKENS, 1), jnp.float32, math.log(0.3), math.log(3.0)))
    column = jnp.arange(D, dtype=jnp.float32)[None, :] / D
    col_scale = 0.3 * jnp.exp(column * math.log(10.0)) * jnp.exp(jax.random.uniform(jax.random.fold_in(key, 42), (1, D), jnp.float32, -0.3, 0.3))
    noise = jnp.clip(jax.random.normal(jax.random.fold_in(key, 43), (TOKENS, D), jnp.float32), -4.0, 4.0)
    return (noise * row_scale * col_scale).astype(jnp.bfloat16)


def slot_layout(key):
    sort_order = jax.random.permutation(jax.random.fold_in(key, 31), EXPERT_SLOTS).astype(jnp.int32)
    additional = jax.random.permutation(jax.random.fold_in(key, 32), EXPERT_COUNT).astype(jnp.int32)
    slot_holders = jnp.concatenate([jnp.arange(EXPERT_COUNT, dtype=jnp.int32), additional[:EXPERT_SLOTS - EXPERT_COUNT]])
    expert_of_slot = jnp.zeros((EXPERT_SLOTS,), jnp.int32).at[sort_order].set(slot_holders)
    return (sort_order, additional, expert_of_slot)


def draw_slot_table(key, part):
    sort_order, additional, expert_of_slot = slot_layout(key)
    placement_index = jnp.argsort(additional, stable=True).astype(jnp.int32)
    primary_slot = sort_order[:EXPERT_COUNT]
    spare_slot = sort_order[jnp.clip(EXPERT_COUNT + placement_index, 0, EXPERT_SLOTS - 1)]
    secondary_slot = jnp.where(placement_index < EXPERT_SLOTS - EXPERT_COUNT, spare_slot, primary_slot)
    return jnp.stack([primary_slot, secondary_slot], axis=1).astype(jnp.int32)


def draw_w_gate_up(key, part):
    sort_order, additional, expert_of_slot = slot_layout(key)
    base = jnp.clip(jax.random.normal(jax.random.fold_in(key, 33), (EXPERT_COUNT, D, 2 * FF), jnp.float32), -5.0, 5.0)
    return (base * D ** (-0.5))[expert_of_slot].astype(jnp.bfloat16)


def draw_w_down(key, part):
    sort_order, additional, expert_of_slot = slot_layout(key)
    base = jnp.clip(jax.random.normal(jax.random.fold_in(key, 34), (EXPERT_COUNT, FF, D), jnp.float32), -5.0, 5.0)
    return (base * FF ** (-0.5))[expert_of_slot].astype(jnp.bfloat16)


def block_scale(stream_key, shape, split, least, largest):
    def one(dim, parts):
        heights = jax.random.uniform(jax.random.fold_in(jax.random.fold_in(stream_key, 6), dim), (parts,), jnp.float32, least / len(split), largest / len(split))
        return jnp.repeat(jnp.exp(heights), shape[dim] // parts).reshape((-1,) + (1,) * (len(shape) - dim - 1))

    level = one(*split[0])
    for cut in split[1:]:
        level = level * one(*cut)
    return level


def deal_out(key, own, number, rows, number_of, top, limit, slope):
    sequence = jax.random.permutation(key, number_of)
    crowded, usual = load_shares(number_of, rows * top, limit, slope, True), load_shares(number_of, rows * top, limit, slope, False)
    places = jnp.arange(number_of)

    def named(sizes, rotation):
        used = int((sizes > 0).sum())
        fixed = max(1, used // 4)
        shifted = fixed + (places - fixed + rotation * (used - fixed)) % max(1, number_of - fixed)
        return jnp.zeros((number_of,), jnp.int32).at[sequence[jnp.where(places < fixed, places, shifted)]].set(jnp.asarray(sizes, jnp.int32))

    sizes = jnp.where(number % 4 == 0, named(crowded, number // 4), named(usual, number - number // 4 - 1))
    mixed = jax.random.permutation(jax.random.fold_in(own, 3), number_of)
    source_of, taker = mixed[0:number_of // 2 * 2:2], mixed[1:number_of // 2 * 2:2]
    room = jnp.minimum(sizes[source_of] - 1, limit - sizes[taker]) // 2
    room = jnp.where((source_of == sequence[0]) | (taker == sequence[0]) | (sizes[taker] == 0), 0, jnp.maximum(room, 0))
    shifted = jax.random.randint(jax.random.fold_in(own, 4), (number_of // 2,), 0, 1 << 20) % (room + 1)
    sizes = sizes.at[source_of].add(-shifted).at[taker].add(shifted)
    labels = jnp.searchsorted(jnp.cumsum(sizes), jnp.arange(rows * top), side="right").astype(jnp.int32)
    listing = labels.reshape(top, rows).T
    listing = listing[jax.random.permutation(jax.random.fold_in(own, 1), rows)]
    rotation = jax.random.randint(jax.random.fold_in(own, 2), (rows, 1), 0, top)
    return jnp.take_along_axis(listing, (jnp.arange(top)[None, :] + rotation) % top, axis=1)


def load_shares(count, total, limit, slope, full):
    loads = [(1 << 20) // math.isqrt(standing ** slope) + 1 for standing in range(1, count + 1)]
    largest = limit if full else min(limit, max(-(-total // count), total * loads[0] // sum(loads)))
    least = 1 if total - largest >= count - 1 else 0
    holding, surplus = [largest] + [least] * (count - 1), total - largest - least * (count - 1)
    while surplus > 0:
        free = [i for i in range(1, count) if holding[i] < largest] or [i for i in range(1, count) if holding[i] < limit]
        mass, remaining = sum([loads[i] for i in free]), surplus
        for i in free:
            extra = min(limit - holding[i], max(1, remaining * loads[i] // mass), surplus)
            holding[i] = holding[i] + extra
            surplus = surplus - extra
    return np.array(holding)


def gaussian(key, extent, scale, most, split=(), kind=jnp.bfloat16):
    level = block_scale(key, extent, split, -0.22, 0.18) if split else 1.0
    values = jax.random.normal(key, extent, jnp.float32) * scale * level
    return jnp.minimum(jnp.maximum(values, -most), most).astype(kind)


def setup_inputs(seed: int = 0) -> dict:
    key_of = jax.random.split(jax.random.key(seed), 15)
    residual_in = draw_residual_in(jax.random.fold_in(key_of[14], 71), 0)
    queries = draw_queries(jax.random.fold_in(key_of[14], 71), 0)
    prefill_attn = gaussian(key_of[2], (PRE, QUERY_HEADS * HEAD_SIZE), 0.2, 1.1953125, ((0, 16), (1, 2)))
    kv_cache = draw_kv_cache(jax.random.fold_in(key_of[14], 71), 0)
    page_table = draw_page_table(jax.random.fold_in(key_of[14], 71), 0)
    lengths = draw_lengths(jax.random.fold_in(key_of[14], 71), 0)
    out_weight = gaussian(key_of[6], (QUERY_HEADS * HEAD_SIZE, D), HEAD_SIZE ** -0.5, 0.75, ((0, 2),))
    norm_gain_in = jnp.clip(1.0 + 0.15 * jax.random.normal(key_of[7], (D,), jnp.float32), 0.25, 1.75)
    norm_gain_out = jnp.clip(1.0 + 0.15 * jax.random.normal(key_of[8], (D,), jnp.float32), 0.25, 1.75)
    expert_ids_keys = jax.random.split(jax.random.fold_in(key_of[9], 1), TOKENS // ROWS_DEV)
    expert_ids_turns = jax.random.permutation(jax.random.fold_in(key_of[9], 3), TOKENS // ROWS_DEV)
    expert_ids = jax.vmap(lambda own, number: deal_out(jax.random.fold_in(key_of[9], 2), own, number, ROWS_DEV, EXPERT_COUNT, TOPK, CAP, 2))(expert_ids_keys, expert_ids_turns).reshape((TOKENS, TOPK))
    route_weight = jnp.clip(jnp.exp(math.log(1.0) - 2.9957323 * jax.random.uniform(key_of[10], (TOKENS, TOPK), jnp.float32) ** block_scale(key_of[10], (TOKENS, TOPK), ((0, 16),), -0.2, 0.2)), 0.05, 1.0)
    slot_table = draw_slot_table(jax.random.fold_in(key_of[14], 71), 0)
    w_gate_up = draw_w_gate_up(jax.random.fold_in(key_of[14], 71), 0)
    w_down = draw_w_down(jax.random.fold_in(key_of[14], 71), 0)
    return {"residual_in": residual_in, "queries": queries, "prefill_attn": prefill_attn, "kv_cache": kv_cache, "page_table": page_table, "lengths": lengths, "out_weight": out_weight, "norm_gain_in": norm_gain_in, "norm_gain_out": norm_gain_out, "expert_ids": expert_ids, "route_weight": route_weight, "slot_table": slot_table, "w_gate_up": w_gate_up, "w_down": w_down}


NEG_FILL = -1e+30
EPSILON = 1e-06

def decode_attention(queries, kv_cache, page_table, lengths):
    head_group = QUERY_HEADS // KEY_VALUE_HEADS

    def one_request(lookup_index):
        pages = page_table[lookup_index]
        block = kv_cache[pages].astype(jnp.float32)
        keys = block[..., :HEAD_SIZE]
        values = block[..., HEAD_SIZE:]
        query_vector = queries[lookup_index].astype(jnp.float32).reshape(KEY_VALUE_HEADS, head_group, HEAD_SIZE)
        scores = jnp.einsum('kgd,pktd->pkgt', query_vector, keys) * HEAD_SIZE ** (-0.5)
        positions = jnp.arange(MAXP, dtype=jnp.int32)[:, None] * PAGE_TOKENS + jnp.arange(PAGE_TOKENS, dtype=jnp.int32)[None, :]
        live = (positions < lengths[lookup_index])[:, None, None, :]
        masked = jnp.where(live, scores, NEG_FILL)
        page_max = lax.optimization_barrier(jnp.max(masked, axis=3))
        probs = jnp.where(live, jnp.exp(masked - page_max[..., None]), 0.0)
        probs = lax.optimization_barrier(probs.astype(jnp.bfloat16)).astype(jnp.float32)
        page_sum = lax.optimization_barrier(jnp.sum(probs, axis=3))
        page_acc = jnp.einsum('pkgt,pktd->pkgd', probs, values)
        highest = lax.optimization_barrier(jnp.max(page_max, axis=0))
        weight = jnp.exp(page_max - highest[None])
        total = lax.optimization_barrier(jnp.sum(weight * page_sum, axis=0))
        result = lax.optimization_barrier(jnp.sum(weight[..., None] * page_acc, axis=0)) / total[..., None]
        return result.reshape(-1)
    return lax.map(one_request, jnp.arange(DECODE_REQUESTS, dtype=jnp.int32)).astype(jnp.bfloat16)

def blockwise(left, right, blocks):
    width = left.shape[1] // blocks
    summed = jnp.zeros((left.shape[0], right.shape[1]), jnp.float32)
    for block_index in range(blocks):
        part = jnp.dot(left[:, block_index * width:(block_index + 1) * width], right[block_index * width:(block_index + 1) * width], preferred_element_type=jnp.float32)
        part = lax.optimization_barrier(part.astype(jnp.bfloat16)).astype(jnp.float32)
        summed = summed + part
    return summed

def rms_norm(values, gain):
    return values * lax.rsqrt(lax.optimization_barrier(jnp.mean(values * values, axis=1, keepdims=True)) + EPSILON) * gain

def reference(residual_in, queries, prefill_attn, kv_cache, page_table, lengths, out_weight, norm_gain_in, norm_gain_out, expert_ids, route_weight, slot_table, w_gate_up, w_down):
    attn_dec = decode_attention(queries, kv_cache, page_table, lengths)
    attn_rows = jnp.concatenate([attn_dec.reshape(N_PG, REQ_DEV, QUERY_HEADS * HEAD_SIZE), prefill_attn.reshape(N_PG, PRE_DEV, QUERY_HEADS * HEAD_SIZE)], axis=1).reshape(TOKENS, QUERY_HEADS * HEAD_SIZE)
    middle = residual_in.astype(jnp.float32) + blockwise(attn_rows, out_weight, N_KV)
    normed = rms_norm(middle, norm_gain_in).astype(jnp.bfloat16)
    row_plus = jnp.arange(TOKENS, dtype=jnp.int32)[:, None] + jnp.arange(TOPK, dtype=jnp.int32)[None, :]
    target_slot = slot_table[expert_ids, row_plus % RMAX].reshape(-1).astype(jnp.int32)
    slot_rows = N_PG * CAP
    entry_list = TOKENS * TOPK
    match_count = (target_slot[:, None] == jnp.arange(EXPERT_SLOTS, dtype=jnp.int32)[None, :]).astype(jnp.int32)
    rank = lax.optimization_barrier(jnp.sum((jnp.cumsum(match_count, axis=0) - match_count) * match_count, axis=1)).astype(jnp.int32)
    token_position = (target_slot * slot_rows + rank).astype(jnp.int32)
    entry_lookup = jnp.full((EXPERT_SLOTS * slot_rows,), entry_list, jnp.int32).at[token_position].set(jnp.arange(entry_list, dtype=jnp.int32)).reshape(EXPERT_SLOTS, slot_rows)
    normed_pad = jnp.concatenate([normed, jnp.zeros((1, D), jnp.bfloat16)], axis=0)
    weight_pad = jnp.concatenate([route_weight.reshape(-1), jnp.zeros((1,), jnp.float32)], axis=0)

    def expert(carry, operands):
        entry_ids, gate_up_w, down_w = operands
        token_ids = (entry_ids // TOPK).astype(jnp.int32)
        picked = normed_pad[token_ids]
        gate_up = jnp.dot(picked, gate_up_w, preferred_element_type=jnp.float32)
        hidden = (jax.nn.silu(gate_up[:, :FF]) * gate_up[:, FF:]).astype(jnp.bfloat16)
        produced = jnp.dot(hidden, down_w, preferred_element_type=jnp.float32).astype(jnp.bfloat16)
        produced = lax.optimization_barrier(produced).astype(jnp.float32)
        carry = carry.at[token_ids].add(produced * weight_pad[entry_ids][:, None])
        return (carry, None)
    start = jnp.zeros((TOKENS + 1, D), jnp.float32)
    routed, unused = lax.scan(expert, start, (entry_lookup, w_gate_up, w_down))
    mixed = middle + routed[:TOKENS]
    return rms_norm(mixed, norm_gain_out).astype(jnp.bfloat16)
```

```python
import jax
import jax.numpy as jnp
from jax import lax
from jax.experimental import pallas as pl
from jax.experimental.pallas import tpu as pltpu
from jax.sharding import PartitionSpec as P

NEG_FILL = -1e30
EPSILON = 1e-06


def merged_2(array, axis, join):
    gathered = jax.tree.map(
        lambda a, kind: lax.all_gather(a.astype(kind), axis),
        array,
        (jnp.bfloat16, jnp.bfloat16, jnp.bfloat16),
    )

    def take(source):
        return jax.tree.map(
            lambda a, own: lax.dynamic_index_in_dim(a, source, 0, False).astype(own.dtype),
            gathered,
            array,
        )

    return lax.fori_loop(
        1, lax.axis_size(axis), lambda source, state: join(state, take(source)), take(0)
    )


def merge_pair(first, secondary_slot):
    highest = jnp.maximum(first[0], secondary_slot[0])
    scale_a = jnp.exp(first[0] - highest)
    scale_b = jnp.exp(secondary_slot[0] - highest)
    head_count = first[0].shape[1]
    acc_a = first[2].reshape(first[2].shape[0], head_count, -1) * scale_a[:, :, None]
    acc_b = (
        secondary_slot[2].reshape(secondary_slot[2].shape[0], head_count, -1) * scale_b[:, :, None]
    )
    return (
        highest,
        first[1] * scale_a + secondary_slot[1] * scale_b,
        (acc_a + acc_b).reshape(first[2].shape),
    )


def general_local(
    residual_in,
    queries,
    prefill_attn,
    kv_cache,
    page_table,
    lengths,
    out_weight,
    norm_gain_in,
    norm_gain_out,
    expert_ids,
    route_weight,
    slot_table,
    w_gate_up,
    w_down,
):
    head_dim = kv_cache.shape[3] // 2
    page_len = kv_cache.shape[2]
    pages_here = kv_cache.shape[0]
    kv_here = kv_cache.shape[1]
    own_req = queries.shape[0]
    heads_here = queries.shape[1] // head_dim
    head_group = heads_here // kv_here
    total_req = page_table.shape[0]
    max_pages = page_table.shape[1]
    full_gate_up, full_down = (
        lax.all_gather(w_gate_up, "kv", axis=1, tiled=True),
        lax.all_gather(w_down, "kv", axis=2, tiled=True),
    )
    gathered = lax.all_gather(queries, "pg", axis=0, tiled=True)
    page_ids = lax.axis_index("pg") * pages_here + jnp.arange(pages_here, dtype=jnp.int32)
    flat_table = page_table.reshape(-1)
    entry_index = jnp.arange(flat_table.shape[0], dtype=jnp.int32)
    found = jnp.sum(
        jnp.where(flat_table[None, :] == page_ids[:, None], entry_index[None, :], 0), axis=1
    )
    owner = found // max_pages
    page_slot = found % max_pages
    owner_len = lengths[owner]
    query_pages = gathered[owner].reshape(pages_here, kv_here, head_group, head_dim)
    keys = kv_cache[:, :, :, :head_dim]
    values = kv_cache[:, :, :, head_dim:]
    scores = jnp.einsum(
        "pkgd,pktd->pkgt", query_pages, keys, preferred_element_type=jnp.float32
    ) * head_dim ** (-0.5)
    positions = page_slot[:, None] * page_len + jnp.arange(page_len, dtype=jnp.int32)[None, :]
    live = (positions < owner_len[:, None])[:, None, None, :]
    masked = jnp.where(live, scores, NEG_FILL)
    page_top = jnp.max(masked, axis=3)
    probs = jnp.where(live, jnp.exp(masked - page_top[..., None]), 0.0).astype(jnp.bfloat16)
    page_sum = jnp.sum(probs.astype(jnp.float32), axis=3).reshape(pages_here, heads_here)
    page_acc = jnp.einsum(
        "pkgt,pktd->pkgd", probs, values, preferred_element_type=jnp.float32
    ).reshape(pages_here, heads_here, head_dim)
    page_top = page_top.reshape(pages_here, heads_here)
    page_live = page_slot * page_len < owner_len
    member = (owner[:, None] == jnp.arange(total_req, dtype=jnp.int32)[None, :]) & page_live[
        :, None
    ]
    local_max = jnp.max(jnp.where(member[:, :, None], page_top[:, None, :], NEG_FILL), axis=0)
    member_t = member.astype(jnp.float32).T
    weight = jnp.exp(page_top - local_max[owner])
    sums = jnp.dot(member_t, weight * page_sum, precision=lax.Precision.HIGHEST)
    accs = jnp.dot(
        member_t,
        (weight[:, :, None] * page_acc).reshape(pages_here, -1),
        precision=lax.Precision.HIGHEST,
    )
    sums, accs = (sums, accs)
    merged = merged_2((local_max, sums, accs), "pg", merge_pair)
    start = lax.axis_index("pg") * own_req
    own_sum = lax.dynamic_slice_in_dim(merged[1], start, own_req, 0)
    own_acc = lax.dynamic_slice_in_dim(merged[2], start, own_req, 0)
    attn_dec = (own_acc.reshape(own_req, heads_here, head_dim) / own_sum[:, :, None]).reshape(
        own_req, -1
    )
    attn_dec = attn_dec.astype(jnp.bfloat16)
    attn_rows = jnp.concatenate([attn_dec, prefill_attn], axis=0)
    projected = jnp.dot(attn_rows, out_weight, preferred_element_type=jnp.float32)
    mixed_in = lax.psum_scatter(
        projected.astype(jnp.bfloat16), "kv", scatter_dimension=1, tiled=True
    ).astype(jnp.float32)
    middle = residual_in.astype(jnp.float32) + mixed_in
    full_width = residual_in.shape[1] * lax.axis_size("kv")
    in_squares = lax.psum(jnp.sum(middle * middle, axis=1), "kv")
    normed = (middle * lax.rsqrt(in_squares / full_width + EPSILON)[:, None] * norm_gain_in).astype(
        jnp.bfloat16
    )
    token_rows, top = expert_ids.shape
    copies = slot_table.shape[1]
    experts_total = slot_table.shape[0]
    kv_count = lax.axis_size("kv")
    capacity = kv_count * max(
        1,
        (token_rows * top * 5 + 4 * experts_total * kv_count - 1) // (4 * experts_total * kv_count),
    )
    slots_here = w_gate_up.shape[0]
    groups = lax.axis_size("pg")
    all_slots = slots_here * groups
    feature_cols = normed.shape[1]
    row_ids = lax.axis_index("pg") * token_rows + jnp.arange(token_rows, dtype=jnp.int32)
    parity = (row_ids[:, None] + jnp.arange(top, dtype=jnp.int32)[None, :]) % copies
    route_key = (expert_ids * copies + parity).reshape(-1)
    table_flat = slot_table.reshape(-1)
    table_index = jnp.arange(table_flat.shape[0], dtype=jnp.int32)
    target_slot = jnp.sum(
        jnp.where(route_key[:, None] == table_index[None, :], table_flat[None, :], 0), axis=1
    )
    match_count = (target_slot[:, None] == jnp.arange(all_slots, dtype=jnp.int32)[None, :]).astype(
        jnp.int32
    )
    rank = jnp.sum((jnp.cumsum(match_count, axis=0) - match_count) * match_count, axis=1)
    dest = target_slot * capacity + rank
    source_row = jnp.arange(token_rows * top, dtype=jnp.int32) // top
    outgoing = (
        jnp.zeros((all_slots * capacity, feature_cols), jnp.bfloat16)
        .at[dest]
        .set(normed[source_row])
    )
    outgoing = outgoing.reshape(groups, slots_here, capacity, feature_cols)
    arrived = lax.all_to_all(outgoing, "pg", split_axis=0, concat_axis=0, tiled=True)
    widened = lax.all_to_all(arrived, "kv", split_axis=2, concat_axis=3, tiled=True)
    gate_up = jnp.einsum(
        "pscd,sdf->pscf", widened, full_gate_up, preferred_element_type=jnp.float32
    )
    half = gate_up.shape[3] // 2
    hidden = (jax.nn.silu(gate_up[..., :half]) * gate_up[..., half:]).astype(jnp.bfloat16)
    produced = jnp.einsum(
        "pscf,sfd->pscd", hidden, full_down, preferred_element_type=jnp.float32
    ).astype(jnp.bfloat16)
    narrowed = lax.all_to_all(produced, "kv", split_axis=3, concat_axis=2, tiled=True)
    returned = lax.all_to_all(narrowed, "pg", split_axis=0, concat_axis=0, tiled=True)
    returned = returned.reshape(all_slots * capacity, feature_cols)
    picked = returned[dest].astype(jnp.float32).reshape(token_rows, top, feature_cols)
    mixed = middle + jnp.sum(picked * route_weight[:, :, None], axis=1)
    out_squares = lax.psum(jnp.sum(mixed * mixed, axis=1), "kv")
    return (mixed * lax.rsqrt(out_squares / full_width + EPSILON)[:, None] * norm_gain_out).astype(
        jnp.bfloat16
    )


F32 = jnp.float32
BF16 = jnp.bfloat16
CAP = 16
HIGH = lax.Precision.HIGHEST


def call(body, outs, scratch=(), smem=(), vmem=32 * 2**20):
    def run(*operands):
        specs = [
            pl.BlockSpec(memory_space=pltpu.SMEM if n in smem else pltpu.VMEM)
            for n in range(len(operands))
        ]
        return pl.pallas_call(
            body,
            out_shape=[jax.ShapeDtypeStruct(s, d) for s, d in outs],
            in_specs=specs,
            out_specs=[pl.BlockSpec(memory_space=pltpu.VMEM) for _ in outs],
            scratch_shapes=list(scratch),
            compiler_params=pltpu.CompilerParams(vmem_limit_bytes=vmem),
        )(*operands)

    return run


def iota(shape, dim):
    return lax.broadcasted_iota(jnp.int32, shape, dim)


def dot(a, b, precision=None):
    return jnp.dot(a, b, preferred_element_type=F32, precision=precision)


def dot_t(a, b):
    return lax.dot_general(a, b, (((1,), (1,)), ((), ())), preferred_element_type=F32)


def t_dot(a, b):
    return lax.dot_general(a, b, (((0,), (0,)), ((), ())), preferred_element_type=F32)


def swap_kv(x):
    return lax.ppermute(x, "kv", [(0, 1), (1, 0)])


def swap_pg(x, mask, n):
    return lax.ppermute(x, "pg", [(i, i ^ mask) for i in range(n)])


def page_attention(sent, kv_cache, owner, live, own_req):
    groups = sent.shape[0]
    cols = sent.shape[2]
    pages, kv_here, page_len, wide = kv_cache.shape
    head_dim = wide // 2
    heads = cols // head_dim
    group = heads // kv_here
    rows = 16
    requests = groups * own_req
    keys = kv_here * page_len

    def body(owner_s, live_s, owner_col, owner_lane, sent_ref, kv_ref, out_ref, q_all, acc, m_all, l_all):
        for g in range(groups):
            q_all[g * own_req : (g + 1) * own_req, :] = sent_ref[g, 0:own_req, :].astype(F32)
        total = pages * rows
        pick = (owner_col[...] == iota((total, requests), 1)).astype(BF16)
        wide_q = dot(pick, q_all[...].astype(BF16))
        head_row = iota((total, cols), 0) % rows
        spread = head_row == iota((total, cols), 1) // head_dim
        fold = (iota((cols, wide), 0) % head_dim == iota((cols, wide), 1)).astype(BF16)
        q = dot(jnp.where(spread, wide_q, 0.0).astype(BF16), fold).astype(BF16)
        col = iota((rows, keys), 1)
        mine = col // page_len == iota((rows, keys), 0) // group
        place = col % page_len
        lane = iota((rows, 128), 1)
        tops = jnp.full((rows, 128), NEG_FILL, F32)
        for p in range(pages):
            block = kv_ref[p].reshape(keys, wide)
            scores = dot_t(q[p * rows : (p + 1) * rows], block) * head_dim ** (-0.5)
            ok = mine & (place < live_s[p])
            masked = jnp.where(ok, scores, NEG_FILL)
            top = jnp.max(masked, axis=1, keepdims=True).astype(BF16).astype(F32)
            probs = jnp.where(ok, jnp.exp(masked - top), 0.0).astype(BF16)
            part = pl.ds(p * rows, rows)
            l_all[part, :] = jnp.broadcast_to(
                jnp.sum(probs.astype(F32), axis=1, keepdims=True), (rows, 128)
            )
            acc[part, :] = dot(probs, block)
            m_all[part, :] = jnp.broadcast_to(top, (rows, 128))
            tops = jnp.where(lane == p, top, tops)
        for p in range(pages):
            part = pl.ds(p * rows, rows)
            same = owner_lane[...] == owner_s[p]
            best = jnp.max(jnp.where(same, tops, NEG_FILL), axis=1, keepdims=True)
            scale = jnp.exp(m_all[part, :] - best)
            acc[part, :] = acc[part, :] * scale
            l_all[part, :] = l_all[part, :] * scale
            first = jnp.int32(1)
            for e in range(p):
                first = jnp.where(owner_s[e] == owner_s[p], 0, first)
            m_all[part, :] = jnp.where(first == 1, jnp.broadcast_to(best, (rows, 128)), 0.0)
        unfold = (iota((wide, cols), 0) - head_dim == iota((wide, cols), 1) % head_dim).astype(BF16)
        spread_acc = jnp.where(spread, dot(acc[...].astype(BF16), unfold), 0.0).astype(BF16)
        here = iota((total, 128), 0) % rows == iota((total, 128), 1)
        tops_out = jnp.where(here, m_all[...], 0.0).astype(BF16)
        sums_out = jnp.where(here, l_all[...], 0.0)
        sums_high = sums_out.astype(BF16)
        sums_low = (sums_out - sums_high.astype(F32)).astype(BF16)
        out_acc = t_dot(pick, spread_acc).astype(BF16)
        out_top = t_dot(pick, tops_out).astype(BF16)
        out_sum = (t_dot(pick, sums_high) + t_dot(pick, sums_low)).astype(BF16)
        for g in range(groups):
            part = slice(g * own_req, (g + 1) * own_req)
            out_ref[g, :, 0:cols] = out_acc[part]
            out_ref[g, :, cols : cols + 128] = out_top[part]
            out_ref[g, :, cols + 128 : cols + 256] = out_sum[part]

    total = pages * rows
    owner_col = jnp.broadcast_to(jnp.repeat(owner, rows)[:, None], (total, requests))
    owner_lane = jnp.broadcast_to(
        jnp.concatenate([owner, jnp.full((128 - pages,), -1, jnp.int32)])[None, :], (rows, 128)
    )
    return call(
        body,
        [((groups, own_req, cols + 256), BF16)],
        [
            pltpu.VMEM((requests, cols), F32),
            pltpu.VMEM((total, wide), F32),
            pltpu.VMEM((total, 128), F32),
            pltpu.VMEM((total, 128), F32),
        ],
        smem=(0, 1),
    )(owner, live, owner_col, owner_lane, sent, kv_cache)[0]


def project(arrived, prefill, weight, residual, me_kv, head_dim):
    groups, own_req, _ = arrived.shape
    rows, cols = residual.shape

    def body(me, arr, pre, w_ref, res, send, base, w_scr, rows_scr):
        top = arr[:, :, cols : cols + 128].astype(F32)
        tot = arr[:, :, cols + 128 : cols + 256].astype(F32)
        top = jnp.where(tot > 0.0, top, NEG_FILL)
        best = jnp.max(top, axis=0)
        scale = jnp.where(tot > 0.0, jnp.exp(top - best[None]), 0.0)
        whole = jnp.sum(scale * tot, axis=0)
        whole = jnp.where(whole > 0.0, whole, 1.0)
        scale = scale / whole[None]
        for g in range(groups):
            w_scr[g * own_req : (g + 1) * own_req, :] = scale[g]
        expand = (iota((128, cols), 0) == iota((128, cols), 1) // head_dim).astype(F32)
        wide = dot(w_scr[...], expand, HIGH)
        merged = jnp.zeros((own_req, cols), F32)
        for g in range(groups):
            merged += wide[g * own_req : (g + 1) * own_req] * arr[g, :, 0:cols].astype(F32)
        rows_scr[0:own_req, :] = merged
        rows_scr[own_req:, :] = pre[...].astype(F32)
        left = rows_scr[...].astype(BF16)
        mine = pl.multiple_of(me[0] * cols, 128)
        other = pl.multiple_of((1 - me[0]) * cols, 128)
        send[:, 0:cols] = dot(left, w_ref[:, pl.ds(other, cols)]).astype(BF16)
        own = dot(left, w_ref[:, pl.ds(mine, cols)]).astype(BF16).astype(F32)
        own = own + res[...].astype(F32)
        base[...] = own
        send[:, cols:] = own.astype(BF16)

    return call(
        body,
        [((rows, 2 * cols), BF16), ((rows, cols), F32)],
        [pltpu.VMEM((groups * own_req, 128), F32), pltpu.VMEM((rows, cols), F32)],
        smem=(0,),
    )(me_kv, arrived, prefill, weight, residual)


def first_norm(base, sent, got, gain):
    rows, cols = base.shape

    def body(base_ref, sent_ref, got_ref, gain_ref, middle, normed):
        mid = base_ref[...] + got_ref[:, 0:cols].astype(F32)
        far = got_ref[:, cols:].astype(F32) + sent_ref[:, 0:cols].astype(F32)
        squares = jnp.sum(mid * mid + far * far, axis=1, keepdims=True)
        middle[...] = mid
        normed[...] = (
            mid * lax.rsqrt(squares / (2 * cols) + EPSILON) * gain_ref[...]
        ).astype(BF16)

    return call(body, [((rows, cols), F32), ((rows, cols), BF16)])(
        base, sent, got, gain.reshape(1, -1)
    )


def one_hot(meta, g, s, block_rows):
    tokens = meta.shape[2]
    blocks = tokens // block_rows
    shape = (blocks * CAP, tokens)
    place = meta[g, s : s + 1, :].astype(jnp.int32)
    row = iota(shape, 0)
    return (place == row % CAP) & (iota(shape, 1) // block_rows == row // CAP)


def gather_and_first(groups, meta, w_gate_up, me_kv, block_rows):
    count, cols, slots = len(groups), groups[0].shape[1], w_gate_up.shape[0]
    tokens = groups[0].shape[0]
    part = tokens // block_rows * CAP
    ff = w_gate_up.shape[2] // 2
    half = ff // 2

    def body(me, meta_ref, w_ref, *refs):
        xs, send = refs[count:]
        for g in range(count):
            pick = jnp.concatenate(
                [one_hot(meta_ref, g, s, block_rows).astype(BF16) for s in range(slots)], axis=0
            )
            rows = dot(pick, refs[g][...]).astype(BF16)
            for s in range(slots):
                xs[s, g * part : (g + 1) * part, :] = rows[s * part : (s + 1) * part]
        far = pl.multiple_of((1 - me[0]) * half, 128)
        up = pl.multiple_of(ff + (1 - me[0]) * half, 128)
        send[:, 0:half] = dot(xs[0], w_ref[0, :, pl.ds(far, half)]).astype(BF16)
        send[:, half:] = dot(xs[0], w_ref[0, :, pl.ds(up, half)]).astype(BF16)

    return call(
        body,
        [((slots, count * part, cols), BF16), ((count * part, ff), BF16)],
        smem=(0,),
    )(me_kv, meta, w_gate_up, *groups)


def rest_of_gate_up(xs, w_gate_up, me_kv):
    slots, rows, cols = xs.shape
    ff = w_gate_up.shape[2] // 2
    half = ff // 2

    def body(me, x_ref, w_ref, *outs):
        sends, own = outs[:-1], outs[-1]
        far = pl.multiple_of((1 - me[0]) * half, 128)
        far_up = pl.multiple_of(ff + (1 - me[0]) * half, 128)
        near = pl.multiple_of(me[0] * half, 128)
        near_up = pl.multiple_of(ff + me[0] * half, 128)
        for s in range(1, slots):
            sends[s - 1][:, 0:half] = dot(x_ref[s], w_ref[s, :, pl.ds(far, half)]).astype(BF16)
            sends[s - 1][:, half:] = dot(x_ref[s], w_ref[s, :, pl.ds(far_up, half)]).astype(BF16)
        for s in range(slots):
            own[s, :, 0:half] = dot(x_ref[s], w_ref[s, :, pl.ds(near, half)])
            own[s, :, half:] = dot(x_ref[s], w_ref[s, :, pl.ds(near_up, half)])

    return call(
        body,
        [((rows, ff), BF16)] * (slots - 1) + [((slots, rows, ff), F32)],
        smem=(0,),
    )(me_kv, xs, w_gate_up)


def activate(own, got, s):
    slots, rows, ff = own.shape
    half = ff // 2

    def body(own_ref, got_ref, out):
        gate = own_ref[s, :, 0:half] + got_ref[:, 0:half].astype(F32)
        up = own_ref[s, :, half:] + got_ref[:, half:].astype(F32)
        out[...] = (gate / (1.0 + jnp.exp(-gate)) * up).astype(BF16)

    return call(body, [((rows, half), BF16)])(own, got)[0]


def down(near, far, w_down, meta, s, me_kv, block_rows):
    rows, half = near.shape
    cols = w_down.shape[2]
    count, _, tokens = meta.shape
    slots = w_down.shape[0]
    part = rows // count

    def body(me, near_ref, far_ref, w_ref, meta_ref, out):
        lo = pl.multiple_of(me[0] * half, 128)
        hi = pl.multiple_of((1 - me[0]) * half, 128)
        made = dot(near_ref[...], w_ref[s, pl.ds(lo, half), :])
        made = made + dot(far_ref[...], w_ref[s, pl.ds(hi, half), :])
        for g in range(count):
            pick = one_hot(meta_ref, g, s, block_rows)
            gate = jnp.sum(
                jnp.where(pick, meta_ref[g, slots + s : slots + s + 1, :], 0.0),
                axis=1,
                keepdims=True,
            )
            out[g * part : (g + 1) * part, :] = (made[g * part : (g + 1) * part] * gate).astype(
                BF16
            )

    return call(body, [((rows, cols), BF16)], smem=(0,))(me_kv, near, far, w_down, meta)[0]


def scatter(made, meta, g, block_rows, plus=None):
    slots = len(made)
    rows, cols = made[0].shape
    count, _, tokens = meta.shape
    part = rows // count

    def body(meta_ref, *refs):
        out = refs[-1]
        pick = jnp.concatenate(
            [one_hot(meta_ref, g, s, block_rows).astype(BF16) for s in range(slots)], axis=0
        )
        rows_here = jnp.concatenate(
            [refs[s][g * part : (g + 1) * part, :] for s in range(slots)], axis=0
        )
        total = t_dot(pick, rows_here)
        if plus is not None:
            total = total + refs[slots][...].astype(F32)
        out[...] = total.astype(BF16)

    extra = [] if plus is None else [plus]
    return call(body, [((tokens, cols), BF16)])(meta, *made, *extra)[0]


def split_sum(a, b, block_rows):
    tokens, cols = a.shape
    count = tokens // block_rows

    def body(a_ref, b_ref, *outs):
        for n in range(count):
            part = slice(n * block_rows, (n + 1) * block_rows)
            total = a_ref[part, :].astype(F32) + b_ref[part, :].astype(F32)
            outs[n][...] = total.astype(outs[n].dtype)

    return call(
        body,
        [((block_rows, cols), F32)] + [((block_rows, cols), BF16)] * (count - 1),
    )(a, b)


def close(middle, parts):
    rows, cols = middle.shape

    def body(mid, *refs):
        mixed, squares = refs[-2:]
        total = mid[...]
        for ref in refs[:-2]:
            total = total + ref[...].astype(F32)
        mixed[...] = total
        total = total * total
        folded = total[:, 0:128]
        for n in range(1, cols // 128):
            folded = folded + total[:, n * 128 : (n + 1) * 128]
        squares[...] = folded

    return call(body, [((rows, cols), F32), ((rows, 128), F32)])(middle, *parts)


def last_norm(mixed, near, far, gain):
    rows, cols = mixed.shape

    def body(mixed_ref, near_ref, far_ref, gain_ref, out):
        squares = jnp.sum(near_ref[...] + far_ref[...], axis=1, keepdims=True)
        out[...] = (
            mixed_ref[...] * lax.rsqrt(squares / (2 * cols) + EPSILON) * gain_ref[...]
        ).astype(BF16)

    return call(body, [((rows, cols), BF16)])(mixed, near, far, gain.reshape(1, -1))[0]


def routing(expert_ids, route_weight, slot_table, first_row, all_slots):
    rows, top = expert_ids.shape
    copies = slot_table.shape[1]
    experts = slot_table.shape[0]
    parity = (
        first_row
        + jnp.arange(rows, dtype=jnp.int32)[:, None]
        + jnp.arange(top, dtype=jnp.int32)[None, :]
    ) % copies
    key = expert_ids * copies + parity
    table = slot_table.reshape(-1)
    target = jnp.sum(
        jnp.where(
            key[:, :, None] == jnp.arange(experts * copies, dtype=jnp.int32)[None, None, :],
            table[None, None, :],
            0,
        ),
        axis=2,
    )
    hit = target.T[None, :, :] == jnp.arange(all_slots, dtype=jnp.int32)[:, None, None]
    named = jnp.sum(hit.astype(F32), axis=1)
    gate = jnp.sum(jnp.where(hit, route_weight.T[None, :, :], 0.0), axis=1)
    before = (
        jnp.arange(rows, dtype=jnp.int32)[:, None] < jnp.arange(rows, dtype=jnp.int32)[None, :]
    )
    rank = jnp.dot(named.astype(BF16), before.astype(BF16), preferred_element_type=F32)
    return jnp.where(named > 0, rank, -1.0), gate


def fast_local(
    residual_in,
    queries,
    prefill_attn,
    kv_cache,
    page_table,
    lengths,
    out_weight,
    norm_gain_in,
    norm_gain_out,
    expert_ids,
    route_weight,
    slot_table,
    w_gate_up,
    w_down,
):
    n_pg = lax.axis_size("pg")
    me = lax.axis_index("pg")
    me_kv = lax.axis_index("kv").reshape(1).astype(jnp.int32)
    rows, cols = residual_in.shape
    own_req = queries.shape[0]
    slots = w_gate_up.shape[0]
    pages, _, page_len, wide = kv_cache.shape
    head_dim = wide // 2
    max_pages = page_table.shape[1]

    place, gate = routing(expert_ids, route_weight, slot_table, me * rows, slots * n_pg)
    gate_high = gate.astype(BF16)
    gate_low = (gate - gate_high.astype(F32)).astype(BF16)
    info = jnp.concatenate(
        [x.reshape(n_pg, slots * rows) for x in (place.astype(BF16), gate_high, gate_low)], axis=1
    )
    lanes = -(-info.shape[1] // cols) * cols
    info = jnp.pad(info, ((0, 0), (0, lanes - info.shape[1]))).reshape(n_pg, -1, cols)
    sent = jnp.concatenate([jnp.broadcast_to(queries[None], (n_pg, own_req, cols)), info], axis=1)
    sent = lax.all_to_all(sent, "pg", split_axis=0, concat_axis=0, tiled=True)

    order = [c + 2 * y + 4 * z for c in range(2) for y in range(2) for z in range(n_pg // 4)]
    info = sent[:, own_req:, :].reshape(n_pg, lanes)[:, : 3 * slots * rows]
    info = info[me ^ jnp.asarray(order, jnp.int32)].astype(F32)
    info = info.reshape(4, n_pg // 4, 3, slots, rows).transpose(0, 2, 3, 1, 4)
    info = info.reshape(4, 3, slots, n_pg // 4 * rows)
    meta = jnp.concatenate([info[:, 0], info[:, 1] + info[:, 2]], axis=1)

    page_ids = me * pages + jnp.arange(pages, dtype=jnp.int32)
    flat_table = page_table.reshape(-1)
    entry_index = jnp.arange(flat_table.shape[0], dtype=jnp.int32)
    found = jnp.sum(
        jnp.where(flat_table[None, :] == page_ids[:, None], entry_index[None, :], 0), axis=1
    )
    owner = found // max_pages
    owner_len = jnp.sum(
        jnp.where(
            owner[:, None] == jnp.arange(lengths.shape[0], dtype=jnp.int32)[None, :],
            lengths[None, :],
            0,
        ),
        axis=1,
    )
    live = owner_len - found % max_pages * page_len
    partial = page_attention(sent, kv_cache, owner, live, own_req)
    arrived = lax.all_to_all(partial, "pg", split_axis=0, concat_axis=0, tiled=True)

    send, base = project(arrived, prefill_attn, out_weight, residual_in, me_kv, head_dim)
    middle, normed = first_norm(base, send, swap_kv(send), norm_gain_in)

    near = jnp.concatenate(
        [normed] + [swap_pg(normed, 4 * z, n_pg) for z in range(1, n_pg // 4)], axis=0
    )
    across = swap_pg(near, 2, n_pg)
    tokens = [near, across, swap_pg(near, 1, n_pg), swap_pg(across, 1, n_pg)]

    xs, send0 = gather_and_first(tokens, meta, w_gate_up, me_kv, rows)
    *sends, own = rest_of_gate_up(xs, w_gate_up, me_kv)
    made = []
    for s, out in enumerate([send0] + sends):
        hidden = activate(own, swap_kv(out), s)
        made.append(down(hidden, swap_kv(hidden), w_down, meta, s, me_kv, rows))

    got3 = swap_pg(scatter(made, meta, 3, rows), 1, n_pg)
    got2 = swap_pg(scatter(made, meta, 2, rows), 1, n_pg)
    sum1 = swap_pg(scatter(made, meta, 1, rows, got3), 2, n_pg)
    sum0 = scatter(made, meta, 0, rows, got2)
    parts = split_sum(sum0, sum1, rows)
    parts = [parts[0]] + [swap_pg(parts[z], 4 * z, n_pg) for z in range(1, n_pg // 4)]
    mixed, squares = close(middle, parts)
    return last_norm(mixed, squares, swap_kv(squares), norm_gain_out)


def solution(mesh):
    fast = mesh.shape["kv"] == 2 and mesh.shape["pg"] == 16
    local = fast_local if fast else general_local
    in_specs = (
        P("pg", "kv"),
        P("pg", "kv"),
        P("pg", "kv"),
        P("pg", "kv", None, None),
        P(),
        P(),
        P("kv", None),
        P("kv"),
        P("kv"),
        P("pg", None),
        P("pg", None),
        P(),
        P("pg", "kv", None),
        P("pg", None, "kv"),
    )
    out_specs = P("pg", "kv")
    return jax.shard_map(local, mesh=mesh, in_specs=in_specs, out_specs=out_specs, check_vma=False)
```

```python
import functools

import jax
import jax.numpy as jnp
from jax import lax
from jax.experimental import pallas as pl
from jax.experimental.pallas import tpu as pltpu
from jax.sharding import PartitionSpec as P

NEG_FILL = -1e30
EPSILON = 1e-06


def merged_2(array, axis, join):
    gathered = jax.tree.map(
        lambda a, kind: lax.all_gather(a.astype(kind), axis),
        array,
        (jnp.bfloat16, jnp.bfloat16, jnp.bfloat16),
    )

    def take(source):
        return jax.tree.map(
            lambda a, own: lax.dynamic_index_in_dim(a, source, 0, False).astype(own.dtype),
            gathered,
            array,
        )

    return lax.fori_loop(
        1, lax.axis_size(axis), lambda source, state: join(state, take(source)), take(0)
    )


def merge_pair(first, secondary_slot):
    highest = jnp.maximum(first[0], secondary_slot[0])
    scale_a = jnp.exp(first[0] - highest)
    scale_b = jnp.exp(secondary_slot[0] - highest)
    head_count = first[0].shape[1]
    acc_a = first[2].reshape(first[2].shape[0], head_count, -1) * scale_a[:, :, None]
    acc_b = (
        secondary_slot[2].reshape(secondary_slot[2].shape[0], head_count, -1) * scale_b[:, :, None]
    )
    return (
        highest,
        first[1] * scale_a + secondary_slot[1] * scale_b,
        (acc_a + acc_b).reshape(first[2].shape),
    )


def general_local(
    residual_in,
    queries,
    prefill_attn,
    kv_cache,
    page_table,
    lengths,
    out_weight,
    norm_gain_in,
    norm_gain_out,
    expert_ids,
    route_weight,
    slot_table,
    w_gate_up,
    w_down,
):
    head_dim = kv_cache.shape[3] // 2
    page_len = kv_cache.shape[2]
    pages_here = kv_cache.shape[0]
    kv_here = kv_cache.shape[1]
    own_req = queries.shape[0]
    heads_here = queries.shape[1] // head_dim
    head_group = heads_here // kv_here
    total_req = page_table.shape[0]
    max_pages = page_table.shape[1]
    full_gate_up, full_down = (
        lax.all_gather(w_gate_up, "kv", axis=1, tiled=True),
        lax.all_gather(w_down, "kv", axis=2, tiled=True),
    )
    gathered = lax.all_gather(queries, "pg", axis=0, tiled=True)
    page_ids = lax.axis_index("pg") * pages_here + jnp.arange(pages_here, dtype=jnp.int32)
    flat_table = page_table.reshape(-1)
    entry_index = jnp.arange(flat_table.shape[0], dtype=jnp.int32)
    found = jnp.sum(
        jnp.where(flat_table[None, :] == page_ids[:, None], entry_index[None, :], 0), axis=1
    )
    owner = found // max_pages
    page_slot = found % max_pages
    owner_len = lengths[owner]
    query_pages = gathered[owner].reshape(pages_here, kv_here, head_group, head_dim)
    keys = kv_cache[:, :, :, :head_dim]
    values = kv_cache[:, :, :, head_dim:]
    scores = jnp.einsum(
        "pkgd,pktd->pkgt", query_pages, keys, preferred_element_type=jnp.float32
    ) * head_dim ** (-0.5)
    positions = page_slot[:, None] * page_len + jnp.arange(page_len, dtype=jnp.int32)[None, :]
    live = (positions < owner_len[:, None])[:, None, None, :]
    masked = jnp.where(live, scores, NEG_FILL)
    page_top = jnp.max(masked, axis=3)
    probs = jnp.where(live, jnp.exp(masked - page_top[..., None]), 0.0).astype(jnp.bfloat16)
    page_sum = jnp.sum(probs.astype(jnp.float32), axis=3).reshape(pages_here, heads_here)
    page_acc = jnp.einsum(
        "pkgt,pktd->pkgd", probs, values, preferred_element_type=jnp.float32
    ).reshape(pages_here, heads_here, head_dim)
    page_top = page_top.reshape(pages_here, heads_here)
    page_live = page_slot * page_len < owner_len
    member = (owner[:, None] == jnp.arange(total_req, dtype=jnp.int32)[None, :]) & page_live[
        :, None
    ]
    local_max = jnp.max(jnp.where(member[:, :, None], page_top[:, None, :], NEG_FILL), axis=0)
    member_t = member.astype(jnp.float32).T
    weight = jnp.exp(page_top - local_max[owner])
    sums = jnp.dot(member_t, weight * page_sum, precision=lax.Precision.HIGHEST)
    accs = jnp.dot(
        member_t,
        (weight[:, :, None] * page_acc).reshape(pages_here, -1),
        precision=lax.Precision.HIGHEST,
    )
    sums, accs = (sums, accs)
    merged = merged_2((local_max, sums, accs), "pg", merge_pair)
    start = lax.axis_index("pg") * own_req
    own_sum = lax.dynamic_slice_in_dim(merged[1], start, own_req, 0)
    own_acc = lax.dynamic_slice_in_dim(merged[2], start, own_req, 0)
    attn_dec = (own_acc.reshape(own_req, heads_here, head_dim) / own_sum[:, :, None]).reshape(
        own_req, -1
    )
    attn_dec = attn_dec.astype(jnp.bfloat16)
    attn_rows = jnp.concatenate([attn_dec, prefill_attn], axis=0)
    projected = jnp.dot(attn_rows, out_weight, preferred_element_type=jnp.float32)
    mixed_in = lax.psum_scatter(
        projected.astype(jnp.bfloat16), "kv", scatter_dimension=1, tiled=True
    ).astype(jnp.float32)
    middle = residual_in.astype(jnp.float32) + mixed_in
    full_width = residual_in.shape[1] * lax.axis_size("kv")
    in_squares = lax.psum(jnp.sum(middle * middle, axis=1), "kv")
    normed = (middle * lax.rsqrt(in_squares / full_width + EPSILON)[:, None] * norm_gain_in).astype(
        jnp.bfloat16
    )
    token_rows, top = expert_ids.shape
    copies = slot_table.shape[1]
    experts_total = slot_table.shape[0]
    kv_count = lax.axis_size("kv")
    capacity = kv_count * max(
        1,
        (token_rows * top * 5 + 4 * experts_total * kv_count - 1) // (4 * experts_total * kv_count),
    )
    slots_here = w_gate_up.shape[0]
    groups = lax.axis_size("pg")
    all_slots = slots_here * groups
    feature_cols = normed.shape[1]
    row_ids = lax.axis_index("pg") * token_rows + jnp.arange(token_rows, dtype=jnp.int32)
    parity = (row_ids[:, None] + jnp.arange(top, dtype=jnp.int32)[None, :]) % copies
    route_key = (expert_ids * copies + parity).reshape(-1)
    table_flat = slot_table.reshape(-1)
    table_index = jnp.arange(table_flat.shape[0], dtype=jnp.int32)
    target_slot = jnp.sum(
        jnp.where(route_key[:, None] == table_index[None, :], table_flat[None, :], 0), axis=1
    )
    match_count = (target_slot[:, None] == jnp.arange(all_slots, dtype=jnp.int32)[None, :]).astype(
        jnp.int32
    )
    rank = jnp.sum((jnp.cumsum(match_count, axis=0) - match_count) * match_count, axis=1)
    dest = target_slot * capacity + rank
    source_row = jnp.arange(token_rows * top, dtype=jnp.int32) // top
    outgoing = (
        jnp.zeros((all_slots * capacity, feature_cols), jnp.bfloat16)
        .at[dest]
        .set(normed[source_row])
    )
    outgoing = outgoing.reshape(groups, slots_here, capacity, feature_cols)
    arrived = lax.all_to_all(outgoing, "pg", split_axis=0, concat_axis=0, tiled=True)
    widened = lax.all_to_all(arrived, "kv", split_axis=2, concat_axis=3, tiled=True)
    gate_up = jnp.einsum(
        "pscd,sdf->pscf", widened, full_gate_up, preferred_element_type=jnp.float32
    )
    half = gate_up.shape[3] // 2
    hidden = (jax.nn.silu(gate_up[..., :half]) * gate_up[..., half:]).astype(jnp.bfloat16)
    produced = jnp.einsum(
        "pscf,sfd->pscd", hidden, full_down, preferred_element_type=jnp.float32
    ).astype(jnp.bfloat16)
    narrowed = lax.all_to_all(produced, "kv", split_axis=3, concat_axis=2, tiled=True)
    returned = lax.all_to_all(narrowed, "pg", split_axis=0, concat_axis=0, tiled=True)
    returned = returned.reshape(all_slots * capacity, feature_cols)
    picked = returned[dest].astype(jnp.float32).reshape(token_rows, top, feature_cols)
    mixed = middle + jnp.sum(picked * route_weight[:, :, None], axis=1)
    out_squares = lax.psum(jnp.sum(mixed * mixed, axis=1), "kv")
    return (mixed * lax.rsqrt(out_squares / full_width + EPSILON)[:, None] * norm_gain_out).astype(
        jnp.bfloat16
    )


F32 = jnp.float32
BF16 = jnp.bfloat16
CAP = 16
HIGH = lax.Precision.HIGHEST


def call(body, outs, scratch=(), smem=(), hbm=(), vmem=16):
    def run(*operands):
        kinds = [
            pltpu.SMEM if n in smem else pltpu.HBM if n in hbm else pltpu.VMEM
            for n in range(len(operands))
        ]
        return pl.pallas_call(
            body,
            out_shape=[jax.ShapeDtypeStruct(s, d) for s, d in outs],
            in_specs=[pl.BlockSpec(memory_space=kind) for kind in kinds],
            out_specs=[pl.BlockSpec(memory_space=pltpu.VMEM) for _ in outs],
            scratch_shapes=list(scratch),
            compiler_params=pltpu.CompilerParams(
                vmem_limit_bytes=vmem * 2**20
            ),
            cost_estimate=pl.CostEstimate(flops=1, bytes_accessed=1, transcendentals=0),
        )(*operands)

    return run


def after(values, *earlier):
    return lax.optimization_barrier((values, earlier))[0]


def iota(shape, dim):
    return lax.broadcasted_iota(jnp.int32, shape, dim)


def dot(a, b, precision=None):
    return jnp.dot(a, b, preferred_element_type=F32, precision=precision)


def dot_t(a, b):
    return lax.dot_general(a, b, (((1,), (1,)), ((), ())), preferred_element_type=F32)


def t_dot(a, b):
    return lax.dot_general(a, b, (((0,), (0,)), ((), ())), preferred_element_type=F32)


def swap_kv(x):
    return lax.ppermute(x, "kv", [(0, 1), (1, 0)])


def swap_pg(x, mask, n):
    return lax.ppermute(x, "pg", [(i, i ^ mask) for i in range(n)])


def pack(queries, residual, expert_ids, route_weight, n_pg):
    own_req, cols = queries.shape
    rows, top = expert_ids.shape
    tiles = cols // 128
    high = 2 * own_req * tiles
    total = -(-(high + 3 * top) // 16) * 16

    def body(q_ref, res_ref, ids_ref, gates_ref, out_ref, scr):
        scr[...] = jnp.zeros((total, 128), F32)
        for n, ref in enumerate((q_ref, res_ref)):
            for i in range(tiles):
                low = (n * tiles + i) * own_req
                scr[low : low + own_req, :] = ref[0:own_req, 128 * i : 128 * (i + 1)].astype(F32)
        gates = gates_ref[...]
        gates_high = gates.astype(BF16).astype(F32)
        for n, x in enumerate((ids_ref[...].astype(F32), gates_high, gates - gates_high)):
            scr[high + n * top : high + (n + 1) * top, 0:rows] = x
        packed = scr[...].astype(BF16)
        for g in range(n_pg):
            out_ref[g] = packed

    return call(body, [((n_pg, total, 128), BF16)], [pltpu.VMEM((total, 128), F32)])(
        queries, residual, expert_ids.T, route_weight.T
    )[0]


def unpack(sent_ref, out, which, own_req):
    tiles = out.shape[1] // 128
    for g in range(sent_ref.shape[0]):
        for i in range(tiles):
            low = (which * tiles + i) * own_req
            out[g * own_req : (g + 1) * own_req, 128 * i : 128 * (i + 1)] = sent_ref[
                g, low : low + own_req, :
            ].astype(F32)


def routing(sent_ref, me, masks, first, top, count):
    got = jnp.concatenate(
        [sent_ref[me ^ mask, first : first + 3 * top, 0:count].astype(F32) for mask in masks],
        axis=1,
    )
    return jnp.concatenate([got[0:top], got[top : 2 * top] + got[2 * top :]], axis=0)


def group_masks(g, zs):
    return [4 * z + 2 * (g % 2) + g // 2 for z in range(zs)]


def page_attention(sent, kv_cache, owner, live, own_req, cols):
    groups = sent.shape[0]
    pages, kv_here, page_len, wide = kv_cache.shape
    head_dim = wide // 2
    heads = cols // head_dim
    group = heads // kv_here
    rows = 16
    requests = groups * own_req
    keys = kv_here * page_len
    total = pages * rows

    def body(owner_col, live_col, sent_ref, kv_ref, out_ref, q_all, scores, probs, acc):
        unpack(sent_ref, q_all, 0, own_req)
        pick = (owner_col[...] == iota((total, requests), 1)).astype(BF16)
        wide_q = dot(pick, q_all[...].astype(BF16))
        spread = iota((total, cols), 0) % rows == iota((total, cols), 1) // head_dim
        fold = (iota((cols, wide), 0) % head_dim == iota((cols, wide), 1)).astype(BF16)
        q = dot(jnp.where(spread, wide_q, 0.0).astype(BF16), fold).astype(BF16)
        for p in range(pages):
            part = slice(p * rows, (p + 1) * rows)
            scores[part, :] = dot_t(q[part], kv_ref[p].reshape(keys, wide)) * head_dim ** (-0.5)
        col = iota((total, keys), 1)
        ok = (col // page_len == iota((total, keys), 0) % rows // group) & (
            col % page_len < live_col[...]
        )
        masked = jnp.where(ok, scores[...], NEG_FILL)
        top = jnp.max(masked, axis=1, keepdims=True).astype(BF16).astype(F32)
        share = jnp.where(ok, jnp.exp(masked - top), 0.0).astype(BF16)
        probs[...] = share
        whole = jnp.sum(share.astype(F32), axis=1, keepdims=True)
        for p in range(pages):
            part = slice(p * rows, (p + 1) * rows)
            acc[part, :] = dot(probs[part, :], kv_ref[p].reshape(keys, wide))
        unfold = (iota((wide, cols), 0) - head_dim == iota((wide, cols), 1) % head_dim).astype(BF16)
        here = iota((total, 128), 0) % rows == iota((total, 128), 1)
        merge = (iota((pages, total), 0) == iota((pages, total), 1) // rows).astype(BF16)
        flat = jnp.where(spread, dot(acc[...].astype(BF16), unfold), 0.0).astype(BF16)
        out_ref[:, 0:cols] = dot(merge, flat).astype(BF16)
        flat = jnp.where(here, top, 0.0).astype(BF16)
        out_ref[:, cols : cols + 128] = dot(merge, flat).astype(BF16)
        flat = jnp.where(here, whole, 0.0).astype(BF16)
        out_ref[:, cols + 128 :] = dot(merge, flat).astype(BF16)

    return call(
        body,
        [((pages, cols + 256), BF16)],
        [
            pltpu.VMEM((requests, cols), F32),
            pltpu.VMEM((total, keys), F32),
            pltpu.VMEM((total, keys), BF16),
            pltpu.VMEM((total, wide), F32),
        ],
    )(jnp.repeat(owner, rows)[:, None], jnp.repeat(live, rows)[:, None], sent, kv_cache)[0]


def half_products(left, w_ref, res, me, cols, send, base):
    mine = pl.multiple_of(me[0] * cols, 128)
    other = pl.multiple_of((1 - me[0]) * cols, 128)
    send[:, 0:cols] = dot(left, w_ref[:, pl.ds(other, cols)]).astype(BF16)
    own = dot(left, w_ref[:, pl.ds(mine, cols)]).astype(BF16).astype(F32) + res
    base[...] = own
    send[:, cols:] = own.astype(BF16)


def project_prefill(prefill, weight, residual, me_kv):
    rows, cols = residual.shape
    skip = rows - prefill.shape[0]

    def body(me, pre, w_ref, res, send, base, rows_scr):
        rows_scr[0:skip, :] = jnp.zeros((skip, cols), F32)
        rows_scr[skip:, :] = pre[...].astype(F32)
        left = rows_scr[...].astype(BF16)
        half_products(left, w_ref, res[...].astype(F32), me, cols, send, base)

    return call(
        body,
        [((rows, 2 * cols), BF16), ((rows, cols), F32)],
        [pltpu.VMEM((rows, cols), F32)],
        smem=(0,),
    )(me_kv, prefill, weight, residual)


def project_decode(pieces, where, sent, weight, me_kv, own_req, head_dim):
    groups = sent.shape[0]
    cols = weight.shape[0]
    requests = groups * own_req
    entries = where.shape[0]
    count = len(pieces)
    total = count * pieces[0].shape[0]

    def body(me, where_ref, w_ref, sent_ref, *refs):
        send, base, res = refs[count:]
        unpack(sent_ref, res, 1, own_req)
        table = jnp.concatenate([ref[...] for ref in refs[:count]], axis=0)
        pick = (where_ref[...] == iota((entries, total), 1)).astype(BF16)
        got = dot(pick, table)
        parts = [got[n : n + requests] for n in range(0, entries, requests)]
        sums = [part[:, cols + 128 :] for part in parts]
        tops = [
            jnp.where(tot > 0.0, part[:, cols : cols + 128], NEG_FILL)
            for part, tot in zip(parts, sums)
        ]
        best = functools.reduce(jnp.maximum, tops)
        scales = [jnp.where(tot > 0.0, jnp.exp(top - best), 0.0) for top, tot in zip(tops, sums)]
        whole = functools.reduce(jnp.add, [scale * tot for scale, tot in zip(scales, sums)])
        whole = jnp.where(whole > 0.0, whole, 1.0)
        expand = (iota((128, cols), 0) == iota((128, cols), 1) // head_dim).astype(BF16)
        share = jnp.concatenate([scale / whole for scale in scales], axis=0)
        share_high = share.astype(BF16)
        share_low = (share - share_high.astype(F32)).astype(BF16)
        wide = dot(share_high, expand) + dot(share_low, expand)
        merged = jnp.zeros((requests, cols), F32)
        for n, part in enumerate(parts):
            merged += wide[n * requests : (n + 1) * requests] * part[:, 0:cols]
        half_products(merged.astype(BF16), w_ref, res[...], me, cols, send, base)

    return call(
        body,
        [((requests, 2 * cols), BF16), ((requests, cols), F32)],
        [pltpu.VMEM((requests, cols), F32)],
        smem=(0,),
    )(me_kv, where, weight, sent, *pieces)


def norm_and_pages(base, sent, got, gain, pages):
    rows, cols = base.shape
    count, wide = pages.shape
    lanes = wide * count // rows

    def body(base_ref, sent_ref, got_ref, gain_ref, pages_ref, middle, out):
        mid = base_ref[...] + got_ref[:, 0:cols].astype(F32)
        far = got_ref[:, cols:].astype(F32) + sent_ref[:, 0:cols].astype(F32)
        squares = jnp.sum(mid * mid + far * far, axis=1, keepdims=True)
        middle[...] = mid
        out[:, 0:cols] = (
            mid * lax.rsqrt(squares / (2 * cols) + EPSILON) * gain_ref[...]
        ).astype(BF16)
        for n in range(rows // count):
            out[n * count : (n + 1) * count, cols:] = pages_ref[:, n * lanes : (n + 1) * lanes]

    return call(body, [((rows, cols), F32), ((rows, cols + lanes), BF16)])(
        base, sent, got, gain.reshape(1, -1), pages
    )


def join(parts, cols, pages):
    rows, wide = parts[0].shape
    lanes = wide - cols
    count = len(parts)
    quarters = rows // pages

    def body(*refs):
        outs, out_pages = refs[-3:-1], refs[-1]
        for n in range(count):
            low = n % (count // 2) * rows
            outs[n // (count // 2)][low : low + rows, :] = refs[n][:, 0:cols]
            for k in range(quarters):
                out_pages[n * pages : (n + 1) * pages, k * lanes : (k + 1) * lanes] = refs[n][
                    k * pages : (k + 1) * pages, cols:
                ]

    return call(
        body,
        [((count // 2 * rows, cols), BF16)] * 2 + [((count * pages, quarters * lanes), BF16)],
    )(*parts)


def first_norm(base, sent, got, gain):
    rows, cols = base.shape

    def body(base_ref, sent_ref, got_ref, gain_ref, middle, normed):
        mid = base_ref[...] + got_ref[:, 0:cols].astype(F32)
        far = got_ref[:, cols:].astype(F32) + sent_ref[:, 0:cols].astype(F32)
        squares = jnp.sum(mid * mid + far * far, axis=1, keepdims=True)
        middle[...] = mid
        normed[...] = (
            mid * lax.rsqrt(squares / (2 * cols) + EPSILON) * gain_ref[...]
        ).astype(BF16)

    return call(body, [((rows, cols), F32), ((rows, cols), BF16)])(
        base, sent, got, gain.reshape(1, -1)
    )


def routes(info, experts, slots, block_rows, skip):
    top = info.shape[0] // 2
    tokens = info.shape[1]
    token = iota((top, tokens), 1) % block_rows
    odd = (token + iota((top, tokens), 0)) % 2 == 1
    hits, gates = [], []
    for s in range(slots):
        wanted = jnp.where(odd, experts[1, s], experts[0, s]).astype(F32)
        hit = (info[0:top] == wanted) & (token >= skip)
        hits.append(jnp.sum(hit.astype(F32), axis=0, keepdims=True))
        gates.append(jnp.sum(jnp.where(hit, info[top:], 0.0), axis=0, keepdims=True))
    fill = [jnp.zeros((8 - slots, tokens), F32)] if slots < 8 else []
    stacked = jnp.concatenate(hits + fill, axis=0)
    row, col = iota((tokens, tokens), 0), iota((tokens, tokens), 1)
    before = ((row < col) & (row // block_rows == col // block_rows)).astype(BF16)
    ranks = dot(stacked.astype(BF16), before).astype(jnp.int32)
    places = [jnp.where(hits[s] > 0.0, ranks[s : s + 1], -1) for s in range(slots)]
    return places, gates


def one_hot(place, block_rows):
    tokens = place.shape[1]
    shape = (tokens // block_rows * CAP, tokens)
    row = iota(shape, 0)
    return (place == row % CAP) & (iota(shape, 1) // block_rows == row // CAP)


def plan(sent, first, top, experts, me_pg, slots, rows, skip, zs):
    part = zs * CAP
    tokens = zs * rows

    def body(pg, es, sent_ref, picks, gates, dec_gates):
        for g in range(4):
            info = routing(sent_ref, pg[0], group_masks(g, zs), first, top, rows)
            places, shares = routes(info, es, slots, rows, 0 if g % 2 else skip)
            for s in range(slots):
                hot = one_hot(places[s], rows)
                low = s * part
                picks[g, low : low + part, :] = hot.astype(BF16)
                gates[g, low : low + part, :] = jnp.broadcast_to(
                    jnp.sum(jnp.where(hot, shares[s], 0.0), axis=1, keepdims=True), (part, 128)
                )
        masks = group_masks(0, zs) + group_masks(2, zs)
        count = len(masks) * skip
        info = routing(sent_ref, pg[0], masks, first, top, skip)
        ids, shares = info[0:top], info[top:]
        odd = (iota((top, count), 1) % skip + iota((top, count), 0)) % 2 == 1
        eye = iota((count, count), 0) == iota((count, count), 1)
        for s in range(slots):
            wanted = jnp.where(odd, es[1, s], es[0, s]).astype(F32)
            share = jnp.sum(jnp.where(ids == wanted, shares, 0.0), axis=0, keepdims=True)
            dec_gates[s * count : (s + 1) * count, :] = jnp.broadcast_to(
                jnp.sum(jnp.where(eye, share, 0.0), axis=1, keepdims=True), (count, 128)
            )

    return call(
        body,
        [
            ((4, slots * part, tokens), BF16),
            ((4, slots * part, 128), F32),
            ((slots * 2 * zs * skip, 128), F32),
        ],
        smem=(0, 1),
    )(me_pg, experts, sent)


def load(arrays):
    count = len(arrays)

    def body(*refs):
        sems = refs[-1]
        copies = [
            pltpu.make_async_copy(refs[n].at[s], refs[count + n].at[s], sems.at[n, s])
            for n in range(count)
            for s in range(arrays[n].shape[0])
        ]
        for copy in copies:
            copy.start()
        for copy in copies:
            copy.wait()

    return call(
        body,
        [(x.shape, x.dtype) for x in arrays],
        [pltpu.SemaphoreType.DMA((count, arrays[0].shape[0]))],
        hbm=tuple(range(count)),
        vmem=44,
    )(*arrays)


def products(xs, w_ref, side, out):
    half = out.shape[2] // 2
    for s in range(out.shape[0]):
        x = xs[s] if len(xs.shape) == 3 else xs[...]
        for k in range(2):
            low = pl.multiple_of(k * 2 * half + side * half, 128)
            out[s, :, k * half : (k + 1) * half] = dot(x, w_ref[s, :, pl.ds(low, half)]).astype(
                out.dtype
            )


def gather(groups, which, picks, w, me_kv, me_pg, rows, skip, decode=None):
    count, slots = len(groups), w.shape[0]
    pieces = len(groups[0])
    cols = w.shape[1]
    tokens = pieces * groups[0][0].shape[0]
    zs = tokens // rows
    part = zs * CAP
    ff = w.shape[2] // 2

    def body(me, pg, w_ref, picks_ref, *refs):
        xs, send = refs[-2:]
        for n, g in enumerate(which):
            x = jnp.concatenate(
                [ref[...] for ref in refs[n * pieces : (n + 1) * pieces]], axis=0
            )
            if decode is not None:
                dec = refs[count * pieces][...]
                shape = (tokens, dec.shape[0])
                row = iota(shape, 0)
                source = jnp.zeros(shape, jnp.int32)
                for z, mask in enumerate(group_masks(g, zs)):
                    source = jnp.where(row // rows == z, (pg[0] ^ mask) * skip, source)
                late = row % rows < skip
                put = late & (iota(shape, 1) == source + row % rows)
                x = jnp.where(
                    iota((tokens, cols), 0) % rows < skip,
                    dot(put.astype(BF16), dec),
                    x.astype(F32),
                ).astype(BF16)
            got = dot(picks_ref[g], x).astype(BF16)
            for s in range(slots):
                xs[s, n * part : (n + 1) * part, :] = got[s * part : (s + 1) * part]
        products(xs, w_ref, 1 - me[0], send)

    more = [] if decode is None else [decode]
    return call(
        body,
        [((slots, count * part, cols), BF16), ((slots, count * part, ff), BF16)],
        smem=(0, 1),
    )(me_kv, me_pg, w, picks, *[x for group in groups for x in group], *more)


def pick_decode(normed, w, me_kv, me_pg, skip, zs):
    slots = w.shape[0]
    total, cols = normed.shape
    masks = group_masks(0, zs) + group_masks(2, zs)
    rows = len(masks) * skip

    def body(me, pg, w_ref, x_ref, xs, send):
        row = iota((rows, total), 0)
        source = jnp.zeros((rows, total), jnp.int32)
        for n, mask in enumerate(masks):
            source = jnp.where(row // skip == n, (pg[0] ^ mask) * skip, source)
        put = iota((rows, total), 1) == source + row % skip
        xs[...] = dot(put.astype(BF16), x_ref[...]).astype(BF16)
        products(xs, w_ref, 1 - me[0], send)

    return call(
        body, [((rows, cols), BF16), ((slots, rows, w.shape[2] // 2), BF16)], smem=(0, 1)
    )(me_kv, me_pg, w, normed)


def own_products(xs, w, me_kv):
    def body(me, w_ref, x_ref, out):
        products(x_ref, w_ref, me[0], out)

    return call(body, [((w.shape[0], xs.shape[-2], w.shape[2] // 2), F32)], smem=(0,))(
        me_kv, w, xs
    )[0]


def activate(own, got):
    slots, rows, ff = own.shape
    half = ff // 2

    def body(own_ref, got_ref, out):
        gate = own_ref[:, :, 0:half] + got_ref[:, :, 0:half].astype(F32)
        up = own_ref[:, :, half:] + got_ref[:, :, half:].astype(F32)
        out[...] = (gate / (1.0 + jnp.exp(-gate)) * up).astype(BF16)

    return call(body, [((slots, rows, half), BF16)])(own, got)[0]


def outputs(near_ref, far_ref, w_ref, me, s):
    half = near_ref.shape[2]
    made = dot(near_ref[s], w_ref[s, pl.ds(pl.multiple_of(me * half, 128), half), :])
    return made + dot(far_ref[s], w_ref[s, pl.ds(pl.multiple_of((1 - me) * half, 128), half), :])


def down_decode(near, far, w_down, gates, me_kv):
    slots, rows, _ = near.shape
    cols = w_down.shape[2]

    def body(me, w_ref, near_ref, far_ref, gates_ref, out):
        total = jnp.zeros((rows, cols), F32)
        for s in range(slots):
            made = outputs(near_ref, far_ref, w_ref, me[0], s)
            gate = gates_ref[s * rows : (s + 1) * rows, 0:1]
            total = total + made.astype(BF16).astype(F32) * gate
        out[...] = total

    return call(body, [((rows, cols), F32)], smem=(0,))(me_kv, w_down, near, far, gates)[0]


def down(near, far, w_down, which, picks, gates, me_kv, rows, skip, decode=None):
    slots, total_rows, _ = near.shape
    cols = w_down.shape[2]
    count = len(which)
    part = total_rows // count
    blocks = part // CAP

    def body(me, w_ref, near_ref, far_ref, picks_ref, gates_ref, *refs):
        outs = refs[-count:]
        made = [outputs(near_ref, far_ref, w_ref, me[0], s) for s in range(slots)]
        for n, g in enumerate(which):
            parts = jnp.concatenate(
                [made[s][n * part : (n + 1) * part] for s in range(slots)], axis=0
            )
            parts = (parts * gates_ref[g, :, 0:1]).astype(BF16)
            total = t_dot(picks_ref[g], parts)
            outs[n][...] = total.astype(BF16)
            if decode is None:
                continue
            for b in range(blocks):
                late = (n * blocks + b) * skip
                late = jnp.concatenate(
                    [refs[0][late : late + skip, :], total[b * rows + skip : b * rows + 16]], axis=0
                )
                outs[n][b * rows : b * rows + 16, :] = late.astype(BF16)

    more = [] if decode is None else [decode]
    return call(body, [((blocks * rows, cols), BF16)] * count, smem=(0,))(
        me_kv, w_down, near, far, picks, gates, *more
    )


def split_sum(a, b, blocks, first=BF16):
    tokens, cols = a.shape
    high = tokens // blocks

    def body(a_ref, b_ref, *outs):
        for n in range(blocks):
            part = slice(n * high, (n + 1) * high)
            total = a_ref[part, :].astype(F32) + b_ref[part, :].astype(F32)
            outs[n][...] = total.astype(outs[n].dtype)

    return call(body, [((high, cols), first)] + [((high, cols), BF16)] * (blocks - 1))(a, b)


def line_base(middle, decode_middle, own, parts, me_pg, skip):
    rows, cols = middle.shape

    def body(pg, mid, dec, *refs):
        out = refs[-1]
        total = refs[0][...]
        for ref in refs[1:-1]:
            total = total + ref[...].astype(F32)
        out[...] = total + mid[...]
        put = iota((8, dec.shape[0]), 1) == pg[0] * skip + iota((8, dec.shape[0]), 0)
        put = put & (iota((8, dec.shape[0]), 0) < skip)
        stream = dot(put.astype(F32), dec[...], HIGH)
        stream = jnp.where(iota((8, cols), 0) < skip, stream, mid[0:8, :])
        out[0:8, :] = total[0:8] + stream

    return call(body, [((rows, cols), F32)], smem=(0,))(
        me_pg, middle, decode_middle, own, *parts
    )[0]


def close(base, parts):
    rows, cols = base.shape

    def body(base_ref, *refs):
        mixed, squares = refs[-2:]
        total = base_ref[...]
        for ref in refs[:-2]:
            total = total + ref[...].astype(F32)
        mixed[...] = total
        total = total * total
        folded = total[:, 0:128]
        for n in range(1, cols // 128):
            folded = folded + total[:, n * 128 : (n + 1) * 128]
        squares[...] = folded

    return call(body, [((rows, cols), F32), ((rows, 128), F32)])(base, *parts)


def last_norm(mixed, near, far, gain):
    rows, cols = mixed.shape

    def body(mixed_ref, near_ref, far_ref, gain_ref, out):
        squares = jnp.sum(near_ref[...] + far_ref[...], axis=1, keepdims=True)
        out[...] = (
            mixed_ref[...] * lax.rsqrt(squares / (2 * cols) + EPSILON) * gain_ref[...]
        ).astype(BF16)

    return call(body, [((rows, cols), BF16)])(mixed, near, far, gain.reshape(1, -1))[0]


def line_pg(x, n_pg):
    return [x] + [swap_pg(x, 4 * z, n_pg) for z in range(1, n_pg // 4)]


def fast_local(
    residual_in,
    queries,
    prefill_attn,
    kv_cache,
    page_table,
    lengths,
    out_weight,
    norm_gain_in,
    norm_gain_out,
    expert_ids,
    route_weight,
    slot_table,
    w_gate_up,
    w_down,
):
    n_pg = lax.axis_size("pg")
    me = lax.axis_index("pg")
    me_kv = lax.axis_index("kv").reshape(1).astype(jnp.int32)
    me_pg = me.reshape(1).astype(jnp.int32)
    rows, cols = residual_in.shape
    own_req = queries.shape[0]
    slots = w_gate_up.shape[0]
    pages, _, page_len, wide = kv_cache.shape
    head_dim = wide // 2
    max_pages = page_table.shape[1]
    top = expert_ids.shape[1]
    zs = n_pg // 4
    first = 2 * own_req * cols // 128

    packed = pack(queries, residual_in, expert_ids, route_weight, n_pg)
    sent = lax.all_to_all(packed, "pg", split_axis=0, concat_axis=0, tiled=True)
    send, base = project_prefill(after(prefill_attn, packed), out_weight, residual_in, me_kv)

    mine = me * slots + jnp.arange(slots, dtype=jnp.int32)
    expert = jnp.arange(slot_table.shape[0], dtype=jnp.int32)
    experts = jnp.max(
        jnp.where(slot_table[:, :, None] == mine[None, None, :], expert[:, None, None], -1), axis=0
    )
    page_ids = me * pages + jnp.arange(pages, dtype=jnp.int32)
    flat_table = page_table.reshape(-1)
    entry_index = jnp.arange(flat_table.shape[0], dtype=jnp.int32)
    found = jnp.sum(
        jnp.where(flat_table[None, :] == page_ids[:, None], entry_index[None, :], 0), axis=1
    )
    owner = found // max_pages
    owner_len = jnp.sum(
        jnp.where(
            owner[:, None] == jnp.arange(lengths.shape[0], dtype=jnp.int32)[None, :],
            lengths[None, :],
            0,
        ),
        axis=1,
    )
    live = owner_len - found % max_pages * page_len
    partial = page_attention(sent, kv_cache, owner, live, own_req, cols)
    middle, payload = norm_and_pages(
        base, send, after(swap_kv(send), partial), norm_gain_in, partial
    )
    line = [swap_pg(payload, 4 * z, n_pg) for z in range(1, zs)]
    picks, gates, dec_gates = plan(
        after(sent, payload), first, top, experts, me_pg, slots, rows, own_req, zs
    )
    w_units, w_rows = load(after([w_gate_up, w_down], picks))
    *near, near_pages = join([payload] + after(line, w_units), cols, pages)
    across_pages = swap_pg(near_pages, 2, n_pg)
    near_pages_core = swap_pg(near_pages, 1, n_pg)

    def swap_halves(halves, mask):
        return [swap_pg(x, mask, n_pg) for x in halves]

    def gathered(which, groups, decode=None):
        return gather(groups, which, picks, w_units, me_kv, me_pg, rows, own_req, decode)

    xs0, out0 = gathered([0, 2], [near, swap_halves(near, 1)])
    got0 = swap_kv(out0)
    across = swap_halves(near, 2)
    across_pages = after(across_pages, out0)
    pieces = [near_pages, across_pages, near_pages_core, swap_pg(across_pages, 1, n_pg)]
    away = (page_table.T // pages) ^ me
    where = ((away % 2) * 2 + away // 2 % 2) * zs + away // 4
    where = (where * pages + page_table.T % pages).reshape(-1, 1)
    dec_send, dec_base = project_decode(
        pieces, where, sent, out_weight, me_kv, own_req, head_dim
    )
    dec_got = swap_kv(dec_send)
    across = after(across, dec_send)
    across_core = swap_halves(across, 1)
    near0 = activate(own_products(xs0, w_units, me_kv), after(got0, across))
    far0 = swap_kv(near0)
    dec_middle, dec_normed = first_norm(dec_base, dec_send, after(dec_got, near0), norm_gain_in)
    xs2, out2 = pick_decode(dec_normed, w_units, me_kv, me_pg, own_req, zs)
    got2 = swap_kv(out2)
    xs1, out1 = gathered([1, 3], after([across, across_core], out2), dec_normed)
    got1 = swap_kv(out1)
    own1 = own_products(xs1, w_units, me_kv)
    own2 = own_products(xs2, w_units, me_kv)
    near2 = activate(own2, after(got2, out1))
    far2 = swap_kv(near2)
    decode = down_decode(near2, after(far2, far0), w_rows, dec_gates, me_kv)
    keep0, give0 = down(
        near0, far0, w_rows, [0, 2], picks, gates, me_kv, rows, own_req, decode
    )
    back0 = swap_pg(give0, 1, n_pg)
    near1 = activate(own1, after(got1, give0))
    far1 = swap_kv(near1)
    parts0 = split_sum(keep0, after(back0, near1), zs, F32)
    lines0 = [swap_pg(parts0[z], 4 * z, n_pg) for z in range(1, zs)]
    base = line_base(middle, dec_middle, parts0[0], lines0, me_pg, own_req)
    keep1, give1 = down(near1, after(far1, base), w_rows, [1, 3], picks, gates, me_kv, rows, own_req)
    parts1 = split_sum(keep1, swap_pg(give1, 1, n_pg), zs)
    mixed, squares = close(base, [swap_pg(parts1[z], 4 * z + 2, n_pg) for z in range(zs)])
    return last_norm(mixed, squares, swap_kv(squares), norm_gain_out)


def solution(mesh):
    fast = mesh.shape["kv"] == 2 and mesh.shape["pg"] == 16
    local = fast_local if fast else general_local
    in_specs = (
        P("pg", "kv"),
        P("pg", "kv"),
        P("pg", "kv"),
        P("pg", "kv", None, None),
        P(),
        P(),
        P("kv", None),
        P("kv"),
        P("kv"),
        P("pg", None),
        P("pg", None),
        P(),
        P("pg", "kv", None),
        P("pg", None, "kv"),
    )
    out_specs = P("pg", "kv")
    return jax.shard_map(local, mesh=mesh, in_specs=in_specs, out_specs=out_specs, check_vma=False)
```

```python
import functools

import jax
import jax.numpy as jnp
from jax import lax
from jax.experimental import pallas as pl
from jax.experimental.pallas import tpu as pltpu
from jax.sharding import PartitionSpec as P

NEG_FILL = -1e30
EPSILON = 1e-06


def merged_2(array, axis, join):
    gathered = jax.tree.map(
        lambda a, kind: lax.all_gather(a.astype(kind), axis),
        array,
        (jnp.bfloat16, jnp.bfloat16, jnp.bfloat16),
    )

    def take(source):
        return jax.tree.map(
            lambda a, own: lax.dynamic_index_in_dim(a, source, 0, False).astype(own.dtype),
            gathered,
            array,
        )

    return lax.fori_loop(
        1, lax.axis_size(axis), lambda source, state: join(state, take(source)), take(0)
    )


def merge_pair(first, secondary_slot):
    highest = jnp.maximum(first[0], secondary_slot[0])
    scale_a = jnp.exp(first[0] - highest)
    scale_b = jnp.exp(secondary_slot[0] - highest)
    head_count = first[0].shape[1]
    acc_a = first[2].reshape(first[2].shape[0], head_count, -1) * scale_a[:, :, None]
    acc_b = (
        secondary_slot[2].reshape(secondary_slot[2].shape[0], head_count, -1) * scale_b[:, :, None]
    )
    return (
        highest,
        first[1] * scale_a + secondary_slot[1] * scale_b,
        (acc_a + acc_b).reshape(first[2].shape),
    )


def general_local(
    residual_in,
    queries,
    prefill_attn,
    kv_cache,
    page_table,
    lengths,
    out_weight,
    norm_gain_in,
    norm_gain_out,
    expert_ids,
    route_weight,
    slot_table,
    w_gate_up,
    w_down,
):
    head_dim = kv_cache.shape[3] // 2
    page_len = kv_cache.shape[2]
    pages_here = kv_cache.shape[0]
    kv_here = kv_cache.shape[1]
    own_req = queries.shape[0]
    heads_here = queries.shape[1] // head_dim
    head_group = heads_here // kv_here
    total_req = page_table.shape[0]
    max_pages = page_table.shape[1]
    full_gate_up, full_down = (
        lax.all_gather(w_gate_up, "kv", axis=1, tiled=True),
        lax.all_gather(w_down, "kv", axis=2, tiled=True),
    )
    gathered = lax.all_gather(queries, "pg", axis=0, tiled=True)
    page_ids = lax.axis_index("pg") * pages_here + jnp.arange(pages_here, dtype=jnp.int32)
    flat_table = page_table.reshape(-1)
    entry_index = jnp.arange(flat_table.shape[0], dtype=jnp.int32)
    found = jnp.sum(
        jnp.where(flat_table[None, :] == page_ids[:, None], entry_index[None, :], 0), axis=1
    )
    owner = found // max_pages
    page_slot = found % max_pages
    owner_len = lengths[owner]
    query_pages = gathered[owner].reshape(pages_here, kv_here, head_group, head_dim)
    keys = kv_cache[:, :, :, :head_dim]
    values = kv_cache[:, :, :, head_dim:]
    scores = jnp.einsum(
        "pkgd,pktd->pkgt", query_pages, keys, preferred_element_type=jnp.float32
    ) * head_dim ** (-0.5)
    positions = page_slot[:, None] * page_len + jnp.arange(page_len, dtype=jnp.int32)[None, :]
    live = (positions < owner_len[:, None])[:, None, None, :]
    masked = jnp.where(live, scores, NEG_FILL)
    page_top = jnp.max(masked, axis=3)
    probs = jnp.where(live, jnp.exp(masked - page_top[..., None]), 0.0).astype(jnp.bfloat16)
    page_sum = jnp.sum(probs.astype(jnp.float32), axis=3).reshape(pages_here, heads_here)
    page_acc = jnp.einsum(
        "pkgt,pktd->pkgd", probs, values, preferred_element_type=jnp.float32
    ).reshape(pages_here, heads_here, head_dim)
    page_top = page_top.reshape(pages_here, heads_here)
    page_live = page_slot * page_len < owner_len
    member = (owner[:, None] == jnp.arange(total_req, dtype=jnp.int32)[None, :]) & page_live[
        :, None
    ]
    local_max = jnp.max(jnp.where(member[:, :, None], page_top[:, None, :], NEG_FILL), axis=0)
    member_t = member.astype(jnp.float32).T
    weight = jnp.exp(page_top - local_max[owner])
    sums = jnp.dot(member_t, weight * page_sum, precision=lax.Precision.HIGHEST)
    accs = jnp.dot(
        member_t,
        (weight[:, :, None] * page_acc).reshape(pages_here, -1),
        precision=lax.Precision.HIGHEST,
    )
    sums, accs = (sums, accs)
    merged = merged_2((local_max, sums, accs), "pg", merge_pair)
    start = lax.axis_index("pg") * own_req
    own_sum = lax.dynamic_slice_in_dim(merged[1], start, own_req, 0)
    own_acc = lax.dynamic_slice_in_dim(merged[2], start, own_req, 0)
    attn_dec = (own_acc.reshape(own_req, heads_here, head_dim) / own_sum[:, :, None]).reshape(
        own_req, -1
    )
    attn_dec = attn_dec.astype(jnp.bfloat16)
    attn_rows = jnp.concatenate([attn_dec, prefill_attn], axis=0)
    projected = jnp.dot(attn_rows, out_weight, preferred_element_type=jnp.float32)
    mixed_in = lax.psum_scatter(
        projected.astype(jnp.bfloat16), "kv", scatter_dimension=1, tiled=True
    ).astype(jnp.float32)
    middle = residual_in.astype(jnp.float32) + mixed_in
    full_width = residual_in.shape[1] * lax.axis_size("kv")
    in_squares = lax.psum(jnp.sum(middle * middle, axis=1), "kv")
    normed = (middle * lax.rsqrt(in_squares / full_width + EPSILON)[:, None] * norm_gain_in).astype(
        jnp.bfloat16
    )
    token_rows, top = expert_ids.shape
    copies = slot_table.shape[1]
    experts_total = slot_table.shape[0]
    kv_count = lax.axis_size("kv")
    capacity = kv_count * max(
        1,
        (token_rows * top * 5 + 4 * experts_total * kv_count - 1) // (4 * experts_total * kv_count),
    )
    slots_here = w_gate_up.shape[0]
    groups = lax.axis_size("pg")
    all_slots = slots_here * groups
    feature_cols = normed.shape[1]
    row_ids = lax.axis_index("pg") * token_rows + jnp.arange(token_rows, dtype=jnp.int32)
    parity = (row_ids[:, None] + jnp.arange(top, dtype=jnp.int32)[None, :]) % copies
    route_key = (expert_ids * copies + parity).reshape(-1)
    table_flat = slot_table.reshape(-1)
    table_index = jnp.arange(table_flat.shape[0], dtype=jnp.int32)
    target_slot = jnp.sum(
        jnp.where(route_key[:, None] == table_index[None, :], table_flat[None, :], 0), axis=1
    )
    match_count = (target_slot[:, None] == jnp.arange(all_slots, dtype=jnp.int32)[None, :]).astype(
        jnp.int32
    )
    rank = jnp.sum((jnp.cumsum(match_count, axis=0) - match_count) * match_count, axis=1)
    dest = target_slot * capacity + rank
    source_row = jnp.arange(token_rows * top, dtype=jnp.int32) // top
    outgoing = (
        jnp.zeros((all_slots * capacity, feature_cols), jnp.bfloat16)
        .at[dest]
        .set(normed[source_row])
    )
    outgoing = outgoing.reshape(groups, slots_here, capacity, feature_cols)
    arrived = lax.all_to_all(outgoing, "pg", split_axis=0, concat_axis=0, tiled=True)
    widened = lax.all_to_all(arrived, "kv", split_axis=2, concat_axis=3, tiled=True)
    gate_up = jnp.einsum(
        "pscd,sdf->pscf", widened, full_gate_up, preferred_element_type=jnp.float32
    )
    half = gate_up.shape[3] // 2
    hidden = (jax.nn.silu(gate_up[..., :half]) * gate_up[..., half:]).astype(jnp.bfloat16)
    produced = jnp.einsum(
        "pscf,sfd->pscd", hidden, full_down, preferred_element_type=jnp.float32
    ).astype(jnp.bfloat16)
    narrowed = lax.all_to_all(produced, "kv", split_axis=3, concat_axis=2, tiled=True)
    returned = lax.all_to_all(narrowed, "pg", split_axis=0, concat_axis=0, tiled=True)
    returned = returned.reshape(all_slots * capacity, feature_cols)
    picked = returned[dest].astype(jnp.float32).reshape(token_rows, top, feature_cols)
    mixed = middle + jnp.sum(picked * route_weight[:, :, None], axis=1)
    out_squares = lax.psum(jnp.sum(mixed * mixed, axis=1), "kv")
    return (mixed * lax.rsqrt(out_squares / full_width + EPSILON)[:, None] * norm_gain_out).astype(
        jnp.bfloat16
    )


F32 = jnp.float32
BF16 = jnp.bfloat16
CAP = 16
HIGH = lax.Precision.HIGHEST


def call(body, outs, scratch=(), smem=(), hbm=(), vmem=16, flops=10**9):
    def run(*operands):
        kinds = [
            pltpu.SMEM if n in smem else pltpu.HBM if n in hbm else pltpu.VMEM
            for n in range(len(operands))
        ]
        return pl.pallas_call(
            body,
            out_shape=[jax.ShapeDtypeStruct(s, d) for s, d in outs],
            in_specs=[pl.BlockSpec(memory_space=kind) for kind in kinds],
            out_specs=[pl.BlockSpec(memory_space=pltpu.VMEM) for _ in outs],
            scratch_shapes=list(scratch),
            compiler_params=pltpu.CompilerParams(
                vmem_limit_bytes=vmem * 2**20
            ),
            cost_estimate=pl.CostEstimate(flops=flops, bytes_accessed=1, transcendentals=0),
        )(*operands)

    return run


def after(values, *earlier):
    return lax.optimization_barrier((values, earlier))[0]


def iota(shape, dim):
    return lax.broadcasted_iota(jnp.int32, shape, dim)


def dot(a, b, precision=None):
    return jnp.dot(a, b, preferred_element_type=F32, precision=precision)


def dot_t(a, b):
    return lax.dot_general(a, b, (((1,), (1,)), ((), ())), preferred_element_type=F32)


def t_dot(a, b):
    return lax.dot_general(a, b, (((0,), (0,)), ((), ())), preferred_element_type=F32)


def swap_kv(x):
    return lax.ppermute(x, "kv", [(0, 1), (1, 0)])


def swap_pg(x, mask, n):
    return lax.ppermute(x, "pg", [(i, i ^ mask) for i in range(n)])


def pack(queries, residual, expert_ids, route_weight, n_pg):
    own_req, cols = queries.shape
    rows, top = expert_ids.shape
    tiles = cols // 128
    high = 2 * own_req * tiles
    total = high + top

    def body(q_hbm, res_hbm, ids_hbm, gates_hbm, out_ref, scr, q_ref, res_ref, ids, gates, sems):
        copies = [
            pltpu.make_async_copy(q_hbm, q_ref, sems.at[0]),
            pltpu.make_async_copy(res_hbm.at[0:16, :], res_ref, sems.at[1]),
            pltpu.make_async_copy(ids_hbm, ids, sems.at[2]),
            pltpu.make_async_copy(gates_hbm, gates, sems.at[3]),
        ]
        for copy in copies:
            copy.start()
        for copy in copies:
            copy.wait()
        for n, ref in enumerate((q_ref, res_ref)):
            for i in range(tiles):
                low = (n * tiles + i) * own_req
                scr[low : low + own_req, :] = ref[0:own_req, 128 * i : 128 * (i + 1)].astype(F32)
        scr[high:, 0:rows] = ids[...].astype(F32)
        scr[high:, 64 : 64 + rows] = gates[...]
        packed = scr[...].astype(BF16)
        for g in range(n_pg):
            out_ref[g] = packed

    return call(
        body,
        [((n_pg, total, 128), BF16)],
        [
            pltpu.VMEM((total, 128), F32),
            pltpu.VMEM((own_req, cols), BF16),
            pltpu.VMEM((16, cols), BF16),
            pltpu.VMEM((top, rows), expert_ids.dtype),
            pltpu.VMEM((top, rows), F32),
            pltpu.SemaphoreType.DMA((4,)),
        ],
        hbm=(0, 1, 2, 3),
        vmem=62,
    )(queries, residual, expert_ids.T, route_weight.T)[0]


def unpack(sent_ref, out, which, own_req):
    tiles = out.shape[1] // 128
    for g in range(sent_ref.shape[0]):
        for i in range(tiles):
            low = (which * tiles + i) * own_req
            out[g * own_req : (g + 1) * own_req, 128 * i : 128 * (i + 1)] = sent_ref[
                g, low : low + own_req, :
            ].astype(F32)


def routing(sent_ref, me, masks, first, top, count):
    got = [sent_ref[me ^ mask, first : first + top, :].astype(F32) for mask in masks]
    ids = jnp.concatenate([x[:, 0:count] for x in got], axis=1)
    gates = jnp.concatenate([x[:, 64 : 64 + count] for x in got], axis=1)
    return jnp.concatenate([ids, gates], axis=0)


def group_masks(g, zs):
    return [4 * z + 2 * (g % 2) + g // 2 for z in range(zs)]


def page_attention(sent, kv_cache, owner, live, own_req, cols):
    groups = sent.shape[0]
    pages, kv_here, page_len, wide = kv_cache.shape
    head_dim = wide // 2
    heads = cols // head_dim
    group = heads // kv_here
    rows = 16
    requests = groups * own_req
    keys = kv_here * page_len
    total = pages * rows

    def body(owner_col, live_col, sent_ref, kv_ref, out_ref, q_all, scores, probs, acc):
        unpack(sent_ref, q_all, 0, own_req)
        pick = (owner_col[...] == iota((total, requests), 1)).astype(BF16)
        wide_q = dot(pick, q_all[...].astype(BF16))
        spread = iota((total, cols), 0) % rows == iota((total, cols), 1) // head_dim
        fold = (iota((cols, wide), 0) % head_dim == iota((cols, wide), 1)).astype(BF16)
        q = dot(jnp.where(spread, wide_q, 0.0).astype(BF16), fold).astype(BF16)
        for p in range(pages):
            part = slice(p * rows, (p + 1) * rows)
            scores[part, :] = dot_t(q[part], kv_ref[p].reshape(keys, wide)) * head_dim ** (-0.5)
        col = iota((total, keys), 1)
        ok = (col // page_len == iota((total, keys), 0) % rows // group) & (
            col % page_len < live_col[...]
        )
        masked = jnp.where(ok, scores[...], NEG_FILL)
        top = jnp.max(masked, axis=1, keepdims=True).astype(BF16).astype(F32)
        share = jnp.where(ok, jnp.exp(masked - top), 0.0).astype(BF16)
        probs[...] = share
        whole = jnp.sum(share.astype(F32), axis=1, keepdims=True)
        for p in range(pages):
            part = slice(p * rows, (p + 1) * rows)
            acc[part, :] = dot(probs[part, :], kv_ref[p].reshape(keys, wide))
        unfold = (iota((wide, cols), 0) - head_dim == iota((wide, cols), 1) % head_dim).astype(BF16)
        here = iota((total, 128), 0) % rows == iota((total, 128), 1)
        merge = (iota((pages, total), 0) == iota((pages, total), 1) // rows).astype(BF16)
        flat = jnp.where(spread, dot(acc[...].astype(BF16), unfold), 0.0).astype(BF16)
        out_ref[:, 0:cols] = dot(merge, flat).astype(BF16)
        flat = jnp.where(here, top, 0.0).astype(BF16)
        out_ref[:, cols : cols + 128] = dot(merge, flat).astype(BF16)
        flat = jnp.where(here, whole, 0.0).astype(BF16)
        out_ref[:, cols + 128 :] = dot(merge, flat).astype(BF16)

    return call(
        body,
        [((pages, cols + 256), BF16)],
        [
            pltpu.VMEM((requests, cols), F32),
            pltpu.VMEM((total, keys), F32),
            pltpu.VMEM((total, keys), BF16),
            pltpu.VMEM((total, wide), F32),
        ],
    )(jnp.repeat(owner, rows)[:, None], jnp.repeat(live, rows)[:, None], sent, kv_cache)[0]


def half_products(left, w_ref, res, me, cols, far, near, base):
    mine = pl.multiple_of(me[0] * cols, 128)
    other = pl.multiple_of((1 - me[0]) * cols, 128)
    far[...] = dot(left, w_ref[:, pl.ds(other, cols)]).astype(BF16)
    own = dot(left, w_ref[:, pl.ds(mine, cols)]).astype(BF16).astype(F32) + res
    base[...] = own
    near[...] = own.astype(BF16)


def project_prefill(prefill, weight, residual, me_kv):
    rows, cols = residual.shape
    skip = rows - prefill.shape[0]

    def body(me, pre, w_ref, res, far, near, base, rows_scr):
        rows_scr[0:skip, :] = jnp.zeros((skip, cols), F32)
        rows_scr[skip:, :] = pre[...].astype(F32)
        left = rows_scr[...].astype(BF16)
        half_products(left, w_ref, res[...].astype(F32), me, cols, far, near, base)

    return call(
        body,
        [((rows, cols), BF16)] * 2 + [((rows, cols), F32)],
        [pltpu.VMEM((rows, cols), F32)],
        smem=(0,),
    )(me_kv, prefill, weight, residual)


def project_decode(pieces, page_table, pages, sent, weight, me_kv, me_pg, own_req, head_dim):
    groups = sent.shape[0]
    cols = weight.shape[0]
    requests = groups * own_req
    entries = page_table.size
    count = len(pieces)
    high = pieces[0].shape[0]
    total = count * high

    def body(me, pg, table_ref, w_ref, sent_ref, *refs):
        far, near, base, res = refs[count:]
        unpack(sent_ref, res, 1, own_req)
        table = jnp.concatenate([ref[...] for ref in refs[:count]], axis=0)
        page = jnp.concatenate(
            [table_ref[j : j + 1, :] for j in range(entries // requests)], axis=1
        )
        away = (page // pages) ^ pg[0]
        where = ((away % 2) * 2 + away // 2 % 2) * high + away // 4 * pages + page % pages
        pick = (iota((total, entries), 0) == where).astype(BF16)
        got = t_dot(pick, table)
        parts = [got[n : n + requests] for n in range(0, entries, requests)]
        sums = [part[:, cols + 128 :] for part in parts]
        tops = [
            jnp.where(tot > 0.0, part[:, cols : cols + 128], NEG_FILL)
            for part, tot in zip(parts, sums)
        ]
        best = functools.reduce(jnp.maximum, tops)
        scales = [jnp.where(tot > 0.0, jnp.exp(top - best), 0.0) for top, tot in zip(tops, sums)]
        whole = functools.reduce(jnp.add, [scale * tot for scale, tot in zip(scales, sums)])
        whole = jnp.where(whole > 0.0, whole, 1.0)
        expand = (iota((128, cols), 0) == iota((128, cols), 1) // head_dim).astype(BF16)
        share = jnp.concatenate([scale / whole for scale in scales], axis=0)
        share_high = share.astype(BF16)
        share_low = (share - share_high.astype(F32)).astype(BF16)
        wide = dot(share_high, expand) + dot(share_low, expand)
        merged = jnp.zeros((requests, cols), F32)
        for n, part in enumerate(parts):
            merged += wide[n * requests : (n + 1) * requests] * part[:, 0:cols]
        half_products(merged.astype(BF16), w_ref, res[...], me, cols, far, near, base)

    return call(
        body,
        [((requests, cols), BF16)] * 2 + [((requests, cols), F32)],
        [pltpu.VMEM((requests, cols), F32)],
        smem=(0, 1),
    )(me_kv, me_pg, page_table.T, weight, sent, *pieces)


def norm_and_pages(base, sent, got_own, got_far, gain, pages):
    rows, cols = base.shape
    count, wide = pages.shape
    lanes = wide * count // rows

    def body(base_ref, sent_ref, got_ref, far_ref, gain_ref, pages_ref, middle, out):
        mid = base_ref[...] + got_ref[...].astype(F32)
        far = far_ref[...].astype(F32) + sent_ref[...].astype(F32)
        squares = jnp.sum(mid * mid + far * far, axis=1, keepdims=True)
        middle[...] = mid
        out[:, 0:cols] = (
            mid * lax.rsqrt(squares / (2 * cols) + EPSILON) * gain_ref[...]
        ).astype(BF16)
        for n in range(rows // count):
            out[n * count : (n + 1) * count, cols:] = pages_ref[:, n * lanes : (n + 1) * lanes]

    return call(body, [((rows, cols), F32), ((rows, cols + lanes), BF16)])(
        base, sent, got_own, got_far, gain.reshape(1, -1), pages
    )


def join(parts, cols, pages):
    rows, wide = parts[0].shape
    lanes = wide - cols
    count = len(parts)
    quarters = rows // pages

    def body(*refs):
        outs, out_pages = refs[-3:-1], refs[-1]
        for n in range(count):
            low = n % (count // 2) * rows
            outs[n // (count // 2)][low : low + rows, :] = refs[n][:, 0:cols]
            for k in range(quarters):
                out_pages[n * pages : (n + 1) * pages, k * lanes : (k + 1) * lanes] = refs[n][
                    k * pages : (k + 1) * pages, cols:
                ]

    return call(
        body,
        [((count // 2 * rows, cols), BF16)] * 2 + [((count * pages, quarters * lanes), BF16)],
    )(*parts)


def first_norm(base, sent, got_own, got_far, gain):
    rows, cols = base.shape

    def body(base_ref, sent_ref, got_ref, far_ref, gain_ref, middle, normed):
        mid = base_ref[...] + got_ref[...].astype(F32)
        far = far_ref[...].astype(F32) + sent_ref[...].astype(F32)
        squares = jnp.sum(mid * mid + far * far, axis=1, keepdims=True)
        middle[...] = mid
        normed[...] = (
            mid * lax.rsqrt(squares / (2 * cols) + EPSILON) * gain_ref[...]
        ).astype(BF16)

    return call(body, [((rows, cols), F32), ((rows, cols), BF16)])(
        base, sent, got_own, got_far, gain.reshape(1, -1)
    )


def routes(info, experts, slots, block_rows, skip):
    top = info.shape[0] // 2
    tokens = info.shape[1]
    token = iota((top, tokens), 1) % block_rows
    odd = (token + iota((top, tokens), 0)) % 2 == 1
    hits, gates = [], []
    for s in range(slots):
        wanted = jnp.where(odd, experts[1, s], experts[0, s]).astype(F32)
        hit = (info[0:top] == wanted) & (token >= skip)
        hits.append(jnp.sum(hit.astype(F32), axis=0, keepdims=True))
        gates.append(jnp.sum(jnp.where(hit, info[top:], 0.0), axis=0, keepdims=True))
    fill = [jnp.zeros((8 - slots, tokens), F32)] if slots < 8 else []
    stacked = jnp.concatenate(hits + fill, axis=0)
    row, col = iota((tokens, tokens), 0), iota((tokens, tokens), 1)
    before = ((row < col) & (row // block_rows == col // block_rows)).astype(BF16)
    ranks = dot(stacked.astype(BF16), before).astype(jnp.int32)
    places = [jnp.where(hits[s] > 0.0, ranks[s : s + 1], -1) for s in range(slots)]
    return places, gates


def one_hot(place, block_rows):
    tokens = place.shape[1]
    shape = (tokens // block_rows * CAP, tokens)
    row = iota(shape, 0)
    return (place == row % CAP) & (iota(shape, 1) // block_rows == row // CAP)


def plan(sent, first, top, experts, me_pg, slots, rows, skip, zs):
    part = zs * CAP
    tokens = zs * rows

    def body(pg, es, sent_ref, picks, gates, dec_gates):
        for g in range(4):
            info = routing(sent_ref, pg[0], group_masks(g, zs), first, top, rows)
            places, shares = routes(info, es, slots, rows, 0 if g % 2 else skip)
            for s in range(slots):
                hot = one_hot(places[s], rows)
                low = s * part
                picks[g, low : low + part, :] = hot.astype(BF16)
                gates[g, low : low + part, :] = jnp.broadcast_to(
                    jnp.sum(jnp.where(hot, shares[s], 0.0), axis=1, keepdims=True), (part, 128)
                )
        masks = group_masks(0, zs) + group_masks(2, zs)
        count = len(masks) * skip
        info = routing(sent_ref, pg[0], masks, first, top, skip)
        ids, shares = info[0:top], info[top:]
        odd = (iota((top, count), 1) % skip + iota((top, count), 0)) % 2 == 1
        eye = iota((count, count), 0) == iota((count, count), 1)
        for s in range(slots):
            wanted = jnp.where(odd, es[1, s], es[0, s]).astype(F32)
            share = jnp.sum(jnp.where(ids == wanted, shares, 0.0), axis=0, keepdims=True)
            dec_gates[s * count : (s + 1) * count, :] = jnp.broadcast_to(
                jnp.sum(jnp.where(eye, share, 0.0), axis=1, keepdims=True), (count, 128)
            )

    return call(
        body,
        [
            ((4, slots * part, tokens), BF16),
            ((4, slots * part, 128), F32),
            ((slots * 2 * zs * skip, 128), F32),
        ],
        smem=(0, 1),
    )(me_pg, experts, sent)


def load(arrays):
    count = len(arrays)

    def body(*refs):
        sems = refs[-1]
        copies = [
            pltpu.make_async_copy(refs[n].at[s], refs[count + n].at[s], sems.at[n, s])
            for n in range(count)
            for s in range(arrays[n].shape[0])
        ]
        for copy in copies:
            copy.start()
        for copy in copies:
            copy.wait()

    return call(
        body,
        [(x.shape, x.dtype) for x in arrays],
        [pltpu.SemaphoreType.DMA((count, arrays[0].shape[0]))],
        hbm=tuple(range(count)),
        vmem=44,
    )(*arrays)


def products(xs, w_ref, side, *outs):
    half = outs[0].shape[2] // 2
    places = [(out, n) for out in outs for n in range(out.shape[0])]
    for s, (out, n) in enumerate(places):
        x = xs[s] if len(xs.shape) == 3 else xs[...]
        for k in range(2):
            low = pl.multiple_of(k * 2 * half + side * half, 128)
            out[n, :, k * half : (k + 1) * half] = dot(x, w_ref[s, :, pl.ds(low, half)]).astype(
                out.dtype
            )


def gather(groups, which, picks, w, me_kv, me_pg, rows, skip, parts, decode=None):
    count, slots = len(groups), w.shape[0]
    pieces = len(groups[0])
    cols = w.shape[1]
    tokens = pieces * groups[0][0].shape[0]
    zs = tokens // rows
    part = zs * CAP
    ff = w.shape[2] // 2

    def body(me, pg, w_ref, picks_ref, *refs):
        xs, sends = refs[-1 - len(parts)], refs[-len(parts) :]
        for n, g in enumerate(which):
            x = jnp.concatenate(
                [ref[...] for ref in refs[n * pieces : (n + 1) * pieces]], axis=0
            )
            if decode is not None:
                dec = refs[count * pieces][...]
                shape = (tokens, dec.shape[0])
                row = iota(shape, 0)
                source = jnp.zeros(shape, jnp.int32)
                for z, mask in enumerate(group_masks(g, zs)):
                    source = jnp.where(row // rows == z, (pg[0] ^ mask) * skip, source)
                late = row % rows < skip
                put = late & (iota(shape, 1) == source + row % rows)
                x = jnp.where(
                    iota((tokens, cols), 0) % rows < skip,
                    dot(put.astype(BF16), dec),
                    x.astype(F32),
                ).astype(BF16)
            got = dot(picks_ref[g], x).astype(BF16)
            for s in range(slots):
                xs[s, n * part : (n + 1) * part, :] = got[s * part : (s + 1) * part]
        products(xs, w_ref, 1 - me[0], *sends)

    more = [] if decode is None else [decode]
    high = count * part
    return call(
        body,
        [((slots, high, cols), BF16)] + [((n, high, ff), BF16) for n in parts],
        smem=(0, 1),
    )(me_kv, me_pg, w, picks, *[x for group in groups for x in group], *more)


def pick_decode(normed, w, me_pg, skip, zs):
    slots, _, wide = w.shape
    total, cols = normed.shape
    masks = group_masks(0, zs) + group_masks(2, zs)
    rows = len(masks) * skip

    def body(pg, w_ref, x_ref, own, send):
        row = iota((rows, total), 0)
        source = jnp.zeros((rows, total), jnp.int32)
        for n, mask in enumerate(masks):
            source = jnp.where(row // skip == n, (pg[0] ^ mask) * skip, source)
        put = iota((rows, total), 1) == source + row % skip
        x = dot(put.astype(BF16), x_ref[...]).astype(BF16)
        for s in range(slots):
            made = dot(x, w_ref[s])
            own[s] = made
            send[s] = made.astype(BF16)

    return call(body, [((slots, rows, wide), F32), ((slots, rows, wide), BF16)], smem=(0,))(
        me_pg, w, normed
    )


def own_products(xs, w, me_kv, flops=1):
    def body(me, w_ref, x_ref, out):
        products(x_ref, w_ref, me[0], out)

    return call(body, [((w.shape[0], xs.shape[-2], w.shape[2] // 2), F32)], smem=(0,), flops=flops)(
        me_kv, w, xs
    )[0]


def activate(own, got):
    slots, rows, ff = own.shape
    half = ff // 2

    def body(own_ref, *refs):
        places = [(ref, n) for ref in refs[:-1] for n in range(ref.shape[0])]
        for s, (ref, n) in enumerate(places):
            gate = own_ref[s, :, 0:half] + ref[n, :, 0:half].astype(F32)
            up = own_ref[s, :, half:] + ref[n, :, half:].astype(F32)
            refs[-1][s] = (gate / (1.0 + jnp.exp(-gate)) * up).astype(BF16)

    return call(body, [((slots, rows, half), BF16)], flops=1)(own, *got)[0]


def outputs(near_ref, far_ref, w_ref, me, s):
    half = near_ref.shape[2]
    made = dot(near_ref[s], w_ref[s, pl.ds(pl.multiple_of(me * half, 128), half), :])
    return made + dot(far_ref[s], w_ref[s, pl.ds(pl.multiple_of((1 - me) * half, 128), half), :])


def decode_experts(own, got, w_down, gates):
    slots, rows, wide = own.shape
    cols = w_down.shape[2]
    half = wide // 2

    def body(w_ref, own_ref, got_ref, gates_ref, out):
        total = jnp.zeros((rows, cols), F32)
        for s in range(slots):
            units = own_ref[s] + got_ref[s].astype(F32)
            gate, up = units[:, 0:half], units[:, half:]
            hidden = (gate / (1.0 + jnp.exp(-gate)) * up).astype(BF16)
            made = dot(hidden, w_ref[s]).astype(BF16).astype(F32)
            total = total + made * gates_ref[s * rows : (s + 1) * rows, 0:1]
        out[...] = total

    return call(body, [((rows, cols), F32)], flops=1)(w_down, own, got, gates)[0]


def down(near, far, w_down, which, picks, gates, me_kv, rows, skip, decode=None):
    slots, total_rows, _ = near.shape
    cols = w_down.shape[2]
    count = len(which)
    part = total_rows // count
    blocks = part // CAP

    def body(me, w_ref, near_ref, far_ref, picks_ref, gates_ref, *refs):
        outs = refs[-3:]
        made = [outputs(near_ref, far_ref, w_ref, me[0], s) for s in range(slots)]
        for n, g in enumerate(which):
            parts = jnp.concatenate(
                [made[s][n * part : (n + 1) * part] for s in range(slots)], axis=0
            )
            parts = (parts * gates_ref[g, :, 0:1]).astype(BF16)
            total = t_dot(picks_ref[g], parts)
            for b in range(blocks):
                out, low = outs[n + b * 2 // blocks if n else 0], b * rows
                low = low % out.shape[0]
                block = total[b * rows : (b + 1) * rows]
                out[low : low + rows, :] = block.astype(BF16)
                if decode is None:
                    continue
                late = (n * blocks + b) * skip
                late = jnp.concatenate([refs[0][late : late + skip, :], block[skip:16]], axis=0)
                out[low : low + 16, :] = late.astype(BF16)

    more = [] if decode is None else [decode]
    shapes = [((blocks * rows, cols), BF16)] + [((blocks // 2 * rows, cols), BF16)] * 2
    return call(body, shapes, smem=(0,), flops=1)(
        me_kv, w_down, near, far, picks, gates, *more
    )


def split_sum(kept, halves, rows, first=BF16):
    cols = kept.shape[1]
    high = halves[0].shape[0]
    count = kept.shape[0] // rows

    def body(kept_ref, *refs):
        for n in range(count):
            low = n * rows
            more = refs[low // high][low % high : low % high + rows, :]
            total = kept_ref[low : low + rows, :].astype(F32) + more.astype(F32)
            refs[2 + n][...] = total.astype(refs[2 + n].dtype)

    return call(
        body, [((rows, cols), first)] + [((rows, cols), BF16)] * (count - 1), flops=1
    )(kept, *halves)


def line_base(middle, decode_middle, own, parts, me_pg, skip):
    rows, cols = middle.shape

    def body(pg, mid, dec, *refs):
        out = refs[-1]
        total = refs[0][...]
        for ref in refs[1:-1]:
            total = total + ref[...].astype(F32)
        out[...] = total + mid[...]
        put = iota((8, dec.shape[0]), 1) == pg[0] * skip + iota((8, dec.shape[0]), 0)
        put = put & (iota((8, dec.shape[0]), 0) < skip)
        stream = dot(put.astype(F32), dec[...], HIGH)
        stream = jnp.where(iota((8, cols), 0) < skip, stream, mid[0:8, :])
        out[0:8, :] = total[0:8] + stream

    return call(body, [((rows, cols), F32)], smem=(0,))(
        me_pg, middle, decode_middle, own, *parts
    )[0]


def close(base, parts):
    rows, cols = base.shape

    def body(base_ref, *refs):
        mixed, squares = refs[-2:]
        total = base_ref[...]
        for ref in refs[:-2]:
            total = total + ref[...].astype(F32)
        mixed[...] = total
        total = total * total
        folded = total[:, 0:128]
        for n in range(1, cols // 128):
            folded = folded + total[:, n * 128 : (n + 1) * 128]
        squares[...] = folded

    return call(body, [((rows, cols), F32), ((rows, 128), F32)])(base, *parts)


def last_norm(mixed, near, far, gain):
    rows, cols = mixed.shape

    def body(mixed_ref, near_ref, far_ref, gain_ref, out):
        squares = jnp.sum(near_ref[...] + far_ref[...], axis=1, keepdims=True)
        out[...] = (
            mixed_ref[...] * lax.rsqrt(squares / (2 * cols) + EPSILON) * gain_ref[...]
        ).astype(BF16)

    return call(body, [((rows, cols), BF16)])(mixed, near, far, gain.reshape(1, -1))[0]


def line_pg(x, n_pg):
    return [x] + [swap_pg(x, 4 * z, n_pg) for z in range(1, n_pg // 4)]


def fast_local(
    residual_in,
    queries,
    prefill_attn,
    kv_cache,
    page_table,
    lengths,
    out_weight,
    norm_gain_in,
    norm_gain_out,
    expert_ids,
    route_weight,
    slot_table,
    w_gate_up,
    w_down,
):
    n_pg = lax.axis_size("pg")
    me = lax.axis_index("pg")
    me_kv = lax.axis_index("kv").reshape(1).astype(jnp.int32)
    me_pg = me.reshape(1).astype(jnp.int32)
    rows, cols = residual_in.shape
    own_req = queries.shape[0]
    slots = w_gate_up.shape[0]
    pages, _, page_len, wide = kv_cache.shape
    head_dim = wide // 2
    max_pages = page_table.shape[1]
    top = expert_ids.shape[1]
    zs = n_pg // 4
    first = 2 * own_req * cols // 128

    packed = pack(queries, residual_in, expert_ids, route_weight, n_pg)
    sent = lax.all_to_all(packed, "pg", split_axis=0, concat_axis=0, tiled=True)
    send, near, base = project_prefill(
        after(prefill_attn, packed), out_weight, residual_in, me_kv
    )

    mine = me * slots + jnp.arange(slots, dtype=jnp.int32)
    expert = jnp.arange(slot_table.shape[0], dtype=jnp.int32)
    experts = jnp.max(
        jnp.where(slot_table[:, :, None] == mine[None, None, :], expert[:, None, None], -1), axis=0
    )
    page_ids = me * pages + jnp.arange(pages, dtype=jnp.int32)
    flat_table = page_table.reshape(-1)
    entry_index = jnp.arange(flat_table.shape[0], dtype=jnp.int32)
    found = jnp.sum(
        jnp.where(flat_table[None, :] == page_ids[:, None], entry_index[None, :], 0), axis=1
    )
    owner = found // max_pages
    owner_len = jnp.sum(
        jnp.where(
            owner[:, None] == jnp.arange(lengths.shape[0], dtype=jnp.int32)[None, :],
            lengths[None, :],
            0,
        ),
        axis=1,
    )
    live = owner_len - found % max_pages * page_len
    partial = page_attention(sent, kv_cache, owner, live, own_req, cols)
    got, far = after([swap_kv(send), swap_kv(near)], partial)
    middle, payload = norm_and_pages(base, send, got, far, norm_gain_in, partial)
    line = [swap_pg(payload, 4 * z, n_pg) for z in range(1, zs)]
    picks, gates, dec_gates = plan(
        after(sent, payload), first, top, experts, me_pg, slots, rows, own_req, zs
    )
    w_units, w_rows = load(after([w_gate_up, w_down], picks))

    def swap_each(arrays, mask):
        return [swap_pg(x, mask, n_pg) for x in arrays]

    def swap_units(arrays):
        return [swap_kv(x) for x in arrays]

    def gathered(which, groups, parts, decode=None):
        return gather(groups, which, picks, w_units, me_kv, me_pg, rows, own_req, parts, decode)

    *near, near_pages = join([payload] + after(line, w_units), cols, pages)
    across_pages = swap_pg(near_pages, 2, n_pg)
    across = swap_each(near, 2)
    near_pages_core = swap_pg(near_pages, 1, n_pg)
    xs0, *out0 = gathered([0, 2], [near, swap_each(near, 1)], (slots,))
    got0 = swap_units(out0)
    own0 = own_products(xs0, w_units, me_kv)
    across_pages = after(across_pages, own0)
    pieces = [near_pages, across_pages, near_pages_core, swap_pg(across_pages, 1, n_pg)]
    dec_send, dec_near, dec_base = project_decode(
        pieces, page_table, pages, sent, out_weight, me_kv, me_pg, own_req, head_dim
    )
    dec_got, dec_far = swap_kv(dec_send), swap_kv(dec_near)
    near0 = activate(own0, after(got0, dec_send))
    far0 = swap_kv(near0)
    across = after(across, near0)
    across_core = swap_each(across, 1)
    dec_got, dec_far = after([dec_got, dec_far], across)
    dec_middle, dec_normed = first_norm(dec_base, dec_send, dec_got, dec_far, norm_gain_in)
    dec_own, dec_units = pick_decode(dec_normed, w_units, me_pg, own_req, zs)
    dec_got = swap_kv(dec_units)
    xs1, *out1 = gathered([1, 3], after([across, across_core], [dec_units, far0]), (slots - 1, 1), dec_normed)
    got1 = swap_units(out1)
    own1 = own_products(xs1, w_units, me_kv)
    decode = decode_experts(dec_own, after(dec_got, out1), w_rows, dec_gates)
    keep0, *give0 = down(
        near0, after(far0, decode), w_rows, [0, 2], picks, gates, me_kv, rows, own_req, decode
    )
    parts0 = split_sum(keep0, swap_each(give0, 1), rows, F32)
    lines0 = [swap_pg(parts0[z], 4 * z, n_pg) for z in range(1, zs)]
    near1 = activate(own1, after(got1, parts0))
    far1 = swap_kv(near1)
    base = line_base(middle, dec_middle, parts0[0], after(lines0, near1), me_pg, own_req)
    keep1, *give1 = down(
        near1, after(far1, base), w_rows, [1, 3], picks, gates, me_kv, rows, own_req
    )
    parts1 = split_sum(keep1, swap_each(give1, 1), rows)
    mixed, squares = close(base, [swap_pg(parts1[z], 4 * z + 2, n_pg) for z in range(zs)])
    return last_norm(mixed, squares, swap_kv(squares), norm_gain_out)


def solution(mesh):
    fast = mesh.shape["kv"] == 2 and mesh.shape["pg"] == 16
    local = fast_local if fast else general_local
    in_specs = (
        P("pg", "kv"),
        P("pg", "kv"),
        P("pg", "kv"),
        P("pg", "kv", None, None),
        P(),
        P(),
        P("kv", None),
        P("kv"),
        P("kv"),
        P("pg", None),
        P("pg", None),
        P(),
        P("pg", "kv", None),
        P("pg", None, "kv"),
    )
    out_specs = P("pg", "kv")
    return jax.shard_map(local, mesh=mesh, in_specs=in_specs, out_specs=out_specs, check_vma=False)
```

```python
import functools

import jax
import jax.numpy as jnp
from jax import lax
from jax.experimental import pallas as pl
from jax.experimental.pallas import tpu as pltpu
from jax.sharding import PartitionSpec as P

NEG_FILL = -1e30
EPSILON = 1e-06


def merged_2(array, axis, join):
    gathered = jax.tree.map(
        lambda a, kind: lax.all_gather(a.astype(kind), axis),
        array,
        (jnp.bfloat16, jnp.bfloat16, jnp.bfloat16),
    )

    def take(source):
        return jax.tree.map(
            lambda a, own: lax.dynamic_index_in_dim(a, source, 0, False).astype(own.dtype),
            gathered,
            array,
        )

    return lax.fori_loop(
        1, lax.axis_size(axis), lambda source, state: join(state, take(source)), take(0)
    )


def merge_pair(first, secondary_slot):
    highest = jnp.maximum(first[0], secondary_slot[0])
    scale_a = jnp.exp(first[0] - highest)
    scale_b = jnp.exp(secondary_slot[0] - highest)
    head_count = first[0].shape[1]
    acc_a = first[2].reshape(first[2].shape[0], head_count, -1) * scale_a[:, :, None]
    acc_b = (
        secondary_slot[2].reshape(secondary_slot[2].shape[0], head_count, -1) * scale_b[:, :, None]
    )
    return (
        highest,
        first[1] * scale_a + secondary_slot[1] * scale_b,
        (acc_a + acc_b).reshape(first[2].shape),
    )


def general_local(
    residual_in,
    queries,
    prefill_attn,
    kv_cache,
    page_table,
    lengths,
    out_weight,
    norm_gain_in,
    norm_gain_out,
    expert_ids,
    route_weight,
    slot_table,
    w_gate_up,
    w_down,
):
    head_dim = kv_cache.shape[3] // 2
    page_len = kv_cache.shape[2]
    pages_here = kv_cache.shape[0]
    kv_here = kv_cache.shape[1]
    own_req = queries.shape[0]
    heads_here = queries.shape[1] // head_dim
    head_group = heads_here // kv_here
    total_req = page_table.shape[0]
    max_pages = page_table.shape[1]
    full_gate_up, full_down = (
        lax.all_gather(w_gate_up, "kv", axis=1, tiled=True),
        lax.all_gather(w_down, "kv", axis=2, tiled=True),
    )
    gathered = lax.all_gather(queries, "pg", axis=0, tiled=True)
    page_ids = lax.axis_index("pg") * pages_here + jnp.arange(pages_here, dtype=jnp.int32)
    flat_table = page_table.reshape(-1)
    entry_index = jnp.arange(flat_table.shape[0], dtype=jnp.int32)
    found = jnp.sum(
        jnp.where(flat_table[None, :] == page_ids[:, None], entry_index[None, :], 0), axis=1
    )
    owner = found // max_pages
    page_slot = found % max_pages
    owner_len = lengths[owner]
    query_pages = gathered[owner].reshape(pages_here, kv_here, head_group, head_dim)
    keys = kv_cache[:, :, :, :head_dim]
    values = kv_cache[:, :, :, head_dim:]
    scores = jnp.einsum(
        "pkgd,pktd->pkgt", query_pages, keys, preferred_element_type=jnp.float32
    ) * head_dim ** (-0.5)
    positions = page_slot[:, None] * page_len + jnp.arange(page_len, dtype=jnp.int32)[None, :]
    live = (positions < owner_len[:, None])[:, None, None, :]
    masked = jnp.where(live, scores, NEG_FILL)
    page_top = jnp.max(masked, axis=3)
    probs = jnp.where(live, jnp.exp(masked - page_top[..., None]), 0.0).astype(jnp.bfloat16)
    page_sum = jnp.sum(probs.astype(jnp.float32), axis=3).reshape(pages_here, heads_here)
    page_acc = jnp.einsum(
        "pkgt,pktd->pkgd", probs, values, preferred_element_type=jnp.float32
    ).reshape(pages_here, heads_here, head_dim)
    page_top = page_top.reshape(pages_here, heads_here)
    page_live = page_slot * page_len < owner_len
    member = (owner[:, None] == jnp.arange(total_req, dtype=jnp.int32)[None, :]) & page_live[
        :, None
    ]
    local_max = jnp.max(jnp.where(member[:, :, None], page_top[:, None, :], NEG_FILL), axis=0)
    member_t = member.astype(jnp.float32).T
    weight = jnp.exp(page_top - local_max[owner])
    sums = jnp.dot(member_t, weight * page_sum, precision=lax.Precision.HIGHEST)
    accs = jnp.dot(
        member_t,
        (weight[:, :, None] * page_acc).reshape(pages_here, -1),
        precision=lax.Precision.HIGHEST,
    )
    sums, accs = (sums, accs)
    merged = merged_2((local_max, sums, accs), "pg", merge_pair)
    start = lax.axis_index("pg") * own_req
    own_sum = lax.dynamic_slice_in_dim(merged[1], start, own_req, 0)
    own_acc = lax.dynamic_slice_in_dim(merged[2], start, own_req, 0)
    attn_dec = (own_acc.reshape(own_req, heads_here, head_dim) / own_sum[:, :, None]).reshape(
        own_req, -1
    )
    attn_dec = attn_dec.astype(jnp.bfloat16)
    attn_rows = jnp.concatenate([attn_dec, prefill_attn], axis=0)
    projected = jnp.dot(attn_rows, out_weight, preferred_element_type=jnp.float32)
    mixed_in = lax.psum_scatter(
        projected.astype(jnp.bfloat16), "kv", scatter_dimension=1, tiled=True
    ).astype(jnp.float32)
    middle = residual_in.astype(jnp.float32) + mixed_in
    full_width = residual_in.shape[1] * lax.axis_size("kv")
    in_squares = lax.psum(jnp.sum(middle * middle, axis=1), "kv")
    normed = (middle * lax.rsqrt(in_squares / full_width + EPSILON)[:, None] * norm_gain_in).astype(
        jnp.bfloat16
    )
    token_rows, top = expert_ids.shape
    copies = slot_table.shape[1]
    experts_total = slot_table.shape[0]
    kv_count = lax.axis_size("kv")
    capacity = kv_count * max(
        1,
        (token_rows * top * 5 + 4 * experts_total * kv_count - 1) // (4 * experts_total * kv_count),
    )
    slots_here = w_gate_up.shape[0]
    groups = lax.axis_size("pg")
    all_slots = slots_here * groups
    feature_cols = normed.shape[1]
    row_ids = lax.axis_index("pg") * token_rows + jnp.arange(token_rows, dtype=jnp.int32)
    parity = (row_ids[:, None] + jnp.arange(top, dtype=jnp.int32)[None, :]) % copies
    route_key = (expert_ids * copies + parity).reshape(-1)
    table_flat = slot_table.reshape(-1)
    table_index = jnp.arange(table_flat.shape[0], dtype=jnp.int32)
    target_slot = jnp.sum(
        jnp.where(route_key[:, None] == table_index[None, :], table_flat[None, :], 0), axis=1
    )
    match_count = (target_slot[:, None] == jnp.arange(all_slots, dtype=jnp.int32)[None, :]).astype(
        jnp.int32
    )
    rank = jnp.sum((jnp.cumsum(match_count, axis=0) - match_count) * match_count, axis=1)
    dest = target_slot * capacity + rank
    source_row = jnp.arange(token_rows * top, dtype=jnp.int32) // top
    outgoing = (
        jnp.zeros((all_slots * capacity, feature_cols), jnp.bfloat16)
        .at[dest]
        .set(normed[source_row])
    )
    outgoing = outgoing.reshape(groups, slots_here, capacity, feature_cols)
    arrived = lax.all_to_all(outgoing, "pg", split_axis=0, concat_axis=0, tiled=True)
    widened = lax.all_to_all(arrived, "kv", split_axis=2, concat_axis=3, tiled=True)
    gate_up = jnp.einsum(
        "pscd,sdf->pscf", widened, full_gate_up, preferred_element_type=jnp.float32
    )
    half = gate_up.shape[3] // 2
    hidden = (jax.nn.silu(gate_up[..., :half]) * gate_up[..., half:]).astype(jnp.bfloat16)
    produced = jnp.einsum(
        "pscf,sfd->pscd", hidden, full_down, preferred_element_type=jnp.float32
    ).astype(jnp.bfloat16)
    narrowed = lax.all_to_all(produced, "kv", split_axis=3, concat_axis=2, tiled=True)
    returned = lax.all_to_all(narrowed, "pg", split_axis=0, concat_axis=0, tiled=True)
    returned = returned.reshape(all_slots * capacity, feature_cols)
    picked = returned[dest].astype(jnp.float32).reshape(token_rows, top, feature_cols)
    mixed = middle + jnp.sum(picked * route_weight[:, :, None], axis=1)
    out_squares = lax.psum(jnp.sum(mixed * mixed, axis=1), "kv")
    return (mixed * lax.rsqrt(out_squares / full_width + EPSILON)[:, None] * norm_gain_out).astype(
        jnp.bfloat16
    )


F32 = jnp.float32
BF16 = jnp.bfloat16
CAP = 16
HIGH = lax.Precision.HIGHEST


def call(body, outs, scratch=(), smem=(), hbm=(), vmem=16, flops=10**9):
    def run(*operands):
        kinds = [
            pltpu.SMEM if n in smem else pltpu.HBM if n in hbm else pltpu.VMEM
            for n in range(len(operands))
        ]
        return pl.pallas_call(
            body,
            out_shape=[jax.ShapeDtypeStruct(s, d) for s, d in outs],
            in_specs=[pl.BlockSpec(memory_space=kind) for kind in kinds],
            out_specs=[pl.BlockSpec(memory_space=pltpu.VMEM) for _ in outs],
            scratch_shapes=list(scratch),
            compiler_params=pltpu.CompilerParams(
                vmem_limit_bytes=vmem * 2**20
            ),
            cost_estimate=pl.CostEstimate(flops=flops, bytes_accessed=1, transcendentals=0),
        )(*operands)

    return run


def after(values, *earlier):
    return lax.optimization_barrier((values, earlier))[0]


def iota(shape, dim):
    return lax.broadcasted_iota(jnp.int32, shape, dim)


def dot(a, b, precision=None):
    return jnp.dot(a, b, preferred_element_type=F32, precision=precision)


def dot_t(a, b):
    return lax.dot_general(a, b, (((1,), (1,)), ((), ())), preferred_element_type=F32)


def t_dot(a, b):
    return lax.dot_general(a, b, (((0,), (0,)), ((), ())), preferred_element_type=F32)


def swap_kv(x):
    return lax.ppermute(x, "kv", [(0, 1), (1, 0)])


def swap_pg(x, mask, n):
    return lax.ppermute(x, "pg", [(i, i ^ mask) for i in range(n)])


def pack(queries, residual, expert_ids, route_weight, n_pg):
    own_req, cols = queries.shape
    rows, top = expert_ids.shape
    tiles = cols // 128
    high = 2 * own_req * tiles
    total = high + top

    def body(q_hbm, res_hbm, ids_hbm, gates_hbm, out_ref, scr, q_ref, res_ref, ids, gates, sems):
        copies = [
            pltpu.make_async_copy(q_hbm, q_ref, sems.at[0]),
            pltpu.make_async_copy(res_hbm.at[0:16, :], res_ref, sems.at[1]),
            pltpu.make_async_copy(ids_hbm, ids, sems.at[2]),
            pltpu.make_async_copy(gates_hbm, gates, sems.at[3]),
        ]
        for copy in copies:
            copy.start()
        for copy in copies:
            copy.wait()
        for n, ref in enumerate((q_ref, res_ref)):
            for i in range(tiles):
                low = (n * tiles + i) * own_req
                scr[low : low + own_req, :] = ref[0:own_req, 128 * i : 128 * (i + 1)].astype(F32)
        scr[high:, 0:rows] = ids[...].astype(F32)
        scr[high:, 64 : 64 + rows] = gates[...]
        packed = scr[...].astype(BF16)
        for g in range(n_pg):
            out_ref[g] = packed

    return call(
        body,
        [((n_pg, total, 128), BF16)],
        [
            pltpu.VMEM((total, 128), F32),
            pltpu.VMEM((own_req, cols), BF16),
            pltpu.VMEM((16, cols), BF16),
            pltpu.VMEM((top, rows), expert_ids.dtype),
            pltpu.VMEM((top, rows), F32),
            pltpu.SemaphoreType.DMA((4,)),
        ],
        hbm=(0, 1, 2, 3),
        vmem=62,
    )(queries, residual, expert_ids.T, route_weight.T)[0]


def unpack(sent_ref, out, which, own_req):
    tiles = out.shape[1] // 128
    for g in range(sent_ref.shape[0]):
        for i in range(tiles):
            low = (which * tiles + i) * own_req
            out[g * own_req : (g + 1) * own_req, 128 * i : 128 * (i + 1)] = sent_ref[
                g, low : low + own_req, :
            ].astype(F32)


def routing(sent_ref, me, masks, first, top, count):
    got = [sent_ref[me ^ mask, first : first + top, :].astype(F32) for mask in masks]
    ids = jnp.concatenate([x[:, 0:count] for x in got], axis=1)
    gates = jnp.concatenate([x[:, 64 : 64 + count] for x in got], axis=1)
    return jnp.concatenate([ids, gates], axis=0)


def group_masks(g, zs):
    return [4 * z + 2 * (g % 2) + g // 2 for z in range(zs)]


def page_attention(sent, kv_cache, owner, live, own_req, cols):
    groups = sent.shape[0]
    pages, kv_here, page_len, wide = kv_cache.shape
    head_dim = wide // 2
    heads = cols // head_dim
    group = heads // kv_here
    rows = 16
    requests = groups * own_req
    keys = kv_here * page_len
    total = pages * rows

    def body(owner_col, live_col, sent_ref, kv_ref, out_ref, q_all, scores, probs, acc):
        unpack(sent_ref, q_all, 0, own_req)
        pick = (owner_col[...] == iota((total, requests), 1)).astype(BF16)
        wide_q = dot(pick, q_all[...].astype(BF16))
        spread = iota((total, cols), 0) % rows == iota((total, cols), 1) // head_dim
        fold = (iota((cols, wide), 0) % head_dim == iota((cols, wide), 1)).astype(BF16)
        q = dot(jnp.where(spread, wide_q, 0.0).astype(BF16), fold).astype(BF16)
        for p in range(pages):
            part = slice(p * rows, (p + 1) * rows)
            scores[part, :] = dot_t(q[part], kv_ref[p].reshape(keys, wide)) * head_dim ** (-0.5)
        col = iota((total, keys), 1)
        ok = (col // page_len == iota((total, keys), 0) % rows // group) & (
            col % page_len < live_col[...]
        )
        masked = jnp.where(ok, scores[...], NEG_FILL)
        top = jnp.max(masked, axis=1, keepdims=True).astype(BF16).astype(F32)
        share = jnp.where(ok, jnp.exp(masked - top), 0.0).astype(BF16)
        probs[...] = share
        whole = jnp.sum(share.astype(F32), axis=1, keepdims=True)
        for p in range(pages):
            part = slice(p * rows, (p + 1) * rows)
            acc[part, :] = dot(probs[part, :], kv_ref[p].reshape(keys, wide))
        unfold = (iota((wide, cols), 0) - head_dim == iota((wide, cols), 1) % head_dim).astype(BF16)
        here = iota((total, 128), 0) % rows == iota((total, 128), 1)
        merge = (iota((pages, total), 0) == iota((pages, total), 1) // rows).astype(BF16)
        flat = jnp.where(spread, dot(acc[...].astype(BF16), unfold), 0.0).astype(BF16)
        out_ref[:, 0:cols] = dot(merge, flat).astype(BF16)
        flat = jnp.where(here, top, 0.0).astype(BF16)
        out_ref[:, cols : cols + 128] = dot(merge, flat).astype(BF16)
        flat = jnp.where(here, whole, 0.0).astype(BF16)
        out_ref[:, cols + 128 :] = dot(merge, flat).astype(BF16)

    return call(
        body,
        [((pages, cols + 256), BF16)],
        [
            pltpu.VMEM((requests, cols), F32),
            pltpu.VMEM((total, keys), F32),
            pltpu.VMEM((total, keys), BF16),
            pltpu.VMEM((total, wide), F32),
        ],
    )(jnp.repeat(owner, rows)[:, None], jnp.repeat(live, rows)[:, None], sent, kv_cache)[0]


def half_products(left, w_ref, res, me, cols, far, near, base):
    mine = pl.multiple_of(me[0] * cols, 128)
    other = pl.multiple_of((1 - me[0]) * cols, 128)
    far[...] = dot(left, w_ref[:, pl.ds(other, cols)]).astype(BF16)
    own = dot(left, w_ref[:, pl.ds(mine, cols)]).astype(BF16).astype(F32) + res
    base[...] = own
    near[...] = own.astype(BF16)


def project_prefill(prefill, weight, residual, me_kv):
    rows, cols = residual.shape
    skip = rows - prefill.shape[0]

    def body(me, pre, w_ref, res, far, near, base, rows_scr):
        rows_scr[0:skip, :] = jnp.zeros((skip, cols), F32)
        rows_scr[skip:, :] = pre[...].astype(F32)
        left = rows_scr[...].astype(BF16)
        half_products(left, w_ref, res[...].astype(F32), me, cols, far, near, base)

    return call(
        body,
        [((rows, cols), BF16)] * 2 + [((rows, cols), F32)],
        [pltpu.VMEM((rows, cols), F32)],
        smem=(0,),
    )(me_kv, prefill, weight, residual)


def project_decode(pieces, page_table, pages, sent, weight, me_kv, me_pg, own_req, head_dim):
    groups = sent.shape[0]
    cols = weight.shape[0]
    requests = groups * own_req
    entries = page_table.size
    count = len(pieces)
    high = pieces[0].shape[0]
    total = count * high

    def body(me, pg, table_ref, w_ref, sent_ref, *refs):
        far, near, base, res = refs[count:]
        unpack(sent_ref, res, 1, own_req)
        table = jnp.concatenate([ref[...] for ref in refs[:count]], axis=0)
        page = jnp.concatenate(
            [table_ref[j : j + 1, :] for j in range(entries // requests)], axis=1
        )
        away = (page // pages) ^ pg[0]
        where = ((away % 2) * 2 + away // 2 % 2) * high + away // 4 * pages + page % pages
        pick = (iota((total, entries), 0) == where).astype(BF16)
        got = t_dot(pick, table)
        parts = [got[n : n + requests] for n in range(0, entries, requests)]
        sums = [part[:, cols + 128 :] for part in parts]
        tops = [
            jnp.where(tot > 0.0, part[:, cols : cols + 128], NEG_FILL)
            for part, tot in zip(parts, sums)
        ]
        best = functools.reduce(jnp.maximum, tops)
        scales = [jnp.where(tot > 0.0, jnp.exp(top - best), 0.0) for top, tot in zip(tops, sums)]
        whole = functools.reduce(jnp.add, [scale * tot for scale, tot in zip(scales, sums)])
        whole = jnp.where(whole > 0.0, whole, 1.0)
        expand = (iota((128, cols), 0) == iota((128, cols), 1) // head_dim).astype(BF16)
        share = jnp.concatenate([scale / whole for scale in scales], axis=0)
        share_high = share.astype(BF16)
        share_low = (share - share_high.astype(F32)).astype(BF16)
        wide = dot(share_high, expand) + dot(share_low, expand)
        merged = jnp.zeros((requests, cols), F32)
        for n, part in enumerate(parts):
            merged += wide[n * requests : (n + 1) * requests] * part[:, 0:cols]
        half_products(merged.astype(BF16), w_ref, res[...], me, cols, far, near, base)

    return call(
        body,
        [((requests, cols), BF16)] * 2 + [((requests, cols), F32)],
        [pltpu.VMEM((requests, cols), F32)],
        smem=(0, 1),
    )(me_kv, me_pg, page_table.T, weight, sent, *pieces)


def norm_and_pages(base, sent, got_own, got_far, gain, pages):
    rows, cols = base.shape
    count, wide = pages.shape
    lanes = wide * count // rows

    def body(base_ref, sent_ref, got_ref, far_ref, gain_ref, pages_ref, middle, out):
        mid = base_ref[...] + got_ref[...].astype(F32)
        far = far_ref[...].astype(F32) + sent_ref[...].astype(F32)
        squares = jnp.sum(mid * mid + far * far, axis=1, keepdims=True)
        middle[...] = mid
        out[:, 0:cols] = (
            mid * lax.rsqrt(squares / (2 * cols) + EPSILON) * gain_ref[...]
        ).astype(BF16)
        for n in range(rows // count):
            out[n * count : (n + 1) * count, cols:] = pages_ref[:, n * lanes : (n + 1) * lanes]

    return call(body, [((rows, cols), F32), ((rows, cols + lanes), BF16)])(
        base, sent, got_own, got_far, gain.reshape(1, -1), pages
    )


def join(parts, cols, pages):
    rows, wide = parts[0].shape
    lanes = wide - cols
    count = len(parts)
    quarters = rows // pages

    def body(*refs):
        outs, out_pages = refs[-3:-1], refs[-1]
        for n in range(count):
            low = n % (count // 2) * rows
            outs[n // (count // 2)][low : low + rows, :] = refs[n][:, 0:cols]
            for k in range(quarters):
                out_pages[n * pages : (n + 1) * pages, k * lanes : (k + 1) * lanes] = refs[n][
                    k * pages : (k + 1) * pages, cols:
                ]

    return call(
        body,
        [((count // 2 * rows, cols), BF16)] * 2 + [((count * pages, quarters * lanes), BF16)],
    )(*parts)


def first_norm(base, sent, got_own, got_far, gain):
    rows, cols = base.shape

    def body(base_ref, sent_ref, got_ref, far_ref, gain_ref, middle, normed):
        mid = base_ref[...] + got_ref[...].astype(F32)
        far = far_ref[...].astype(F32) + sent_ref[...].astype(F32)
        squares = jnp.sum(mid * mid + far * far, axis=1, keepdims=True)
        middle[...] = mid
        normed[...] = (
            mid * lax.rsqrt(squares / (2 * cols) + EPSILON) * gain_ref[...]
        ).astype(BF16)

    return call(body, [((rows, cols), F32), ((rows, cols), BF16)])(
        base, sent, got_own, got_far, gain.reshape(1, -1)
    )


def routes(info, experts, slots, block_rows, skip):
    top = info.shape[0] // 2
    tokens = info.shape[1]
    token = iota((top, tokens), 1) % block_rows
    odd = (token + iota((top, tokens), 0)) % 2 == 1
    hits, gates = [], []
    for s in range(slots):
        wanted = jnp.where(odd, experts[1, s], experts[0, s]).astype(F32)
        hit = (info[0:top] == wanted) & (token >= skip)
        hits.append(jnp.sum(hit.astype(F32), axis=0, keepdims=True))
        gates.append(jnp.sum(jnp.where(hit, info[top:], 0.0), axis=0, keepdims=True))
    fill = [jnp.zeros((8 - slots, tokens), F32)] if slots < 8 else []
    stacked = jnp.concatenate(hits + fill, axis=0)
    row, col = iota((tokens, tokens), 0), iota((tokens, tokens), 1)
    before = ((row < col) & (row // block_rows == col // block_rows)).astype(BF16)
    ranks = dot(stacked.astype(BF16), before).astype(jnp.int32)
    places = [jnp.where(hits[s] > 0.0, ranks[s : s + 1], -1) for s in range(slots)]
    return places, gates


def one_hot(place, block_rows):
    tokens = place.shape[1]
    shape = (tokens // block_rows * CAP, tokens)
    row = iota(shape, 0)
    return (place == row % CAP) & (iota(shape, 1) // block_rows == row // CAP)


def plan(sent, first, top, experts, me_pg, slots, rows, skip, zs):
    part = zs * CAP
    tokens = zs * rows

    def body(pg, es, sent_ref, picks, gates, dec_gates):
        for g in range(4):
            info = routing(sent_ref, pg[0], group_masks(g, zs), first, top, rows)
            places, shares = routes(info, es, slots, rows, 0 if g % 2 else skip)
            for s in range(slots):
                hot = one_hot(places[s], rows)
                low = s * part
                picks[g, low : low + part, :] = hot.astype(BF16)
                gates[g, low : low + part, :] = jnp.broadcast_to(
                    jnp.sum(jnp.where(hot, shares[s], 0.0), axis=1, keepdims=True), (part, 128)
                )
        masks = group_masks(0, zs) + group_masks(2, zs)
        count = len(masks) * skip
        info = routing(sent_ref, pg[0], masks, first, top, skip)
        ids, shares = info[0:top], info[top:]
        odd = (iota((top, count), 1) % skip + iota((top, count), 0)) % 2 == 1
        eye = iota((count, count), 0) == iota((count, count), 1)
        for s in range(slots):
            wanted = jnp.where(odd, es[1, s], es[0, s]).astype(F32)
            share = jnp.sum(jnp.where(ids == wanted, shares, 0.0), axis=0, keepdims=True)
            dec_gates[s * count : (s + 1) * count, :] = jnp.broadcast_to(
                jnp.sum(jnp.where(eye, share, 0.0), axis=1, keepdims=True), (count, 128)
            )

    return call(
        body,
        [
            ((4, slots * part, tokens), BF16),
            ((4, slots * part, 128), F32),
            ((slots * 2 * zs * skip, 128), F32),
        ],
        smem=(0, 1),
    )(me_pg, experts, sent)


def load(arrays):
    count = len(arrays)

    def body(*refs):
        sems = refs[-1]
        copies = [
            pltpu.make_async_copy(refs[n].at[s], refs[count + n].at[s], sems.at[n, s])
            for n in range(count)
            for s in range(arrays[n].shape[0])
        ]
        for copy in copies:
            copy.start()
        for copy in copies:
            copy.wait()

    return call(
        body,
        [(x.shape, x.dtype) for x in arrays],
        [pltpu.SemaphoreType.DMA((count, arrays[0].shape[0]))],
        hbm=tuple(range(count)),
        vmem=44,
    )(*arrays)


def products(xs, w_ref, side, *outs):
    half = outs[0].shape[2] // 2
    places = [(out, n) for out in outs for n in range(out.shape[0])]
    for s, (out, n) in enumerate(places):
        x = xs[s] if len(xs.shape) == 3 else xs[...]
        for k in range(2):
            low = pl.multiple_of(k * 2 * half + side * half, 128)
            out[n, :, k * half : (k + 1) * half] = dot(x, w_ref[s, :, pl.ds(low, half)]).astype(
                out.dtype
            )


def gather(groups, which, picks, w, me_kv, me_pg, rows, skip, parts, decode=None):
    count, slots = len(groups), w.shape[0]
    pieces = len(groups[0])
    cols = w.shape[1]
    tokens = pieces * groups[0][0].shape[0]
    zs = tokens // rows
    part = zs * CAP
    ff = w.shape[2] // 2

    def body(me, pg, w_ref, picks_ref, *refs):
        xs, sends = refs[-1 - len(parts)], refs[-len(parts) :]
        for n, g in enumerate(which):
            x = jnp.concatenate(
                [ref[...] for ref in refs[n * pieces : (n + 1) * pieces]], axis=0
            )
            if decode is not None:
                dec = refs[count * pieces][...]
                shape = (tokens, dec.shape[0])
                row = iota(shape, 0)
                source = jnp.zeros(shape, jnp.int32)
                for z, mask in enumerate(group_masks(g, zs)):
                    source = jnp.where(row // rows == z, (pg[0] ^ mask) * skip, source)
                late = row % rows < skip
                put = late & (iota(shape, 1) == source + row % rows)
                x = jnp.where(
                    iota((tokens, cols), 0) % rows < skip,
                    dot(put.astype(BF16), dec),
                    x.astype(F32),
                ).astype(BF16)
            got = dot(picks_ref[g], x).astype(BF16)
            for s in range(slots):
                xs[s, n * part : (n + 1) * part, :] = got[s * part : (s + 1) * part]
        products(xs, w_ref, 1 - me[0], *sends)

    more = [] if decode is None else [decode]
    high = count * part
    return call(
        body,
        [((slots, high, cols), BF16)] + [((n, high, ff), BF16) for n in parts],
        smem=(0, 1),
    )(me_kv, me_pg, w, picks, *[x for group in groups for x in group], *more)


def pick_decode(normed, w, me_pg, skip, zs):
    slots, _, wide = w.shape
    total, cols = normed.shape
    masks = group_masks(0, zs) + group_masks(2, zs)
    rows = len(masks) * skip

    def body(pg, w_ref, x_ref, own, send):
        row = iota((rows, total), 0)
        source = jnp.zeros((rows, total), jnp.int32)
        for n, mask in enumerate(masks):
            source = jnp.where(row // skip == n, (pg[0] ^ mask) * skip, source)
        put = iota((rows, total), 1) == source + row % skip
        x = dot(put.astype(BF16), x_ref[...]).astype(BF16)
        for s in range(slots):
            made = dot(x, w_ref[s])
            own[s] = made
            send[s] = made.astype(BF16)

    return call(body, [((slots, rows, wide), F32), ((slots, rows, wide), BF16)], smem=(0,))(
        me_pg, w, normed
    )


def own_products(xs, w, me_kv, flops=1):
    def body(me, w_ref, x_ref, out):
        products(x_ref, w_ref, me[0], out)

    return call(body, [((w.shape[0], xs.shape[-2], w.shape[2] // 2), F32)], smem=(0,), flops=flops)(
        me_kv, w, xs
    )[0]


def activate(own, got, parts=1):
    slots, rows, ff = own.shape
    half = ff // 2
    high = rows // parts

    def body(own_ref, *refs):
        places = [(ref, n) for ref in refs[:-parts] for n in range(ref.shape[0])]
        for s, (ref, n) in enumerate(places):
            gate = own_ref[s, :, 0:half] + ref[n, :, 0:half].astype(F32)
            up = own_ref[s, :, half:] + ref[n, :, half:].astype(F32)
            hidden = (gate / (1.0 + jnp.exp(-gate)) * up).astype(BF16)
            for k in range(parts):
                refs[k - parts][s] = hidden[k * high : (k + 1) * high]

    return call(body, [((slots, high, half), BF16)] * parts, flops=1)(own, *got)


def outputs(near, far, w_ref, me, s):
    half = near[0].shape[2]
    made = dot(
        jnp.concatenate([ref[s] for ref in near], axis=0),
        w_ref[s, pl.ds(pl.multiple_of(me * half, 128), half), :],
    )
    return made + dot(
        jnp.concatenate([ref[s] for ref in far], axis=0),
        w_ref[s, pl.ds(pl.multiple_of((1 - me) * half, 128), half), :],
    )


def decode_experts(own, got, w_down, gates):
    slots, rows, wide = own.shape
    cols = w_down.shape[2]
    half = wide // 2

    def body(w_ref, own_ref, got_ref, gates_ref, out):
        total = jnp.zeros((rows, cols), F32)
        for s in range(slots):
            units = own_ref[s] + got_ref[s].astype(F32)
            gate, up = units[:, 0:half], units[:, half:]
            hidden = (gate / (1.0 + jnp.exp(-gate)) * up).astype(BF16)
            made = dot(hidden, w_ref[s]).astype(BF16).astype(F32)
            total = total + made * gates_ref[s * rows : (s + 1) * rows, 0:1]
        out[...] = total

    return call(body, [((rows, cols), F32)], flops=1)(w_down, own, got, gates)[0]


def down(near, far, w_down, which, picks, gates, me_kv, rows, skip, decode=None):
    pieces = len(near)
    slots, total_rows, _ = near[0].shape
    total_rows = total_rows * pieces
    cols = w_down.shape[2]
    count = len(which)
    part = total_rows // count
    blocks = part // CAP

    def body(me, w_ref, picks_ref, gates_ref, *refs):
        near_refs, far_refs = refs[:pieces], refs[pieces : 2 * pieces]
        outs = refs[-3:]
        made = [outputs(near_refs, far_refs, w_ref, me[0], s) for s in range(slots)]
        for n, g in enumerate(which):
            parts = jnp.concatenate(
                [made[s][n * part : (n + 1) * part] for s in range(slots)], axis=0
            )
            parts = (parts * gates_ref[g, :, 0:1]).astype(BF16)
            total = t_dot(picks_ref[g], parts)
            for b in range(blocks):
                out, low = outs[n + b * 2 // blocks if n else 0], b * rows
                low = low % out.shape[0]
                block = total[b * rows : (b + 1) * rows]
                out[low : low + rows, :] = block.astype(BF16)
                if decode is None:
                    continue
                late = (n * blocks + b) * skip
                late = jnp.concatenate([refs[2 * pieces][late : late + skip, :], block[skip:16]], axis=0)
                out[low : low + 16, :] = late.astype(BF16)

    more = [] if decode is None else [decode]
    shapes = [((blocks * rows, cols), BF16)] + [((blocks // 2 * rows, cols), BF16)] * 2
    return call(body, shapes, smem=(0,), flops=1)(
        me_kv, w_down, picks, gates, *near, *far, *more
    )


def split_sum(kept, halves, rows, first=BF16, pad=0):
    cols = kept.shape[1]
    high = halves[0].shape[0]
    count = kept.shape[0] // rows

    def body(kept_ref, *refs):
        for n in range(count):
            low = n * rows
            more = refs[low // high][low % high : low % high + rows, :]
            total = kept_ref[low : low + rows, :].astype(F32) + more.astype(F32)
            out = refs[2 + n]
            out[0:rows, :] = total.astype(out.dtype)
            if n and pad:
                out[rows:, :] = jnp.zeros((pad, cols), out.dtype)

    return call(
        body, [((rows, cols), first)] + [((rows + pad, cols), BF16)] * (count - 1), flops=1
    )(kept, *halves)


def line_base(middle, decode_middle, own, parts, me_pg, skip):
    rows, cols = middle.shape

    def body(pg, mid, dec, *refs):
        out = refs[-1]
        total = refs[0][...]
        for ref in refs[1:-1]:
            total = total + ref[0:rows, :].astype(F32)
        out[...] = total + mid[...]
        put = iota((8, dec.shape[0]), 1) == pg[0] * skip + iota((8, dec.shape[0]), 0)
        put = put & (iota((8, dec.shape[0]), 0) < skip)
        stream = dot(put.astype(F32), dec[...], HIGH)
        stream = jnp.where(iota((8, cols), 0) < skip, stream, mid[0:8, :])
        out[0:8, :] = total[0:8] + stream

    return call(body, [((rows, cols), F32)], smem=(0,))(
        me_pg, middle, decode_middle, own, *parts
    )[0]


def close(base, parts):
    rows, cols = base.shape

    def body(base_ref, *refs):
        mixed, squares = refs[-2:]
        total = base_ref[...]
        for ref in refs[:-2]:
            total = total + ref[...].astype(F32)
        mixed[...] = total
        total = total * total
        folded = total[:, 0:128]
        for n in range(1, cols // 128):
            folded = folded + total[:, n * 128 : (n + 1) * 128]
        squares[...] = folded

    return call(body, [((rows, cols), F32), ((rows, 128), F32)])(base, *parts)


def last_norm(mixed, near, far, gain):
    rows, cols = mixed.shape

    def body(mixed_ref, near_ref, far_ref, gain_ref, out):
        squares = jnp.sum(near_ref[...] + far_ref[...], axis=1, keepdims=True)
        out[...] = (
            mixed_ref[...] * lax.rsqrt(squares / (2 * cols) + EPSILON) * gain_ref[...]
        ).astype(BF16)

    return call(body, [((rows, cols), BF16)])(mixed, near, far, gain.reshape(1, -1))[0]


def line_pg(x, n_pg):
    return [x] + [swap_pg(x, 4 * z, n_pg) for z in range(1, n_pg // 4)]


def fast_local(
    residual_in,
    queries,
    prefill_attn,
    kv_cache,
    page_table,
    lengths,
    out_weight,
    norm_gain_in,
    norm_gain_out,
    expert_ids,
    route_weight,
    slot_table,
    w_gate_up,
    w_down,
):
    n_pg = lax.axis_size("pg")
    me = lax.axis_index("pg")
    me_kv = lax.axis_index("kv").reshape(1).astype(jnp.int32)
    me_pg = me.reshape(1).astype(jnp.int32)
    rows, cols = residual_in.shape
    own_req = queries.shape[0]
    slots = w_gate_up.shape[0]
    pages, _, page_len, wide = kv_cache.shape
    head_dim = wide // 2
    max_pages = page_table.shape[1]
    top = expert_ids.shape[1]
    zs = n_pg // 4
    first = 2 * own_req * cols // 128

    packed = pack(queries, residual_in, expert_ids, route_weight, n_pg)
    sent = lax.all_to_all(packed, "pg", split_axis=0, concat_axis=0, tiled=True)
    send, near, base = project_prefill(
        after(prefill_attn, packed), out_weight, residual_in, me_kv
    )

    mine = me * slots + jnp.arange(slots, dtype=jnp.int32)
    expert = jnp.arange(slot_table.shape[0], dtype=jnp.int32)
    experts = jnp.max(
        jnp.where(slot_table[:, :, None] == mine[None, None, :], expert[:, None, None], -1), axis=0
    )
    page_ids = me * pages + jnp.arange(pages, dtype=jnp.int32)
    flat_table = page_table.reshape(-1)
    entry_index = jnp.arange(flat_table.shape[0], dtype=jnp.int32)
    found = jnp.sum(
        jnp.where(flat_table[None, :] == page_ids[:, None], entry_index[None, :], 0), axis=1
    )
    owner = found // max_pages
    owner_len = jnp.sum(
        jnp.where(
            owner[:, None] == jnp.arange(lengths.shape[0], dtype=jnp.int32)[None, :],
            lengths[None, :],
            0,
        ),
        axis=1,
    )
    live = owner_len - found % max_pages * page_len
    partial = page_attention(sent, kv_cache, owner, live, own_req, cols)
    got, far = after([swap_kv(send), swap_kv(near)], partial)
    middle, payload = norm_and_pages(base, send, got, far, norm_gain_in, partial)
    line = [swap_pg(payload, 4 * z, n_pg) for z in reversed(range(1, zs))][::-1]
    picks, gates, dec_gates = plan(
        after(sent, payload), first, top, experts, me_pg, slots, rows, own_req, zs
    )
    w_units, w_rows = load(after([w_gate_up, w_down], picks))

    def swap_each(arrays, mask):
        return [swap_pg(x, mask, n_pg) for x in arrays]

    def swap_units(arrays):
        return [swap_kv(x) for x in arrays]

    def gathered(which, groups, parts, decode=None):
        return gather(groups, which, picks, w_units, me_kv, me_pg, rows, own_req, parts, decode)

    *near, near_pages = join([payload] + after(line, w_units), cols, pages)
    across_pages = swap_pg(near_pages, 2, n_pg)
    across = swap_each(near, 2)
    near_pages_core = swap_pg(near_pages, 1, n_pg)
    xs0, *out0 = gathered([0, 2], [near, swap_each(near, 1)], (slots,))
    got0 = swap_units(out0)
    own0 = own_products(xs0, w_units, me_kv)
    across_pages = after(across_pages, own0)
    pieces = [near_pages, across_pages, near_pages_core, swap_pg(across_pages, 1, n_pg)]
    dec_send, dec_near, dec_base = project_decode(
        pieces, page_table, pages, sent, out_weight, me_kv, me_pg, own_req, head_dim
    )
    dec_got, dec_far = swap_kv(dec_send), swap_kv(dec_near)
    near0 = activate(own0, after(got0, dec_send))
    far0 = swap_units(near0)
    across = after(across, near0)
    across_core = swap_each(across, 1)
    dec_got, dec_far = after([dec_got, dec_far], across)
    dec_middle, dec_normed = first_norm(dec_base, dec_send, dec_got, dec_far, norm_gain_in)
    dec_own, dec_units = pick_decode(dec_normed, w_units, me_pg, own_req, zs)
    dec_got = swap_kv(dec_units)
    xs1, *out1 = gathered([1, 3], after([across, across_core], [dec_units, far0]), (slots,), dec_normed)
    got1 = swap_units(out1)
    own1 = own_products(xs1, w_units, me_kv)
    decode = decode_experts(dec_own, after(dec_got, own1), w_rows, dec_gates)
    keep0, *give0 = down(
        near0, after(far0, decode), w_rows, [0, 2], picks, gates, me_kv, rows, own_req, decode
    )
    parts0 = split_sum(keep0, swap_each(give0, 1), rows, F32, 8)
    lines0 = [swap_pg(parts0[z], 4 * z, n_pg) for z in reversed(range(1, zs))]
    near1 = activate(own1, after(got1, parts0), 2)
    far1 = swap_units(near1)
    base = line_base(middle, dec_middle, parts0[0], after(lines0, near1), me_pg, own_req)
    keep1, *give1 = down(
        near1, after(far1, base), w_rows, [1, 3], picks, gates, me_kv, rows, own_req
    )
    parts1 = split_sum(keep1, swap_each(give1, 1), rows)
    mixed, squares = close(
        base, [swap_pg(parts1[z], 4 * z + 2, n_pg) for z in reversed(range(zs))]
    )
    return last_norm(mixed, squares, swap_kv(squares), norm_gain_out)


def solution(mesh):
    fast = mesh.shape["kv"] == 2 and mesh.shape["pg"] == 16
    local = fast_local if fast else general_local
    in_specs = (
        P("pg", "kv"),
        P("pg", "kv"),
        P("pg", "kv"),
        P("pg", "kv", None, None),
        P(),
        P(),
        P("kv", None),
        P("kv"),
        P("kv"),
        P("pg", None),
        P("pg", None),
        P(),
        P("pg", "kv", None),
        P("pg", None, "kv"),
    )
    out_specs = P("pg", "kv")
    return jax.shard_map(local, mesh=mesh, in_specs=in_specs, out_specs=out_specs, check_vma=False)
```

```python
import functools

import jax
import jax.numpy as jnp
from jax import lax
from jax.experimental import pallas as pl
from jax.experimental.pallas import tpu as pltpu
from jax.sharding import PartitionSpec as P

NEG_FILL = -1e30
EPSILON = 1e-06


def merged_2(array, axis, join):
    gathered = jax.tree.map(
        lambda a, kind: lax.all_gather(a.astype(kind), axis),
        array,
        (jnp.bfloat16, jnp.bfloat16, jnp.bfloat16),
    )

    def take(source):
        return jax.tree.map(
            lambda a, own: lax.dynamic_index_in_dim(a, source, 0, False).astype(own.dtype),
            gathered,
            array,
        )

    return lax.fori_loop(
        1, lax.axis_size(axis), lambda source, state: join(state, take(source)), take(0)
    )


def merge_pair(first, secondary_slot):
    highest = jnp.maximum(first[0], secondary_slot[0])
    scale_a = jnp.exp(first[0] - highest)
    scale_b = jnp.exp(secondary_slot[0] - highest)
    head_count = first[0].shape[1]
    acc_a = first[2].reshape(first[2].shape[0], head_count, -1) * scale_a[:, :, None]
    acc_b = (
        secondary_slot[2].reshape(secondary_slot[2].shape[0], head_count, -1) * scale_b[:, :, None]
    )
    return (
        highest,
        first[1] * scale_a + secondary_slot[1] * scale_b,
        (acc_a + acc_b).reshape(first[2].shape),
    )


def general_local(
    residual_in,
    queries,
    prefill_attn,
    kv_cache,
    page_table,
    lengths,
    out_weight,
    norm_gain_in,
    norm_gain_out,
    expert_ids,
    route_weight,
    slot_table,
    w_gate_up,
    w_down,
):
    head_dim = kv_cache.shape[3] // 2
    page_len = kv_cache.shape[2]
    pages_here = kv_cache.shape[0]
    kv_here = kv_cache.shape[1]
    own_req = queries.shape[0]
    heads_here = queries.shape[1] // head_dim
    head_group = heads_here // kv_here
    total_req = page_table.shape[0]
    max_pages = page_table.shape[1]
    full_gate_up, full_down = (
        lax.all_gather(w_gate_up, "kv", axis=1, tiled=True),
        lax.all_gather(w_down, "kv", axis=2, tiled=True),
    )
    gathered = lax.all_gather(queries, "pg", axis=0, tiled=True)
    page_ids = lax.axis_index("pg") * pages_here + jnp.arange(pages_here, dtype=jnp.int32)
    flat_table = page_table.reshape(-1)
    entry_index = jnp.arange(flat_table.shape[0], dtype=jnp.int32)
    found = jnp.sum(
        jnp.where(flat_table[None, :] == page_ids[:, None], entry_index[None, :], 0), axis=1
    )
    owner = found // max_pages
    page_slot = found % max_pages
    owner_len = lengths[owner]
    query_pages = gathered[owner].reshape(pages_here, kv_here, head_group, head_dim)
    keys = kv_cache[:, :, :, :head_dim]
    values = kv_cache[:, :, :, head_dim:]
    scores = jnp.einsum(
        "pkgd,pktd->pkgt", query_pages, keys, preferred_element_type=jnp.float32
    ) * head_dim ** (-0.5)
    positions = page_slot[:, None] * page_len + jnp.arange(page_len, dtype=jnp.int32)[None, :]
    live = (positions < owner_len[:, None])[:, None, None, :]
    masked = jnp.where(live, scores, NEG_FILL)
    page_top = jnp.max(masked, axis=3)
    probs = jnp.where(live, jnp.exp(masked - page_top[..., None]), 0.0).astype(jnp.bfloat16)
    page_sum = jnp.sum(probs.astype(jnp.float32), axis=3).reshape(pages_here, heads_here)
    page_acc = jnp.einsum(
        "pkgt,pktd->pkgd", probs, values, preferred_element_type=jnp.float32
    ).reshape(pages_here, heads_here, head_dim)
    page_top = page_top.reshape(pages_here, heads_here)
    page_live = page_slot * page_len < owner_len
    member = (owner[:, None] == jnp.arange(total_req, dtype=jnp.int32)[None, :]) & page_live[
        :, None
    ]
    local_max = jnp.max(jnp.where(member[:, :, None], page_top[:, None, :], NEG_FILL), axis=0)
    member_t = member.astype(jnp.float32).T
    weight = jnp.exp(page_top - local_max[owner])
    sums = jnp.dot(member_t, weight * page_sum, precision=lax.Precision.HIGHEST)
    accs = jnp.dot(
        member_t,
        (weight[:, :, None] * page_acc).reshape(pages_here, -1),
        precision=lax.Precision.HIGHEST,
    )
    sums, accs = (sums, accs)
    merged = merged_2((local_max, sums, accs), "pg", merge_pair)
    start = lax.axis_index("pg") * own_req
    own_sum = lax.dynamic_slice_in_dim(merged[1], start, own_req, 0)
    own_acc = lax.dynamic_slice_in_dim(merged[2], start, own_req, 0)
    attn_dec = (own_acc.reshape(own_req, heads_here, head_dim) / own_sum[:, :, None]).reshape(
        own_req, -1
    )
    attn_dec = attn_dec.astype(jnp.bfloat16)
    attn_rows = jnp.concatenate([attn_dec, prefill_attn], axis=0)
    projected = jnp.dot(attn_rows, out_weight, preferred_element_type=jnp.float32)
    mixed_in = lax.psum_scatter(
        projected.astype(jnp.bfloat16), "kv", scatter_dimension=1, tiled=True
    ).astype(jnp.float32)
    middle = residual_in.astype(jnp.float32) + mixed_in
    full_width = residual_in.shape[1] * lax.axis_size("kv")
    in_squares = lax.psum(jnp.sum(middle * middle, axis=1), "kv")
    normed = (middle * lax.rsqrt(in_squares / full_width + EPSILON)[:, None] * norm_gain_in).astype(
        jnp.bfloat16
    )
    token_rows, top = expert_ids.shape
    copies = slot_table.shape[1]
    experts_total = slot_table.shape[0]
    kv_count = lax.axis_size("kv")
    capacity = kv_count * max(
        1,
        (token_rows * top * 5 + 4 * experts_total * kv_count - 1) // (4 * experts_total * kv_count),
    )
    slots_here = w_gate_up.shape[0]
    groups = lax.axis_size("pg")
    all_slots = slots_here * groups
    feature_cols = normed.shape[1]
    row_ids = lax.axis_index("pg") * token_rows + jnp.arange(token_rows, dtype=jnp.int32)
    parity = (row_ids[:, None] + jnp.arange(top, dtype=jnp.int32)[None, :]) % copies
    route_key = (expert_ids * copies + parity).reshape(-1)
    table_flat = slot_table.reshape(-1)
    table_index = jnp.arange(table_flat.shape[0], dtype=jnp.int32)
    target_slot = jnp.sum(
        jnp.where(route_key[:, None] == table_index[None, :], table_flat[None, :], 0), axis=1
    )
    match_count = (target_slot[:, None] == jnp.arange(all_slots, dtype=jnp.int32)[None, :]).astype(
        jnp.int32
    )
    rank = jnp.sum((jnp.cumsum(match_count, axis=0) - match_count) * match_count, axis=1)
    dest = target_slot * capacity + rank
    source_row = jnp.arange(token_rows * top, dtype=jnp.int32) // top
    outgoing = (
        jnp.zeros((all_slots * capacity, feature_cols), jnp.bfloat16)
        .at[dest]
        .set(normed[source_row])
    )
    outgoing = outgoing.reshape(groups, slots_here, capacity, feature_cols)
    arrived = lax.all_to_all(outgoing, "pg", split_axis=0, concat_axis=0, tiled=True)
    widened = lax.all_to_all(arrived, "kv", split_axis=2, concat_axis=3, tiled=True)
    gate_up = jnp.einsum(
        "pscd,sdf->pscf", widened, full_gate_up, preferred_element_type=jnp.float32
    )
    half = gate_up.shape[3] // 2
    hidden = (jax.nn.silu(gate_up[..., :half]) * gate_up[..., half:]).astype(jnp.bfloat16)
    produced = jnp.einsum(
        "pscf,sfd->pscd", hidden, full_down, preferred_element_type=jnp.float32
    ).astype(jnp.bfloat16)
    narrowed = lax.all_to_all(produced, "kv", split_axis=3, concat_axis=2, tiled=True)
    returned = lax.all_to_all(narrowed, "pg", split_axis=0, concat_axis=0, tiled=True)
    returned = returned.reshape(all_slots * capacity, feature_cols)
    picked = returned[dest].astype(jnp.float32).reshape(token_rows, top, feature_cols)
    mixed = middle + jnp.sum(picked * route_weight[:, :, None], axis=1)
    out_squares = lax.psum(jnp.sum(mixed * mixed, axis=1), "kv")
    return (mixed * lax.rsqrt(out_squares / full_width + EPSILON)[:, None] * norm_gain_out).astype(
        jnp.bfloat16
    )


F32 = jnp.float32
BF16 = jnp.bfloat16
CAP = 16
HIGH = lax.Precision.HIGHEST


def call(body, outs, scratch=(), smem=(), hbm=(), vmem=16, flops=10**9):
    def run(*operands):
        kinds = [
            pltpu.SMEM if n in smem else pltpu.HBM if n in hbm else pltpu.VMEM
            for n in range(len(operands))
        ]
        return pl.pallas_call(
            body,
            out_shape=[jax.ShapeDtypeStruct(s, d) for s, d in outs],
            in_specs=[pl.BlockSpec(memory_space=kind) for kind in kinds],
            out_specs=[pl.BlockSpec(memory_space=pltpu.VMEM) for _ in outs],
            scratch_shapes=list(scratch),
            compiler_params=pltpu.CompilerParams(
                vmem_limit_bytes=vmem * 2**20
            ),
            cost_estimate=pl.CostEstimate(flops=flops, bytes_accessed=1, transcendentals=0),
        )(*operands)

    return run


def after(values, *earlier):
    return lax.optimization_barrier((values, earlier))[0]


def iota(shape, dim):
    return lax.broadcasted_iota(jnp.int32, shape, dim)


def dot(a, b, precision=None):
    return jnp.dot(a, b, preferred_element_type=F32, precision=precision)


def dot_t(a, b):
    return lax.dot_general(a, b, (((1,), (1,)), ((), ())), preferred_element_type=F32)


def t_dot(a, b):
    return lax.dot_general(a, b, (((0,), (0,)), ((), ())), preferred_element_type=F32)


def swap_kv(x):
    return lax.ppermute(x, "kv", [(0, 1), (1, 0)])


def swap_pg(x, mask, n):
    return lax.ppermute(x, "pg", [(i, i ^ mask) for i in range(n)])


def pack(queries, residual, expert_ids, route_weight, n_pg):
    own_req, cols = queries.shape
    rows, top = expert_ids.shape
    tiles = cols // 128
    high = 2 * own_req * tiles
    total = high + top

    def body(q_hbm, res_hbm, ids_hbm, gates_hbm, out_ref, scr, q_ref, res_ref, ids, gates, sems):
        copies = [
            pltpu.make_async_copy(q_hbm, q_ref, sems.at[0]),
            pltpu.make_async_copy(res_hbm.at[0:16, :], res_ref, sems.at[1]),
            pltpu.make_async_copy(ids_hbm, ids, sems.at[2]),
            pltpu.make_async_copy(gates_hbm, gates, sems.at[3]),
        ]
        for copy in copies:
            copy.start()
        for copy in copies:
            copy.wait()
        for n, ref in enumerate((q_ref, res_ref)):
            for i in range(tiles):
                low = (n * tiles + i) * own_req
                scr[low : low + own_req, :] = ref[0:own_req, 128 * i : 128 * (i + 1)].astype(F32)
        scr[high:, 0:rows] = ids[...].astype(F32)
        scr[high:, 64 : 64 + rows] = gates[...]
        packed = scr[...].astype(BF16)
        for g in range(n_pg):
            out_ref[g] = packed

    return call(
        body,
        [((n_pg, total, 128), BF16)],
        [
            pltpu.VMEM((total, 128), F32),
            pltpu.VMEM((own_req, cols), BF16),
            pltpu.VMEM((16, cols), BF16),
            pltpu.VMEM((top, rows), expert_ids.dtype),
            pltpu.VMEM((top, rows), F32),
            pltpu.SemaphoreType.DMA((4,)),
        ],
        hbm=(0, 1, 2, 3),
        vmem=62,
    )(queries, residual, expert_ids.T, route_weight.T)[0]


def unpack(sent_ref, out, which, own_req):
    tiles = out.shape[1] // 128
    for g in range(sent_ref.shape[0]):
        for i in range(tiles):
            low = (which * tiles + i) * own_req
            out[g * own_req : (g + 1) * own_req, 128 * i : 128 * (i + 1)] = sent_ref[
                g, low : low + own_req, :
            ].astype(F32)


def routing(sent_ref, me, masks, first, top, count):
    got = [sent_ref[me ^ mask, first : first + top, :].astype(F32) for mask in masks]
    ids = jnp.concatenate([x[:, 0:count] for x in got], axis=1)
    gates = jnp.concatenate([x[:, 64 : 64 + count] for x in got], axis=1)
    return jnp.concatenate([ids, gates], axis=0)


def group_masks(g, zs):
    return [4 * z + 2 * (g % 2) + g // 2 for z in range(zs)]


def page_attention(sent, kv_cache, owner, live, own_req, cols):
    groups = sent.shape[0]
    pages, kv_here, page_len, wide = kv_cache.shape
    head_dim = wide // 2
    heads = cols // head_dim
    group = heads // kv_here
    rows = 16
    requests = groups * own_req
    keys = kv_here * page_len
    total = pages * rows

    def body(owner_col, live_col, sent_ref, kv_ref, out_ref, q_all, scores, probs, acc):
        unpack(sent_ref, q_all, 0, own_req)
        pick = (owner_col[...] == iota((total, requests), 1)).astype(BF16)
        wide_q = dot(pick, q_all[...].astype(BF16))
        spread = iota((total, cols), 0) % rows == iota((total, cols), 1) // head_dim
        fold = (iota((cols, wide), 0) % head_dim == iota((cols, wide), 1)).astype(BF16)
        q = dot(jnp.where(spread, wide_q, 0.0).astype(BF16), fold).astype(BF16)
        for p in range(pages):
            part = slice(p * rows, (p + 1) * rows)
            scores[part, :] = dot_t(q[part], kv_ref[p].reshape(keys, wide)) * head_dim ** (-0.5)
        col = iota((total, keys), 1)
        ok = (col // page_len == iota((total, keys), 0) % rows // group) & (
            col % page_len < live_col[...]
        )
        masked = jnp.where(ok, scores[...], NEG_FILL)
        top = jnp.max(masked, axis=1, keepdims=True).astype(BF16).astype(F32)
        share = jnp.where(ok, jnp.exp(masked - top), 0.0).astype(BF16)
        probs[...] = share
        whole = jnp.sum(share.astype(F32), axis=1, keepdims=True)
        for p in range(pages):
            part = slice(p * rows, (p + 1) * rows)
            acc[part, :] = dot(probs[part, :], kv_ref[p].reshape(keys, wide))
        unfold = (iota((wide, cols), 0) - head_dim == iota((wide, cols), 1) % head_dim).astype(BF16)
        here = iota((total, 128), 0) % rows == iota((total, 128), 1)
        merge = (iota((pages, total), 0) == iota((pages, total), 1) // rows).astype(BF16)
        flat = jnp.where(spread, dot(acc[...].astype(BF16), unfold), 0.0).astype(BF16)
        out_ref[:, 0:cols] = dot(merge, flat).astype(BF16)
        flat = jnp.where(here, top, 0.0).astype(BF16)
        out_ref[:, cols : cols + 128] = dot(merge, flat).astype(BF16)
        flat = jnp.where(here, whole, 0.0).astype(BF16)
        out_ref[:, cols + 128 :] = dot(merge, flat).astype(BF16)

    return call(
        body,
        [((pages, cols + 256), BF16)],
        [
            pltpu.VMEM((requests, cols), F32),
            pltpu.VMEM((total, keys), F32),
            pltpu.VMEM((total, keys), BF16),
            pltpu.VMEM((total, wide), F32),
        ],
    )(jnp.repeat(owner, rows)[:, None], jnp.repeat(live, rows)[:, None], sent, kv_cache)[0]


def half_products(left, w_ref, res, me, cols, far, near, base):
    mine = pl.multiple_of(me[0] * cols, 128)
    other = pl.multiple_of((1 - me[0]) * cols, 128)
    far[...] = dot(left, w_ref[:, pl.ds(other, cols)]).astype(BF16)
    own = dot(left, w_ref[:, pl.ds(mine, cols)]).astype(BF16).astype(F32) + res
    base[...] = own
    near[...] = own.astype(BF16)


def project_prefill(prefill, weight, residual, me_kv):
    rows, cols = residual.shape
    skip = rows - prefill.shape[0]

    def body(me, pre, w_ref, res, far, near, base, rows_scr):
        rows_scr[0:skip, :] = jnp.zeros((skip, cols), F32)
        rows_scr[skip:, :] = pre[...].astype(F32)
        left = rows_scr[...].astype(BF16)
        half_products(left, w_ref, res[...].astype(F32), me, cols, far, near, base)

    return call(
        body,
        [((rows, cols), BF16)] * 2 + [((rows, cols), F32)],
        [pltpu.VMEM((rows, cols), F32)],
        smem=(0,),
    )(me_kv, prefill, weight, residual)


def project_decode(pieces, page_table, pages, sent, weight, me_kv, me_pg, own_req, head_dim):
    groups = sent.shape[0]
    cols = weight.shape[0]
    requests = groups * own_req
    entries = page_table.size
    count = len(pieces)
    high = pieces[0].shape[0]
    total = count * high

    def body(me, pg, table_ref, w_ref, sent_ref, *refs):
        far, near, base, res = refs[count:]
        unpack(sent_ref, res, 1, own_req)
        table = jnp.concatenate([ref[...] for ref in refs[:count]], axis=0)
        page = jnp.concatenate(
            [table_ref[j : j + 1, :] for j in range(entries // requests)], axis=1
        )
        away = (page // pages) ^ pg[0]
        where = ((away % 2) * 2 + away // 2 % 2) * high + away // 4 * pages + page % pages
        pick = (iota((total, entries), 0) == where).astype(BF16)
        got = t_dot(pick, table)
        parts = [got[n : n + requests] for n in range(0, entries, requests)]
        sums = [part[:, cols + 128 :] for part in parts]
        tops = [
            jnp.where(tot > 0.0, part[:, cols : cols + 128], NEG_FILL)
            for part, tot in zip(parts, sums)
        ]
        best = functools.reduce(jnp.maximum, tops)
        scales = [jnp.where(tot > 0.0, jnp.exp(top - best), 0.0) for top, tot in zip(tops, sums)]
        whole = functools.reduce(jnp.add, [scale * tot for scale, tot in zip(scales, sums)])
        whole = jnp.where(whole > 0.0, whole, 1.0)
        expand = (iota((128, cols), 0) == iota((128, cols), 1) // head_dim).astype(BF16)
        share = jnp.concatenate([scale / whole for scale in scales], axis=0)
        share_high = share.astype(BF16)
        share_low = (share - share_high.astype(F32)).astype(BF16)
        wide = dot(share_high, expand) + dot(share_low, expand)
        merged = jnp.zeros((requests, cols), F32)
        for n, part in enumerate(parts):
            merged += wide[n * requests : (n + 1) * requests] * part[:, 0:cols]
        half_products(merged.astype(BF16), w_ref, res[...], me, cols, far, near, base)

    return call(
        body,
        [((requests, cols), BF16)] * 2 + [((requests, cols), F32)],
        [pltpu.VMEM((requests, cols), F32)],
        smem=(0, 1),
    )(me_kv, me_pg, page_table.T, weight, sent, *pieces)


def norm_and_pages(base, sent, got_own, got_far, gain, pages):
    rows, cols = base.shape
    count, wide = pages.shape
    lanes = wide * count // rows

    def body(base_ref, sent_ref, got_ref, far_ref, gain_ref, pages_ref, middle, out):
        mid = base_ref[...] + got_ref[...].astype(F32)
        far = far_ref[...].astype(F32) + sent_ref[...].astype(F32)
        squares = jnp.sum(mid * mid + far * far, axis=1, keepdims=True)
        middle[...] = mid
        out[:, 0:cols] = (
            mid * lax.rsqrt(squares / (2 * cols) + EPSILON) * gain_ref[...]
        ).astype(BF16)
        for n in range(rows // count):
            out[n * count : (n + 1) * count, cols:] = pages_ref[:, n * lanes : (n + 1) * lanes]

    return call(body, [((rows, cols), F32), ((rows, cols + lanes), BF16)])(
        base, sent, got_own, got_far, gain.reshape(1, -1), pages
    )


def join(parts, cols, pages):
    rows, wide = parts[0].shape
    lanes = wide - cols
    count = len(parts)
    quarters = rows // pages

    def body(*refs):
        outs, out_pages = refs[-3:-1], refs[-1]
        for n in range(count):
            low = n % (count // 2) * rows
            outs[n // (count // 2)][low : low + rows, :] = refs[n][:, 0:cols]
            for k in range(quarters):
                out_pages[n * pages : (n + 1) * pages, k * lanes : (k + 1) * lanes] = refs[n][
                    k * pages : (k + 1) * pages, cols:
                ]

    return call(
        body,
        [((count // 2 * rows, cols), BF16)] * 2 + [((count * pages, quarters * lanes), BF16)],
    )(*parts)


def first_norm(base, sent, got_own, got_far, gain):
    rows, cols = base.shape

    def body(base_ref, sent_ref, got_ref, far_ref, gain_ref, middle, normed):
        mid = base_ref[...] + got_ref[...].astype(F32)
        far = far_ref[...].astype(F32) + sent_ref[...].astype(F32)
        squares = jnp.sum(mid * mid + far * far, axis=1, keepdims=True)
        middle[...] = mid
        normed[...] = (
            mid * lax.rsqrt(squares / (2 * cols) + EPSILON) * gain_ref[...]
        ).astype(BF16)

    return call(body, [((rows, cols), F32), ((rows, cols), BF16)])(
        base, sent, got_own, got_far, gain.reshape(1, -1)
    )


def routes(info, experts, slots, block_rows, skip):
    top = info.shape[0] // 2
    tokens = info.shape[1]
    token = iota((top, tokens), 1) % block_rows
    odd = (token + iota((top, tokens), 0)) % 2 == 1
    hits, gates = [], []
    for s in range(slots):
        wanted = jnp.where(odd, experts[1, s], experts[0, s]).astype(F32)
        hit = (info[0:top] == wanted) & (token >= skip)
        hits.append(jnp.sum(hit.astype(F32), axis=0, keepdims=True))
        gates.append(jnp.sum(jnp.where(hit, info[top:], 0.0), axis=0, keepdims=True))
    fill = [jnp.zeros((8 - slots, tokens), F32)] if slots < 8 else []
    stacked = jnp.concatenate(hits + fill, axis=0)
    row, col = iota((tokens, tokens), 0), iota((tokens, tokens), 1)
    before = ((row < col) & (row // block_rows == col // block_rows)).astype(BF16)
    ranks = dot(stacked.astype(BF16), before).astype(jnp.int32)
    places = [jnp.where(hits[s] > 0.0, ranks[s : s + 1], -1) for s in range(slots)]
    return places, gates


def one_hot(place, block_rows):
    tokens = place.shape[1]
    shape = (tokens // block_rows * CAP, tokens)
    row = iota(shape, 0)
    return (place == row % CAP) & (iota(shape, 1) // block_rows == row // CAP)


def plan(sent, first, top, experts, me_pg, slots, rows, skip, zs):
    part = zs * CAP
    tokens = zs * rows

    def body(pg, es, sent_ref, picks, gates, dec_gates):
        for g in range(4):
            info = routing(sent_ref, pg[0], group_masks(g, zs), first, top, rows)
            places, shares = routes(info, es, slots, rows, 0 if g % 2 else skip)
            for s in range(slots):
                hot = one_hot(places[s], rows)
                low = s * part
                picks[g, low : low + part, :] = hot.astype(BF16)
                gates[g, low : low + part, :] = jnp.broadcast_to(
                    jnp.sum(jnp.where(hot, shares[s], 0.0), axis=1, keepdims=True), (part, 128)
                )
        masks = group_masks(0, zs) + group_masks(2, zs)
        count = len(masks) * skip
        info = routing(sent_ref, pg[0], masks, first, top, skip)
        ids, shares = info[0:top], info[top:]
        odd = (iota((top, count), 1) % skip + iota((top, count), 0)) % 2 == 1
        eye = iota((count, count), 0) == iota((count, count), 1)
        for s in range(slots):
            wanted = jnp.where(odd, es[1, s], es[0, s]).astype(F32)
            share = jnp.sum(jnp.where(ids == wanted, shares, 0.0), axis=0, keepdims=True)
            dec_gates[s * count : (s + 1) * count, :] = jnp.broadcast_to(
                jnp.sum(jnp.where(eye, share, 0.0), axis=1, keepdims=True), (count, 128)
            )

    return call(
        body,
        [
            ((4, slots * part, tokens), BF16),
            ((4, slots * part, 128), F32),
            ((slots * 2 * zs * skip, 128), F32),
        ],
        smem=(0, 1),
    )(me_pg, experts, sent)


def load(arrays):
    count = len(arrays)

    def body(*refs):
        sems = refs[-1]
        copies = [
            pltpu.make_async_copy(refs[n].at[s], refs[count + n].at[s], sems.at[n, s])
            for n in range(count)
            for s in range(arrays[n].shape[0])
        ]
        for copy in copies:
            copy.start()
        for copy in copies:
            copy.wait()

    return call(
        body,
        [(x.shape, x.dtype) for x in arrays],
        [pltpu.SemaphoreType.DMA((count, arrays[0].shape[0]))],
        hbm=tuple(range(count)),
        vmem=44,
    )(*arrays)


def products(xs, w_ref, side, *outs):
    half = outs[0].shape[2] // 2
    places = [(out, n) for out in outs for n in range(out.shape[0])]
    for s, (out, n) in enumerate(places):
        x = xs[s] if len(xs.shape) == 3 else xs[...]
        for k in range(2):
            low = pl.multiple_of(k * 2 * half + side * half, 128)
            out[n, :, k * half : (k + 1) * half] = dot(x, w_ref[s, :, pl.ds(low, half)]).astype(
                out.dtype
            )


def gather(groups, which, picks, w, me_kv, me_pg, rows, skip, parts, decode=None):
    count, slots = len(groups), w.shape[0]
    pieces = len(groups[0])
    cols = w.shape[1]
    tokens = pieces * groups[0][0].shape[0]
    zs = tokens // rows
    part = zs * CAP
    ff = w.shape[2] // 2

    def body(me, pg, w_ref, picks_ref, *refs):
        xs, sends = refs[-1 - len(parts)], refs[-len(parts) :]
        for n, g in enumerate(which):
            x = jnp.concatenate(
                [ref[...] for ref in refs[n * pieces : (n + 1) * pieces]], axis=0
            )
            if decode is not None:
                dec = refs[count * pieces][...]
                shape = (tokens, dec.shape[0])
                row = iota(shape, 0)
                source = jnp.zeros(shape, jnp.int32)
                for z, mask in enumerate(group_masks(g, zs)):
                    source = jnp.where(row // rows == z, (pg[0] ^ mask) * skip, source)
                late = row % rows < skip
                put = late & (iota(shape, 1) == source + row % rows)
                x = jnp.where(
                    iota((tokens, cols), 0) % rows < skip,
                    dot(put.astype(BF16), dec),
                    x.astype(F32),
                ).astype(BF16)
            got = dot(picks_ref[g], x).astype(BF16)
            for s in range(slots):
                xs[s, n * part : (n + 1) * part, :] = got[s * part : (s + 1) * part]
        products(xs, w_ref, 1 - me[0], *sends)

    more = [] if decode is None else [decode]
    high = count * part
    return call(
        body,
        [((slots, high, cols), BF16)] + [((n, high, ff), BF16) for n in parts],
        smem=(0, 1),
    )(me_kv, me_pg, w, picks, *[x for group in groups for x in group], *more)


def pick_decode(normed, w, me_pg, skip, zs):
    slots, _, wide = w.shape
    total, cols = normed.shape
    masks = group_masks(0, zs) + group_masks(2, zs)
    rows = len(masks) * skip

    def body(pg, w_ref, x_ref, own, send):
        row = iota((rows, total), 0)
        source = jnp.zeros((rows, total), jnp.int32)
        for n, mask in enumerate(masks):
            source = jnp.where(row // skip == n, (pg[0] ^ mask) * skip, source)
        put = iota((rows, total), 1) == source + row % skip
        x = dot(put.astype(BF16), x_ref[...]).astype(BF16)
        for s in range(slots):
            made = dot(x, w_ref[s])
            own[s] = made
            send[s] = made.astype(BF16)

    return call(body, [((slots, rows, wide), F32), ((slots, rows, wide), BF16)], smem=(0,))(
        me_pg, w, normed
    )


def own_products(xs, w, me_kv, flops=1):
    def body(me, w_ref, x_ref, out):
        products(x_ref, w_ref, me[0], out)

    return call(body, [((w.shape[0], xs.shape[-2], w.shape[2] // 2), F32)], smem=(0,), flops=flops)(
        me_kv, w, xs
    )[0]


def activate(own, got, parts=1):
    slots, rows, ff = own.shape
    half = ff // 2
    high = rows // parts

    def body(own_ref, *refs):
        places = [(ref, n) for ref in refs[:-parts] for n in range(ref.shape[0])]
        for s, (ref, n) in enumerate(places):
            gate = own_ref[s, :, 0:half] + ref[n, :, 0:half].astype(F32)
            up = own_ref[s, :, half:] + ref[n, :, half:].astype(F32)
            hidden = (gate / (1.0 + jnp.exp(-gate)) * up).astype(BF16)
            for k in range(parts):
                refs[k - parts][s] = hidden[k * high : (k + 1) * high]

    return call(body, [((slots, high, half), BF16)] * parts, flops=1)(own, *got)


def outputs(near, far, w_ref, me, s):
    half = near[0].shape[2]
    made = dot(
        jnp.concatenate([ref[s] for ref in near], axis=0),
        w_ref[s, pl.ds(pl.multiple_of(me * half, 128), half), :],
    )
    return made + dot(
        jnp.concatenate([ref[s] for ref in far], axis=0),
        w_ref[s, pl.ds(pl.multiple_of((1 - me) * half, 128), half), :],
    )


def decode_experts(own, got, w_down, gates):
    slots, rows, wide = own.shape
    cols = w_down.shape[2]
    half = wide // 2

    def body(w_ref, own_ref, got_ref, gates_ref, out):
        total = jnp.zeros((rows, cols), F32)
        for s in range(slots):
            units = own_ref[s] + got_ref[s].astype(F32)
            gate, up = units[:, 0:half], units[:, half:]
            hidden = (gate / (1.0 + jnp.exp(-gate)) * up).astype(BF16)
            made = dot(hidden, w_ref[s]).astype(BF16).astype(F32)
            total = total + made * gates_ref[s * rows : (s + 1) * rows, 0:1]
        out[...] = total

    return call(body, [((rows, cols), F32)], flops=1)(w_down, own, got, gates)[0]


def down(near, far, w_down, which, picks, gates, me_kv, rows, skip, decode=None):
    pieces = len(near)
    slots, total_rows, _ = near[0].shape
    total_rows = total_rows * pieces
    cols = w_down.shape[2]
    count = len(which)
    part = total_rows // count
    blocks = part // CAP

    def body(me, w_ref, picks_ref, gates_ref, *refs):
        near_refs, far_refs = refs[:pieces], refs[pieces : 2 * pieces]
        outs = refs[-3:]
        made = [outputs(near_refs, far_refs, w_ref, me[0], s) for s in range(slots)]
        for n, g in enumerate(which):
            parts = jnp.concatenate(
                [made[s][n * part : (n + 1) * part] for s in range(slots)], axis=0
            )
            parts = (parts * gates_ref[g, :, 0:1]).astype(BF16)
            total = t_dot(picks_ref[g], parts)
            for b in range(blocks):
                out, low = outs[n + b * 2 // blocks if n else 0], b * rows
                low = low % out.shape[0]
                block = total[b * rows : (b + 1) * rows]
                out[low : low + rows, :] = block.astype(BF16)
                if decode is None:
                    continue
                late = (n * blocks + b) * skip
                late = jnp.concatenate([refs[2 * pieces][late : late + skip, :], block[skip:16]], axis=0)
                out[low : low + 16, :] = late.astype(BF16)

    more = [] if decode is None else [decode]
    shapes = [((blocks * rows, cols), BF16)] + [((blocks // 2 * rows, cols), BF16)] * 2
    return call(body, shapes, smem=(0,), flops=1)(
        me_kv, w_down, picks, gates, *near, *far, *more
    )


def split_sum(kept, halves, rows, first=BF16, pad=0):
    cols = kept.shape[1]
    high = halves[0].shape[0]
    count = kept.shape[0] // rows

    def body(kept_ref, *refs):
        for n in range(count):
            low = n * rows
            more = refs[low // high][low % high : low % high + rows, :]
            total = kept_ref[low : low + rows, :].astype(F32) + more.astype(F32)
            out = refs[2 + n]
            out[0:rows, :] = total.astype(out.dtype)
            if n and pad:
                out[rows:, :] = jnp.zeros((pad, cols), out.dtype)

    return call(
        body, [((rows, cols), first)] + [((rows + pad, cols), BF16)] * (count - 1), flops=1
    )(kept, *halves)


def line_base(middle, decode_middle, own, parts, me_pg, skip):
    rows, cols = middle.shape

    def body(pg, mid, dec, *refs):
        out = refs[-1]
        total = refs[0][...]
        for ref in refs[1:-1]:
            total = total + ref[0:rows, :].astype(F32)
        out[...] = total + mid[...]
        put = iota((8, dec.shape[0]), 1) == pg[0] * skip + iota((8, dec.shape[0]), 0)
        put = put & (iota((8, dec.shape[0]), 0) < skip)
        stream = dot(put.astype(F32), dec[...], HIGH)
        stream = jnp.where(iota((8, cols), 0) < skip, stream, mid[0:8, :])
        out[0:8, :] = total[0:8] + stream

    return call(body, [((rows, cols), F32)], smem=(0,))(
        me_pg, middle, decode_middle, own, *parts
    )[0]


def close(base, parts):
    rows, cols = base.shape

    def body(base_ref, *refs):
        mixed, squares = refs[-2:]
        total = base_ref[...]
        for ref in refs[:-2]:
            total = total + ref[...].astype(F32)
        mixed[...] = total
        total = total * total
        folded = total[:, 0:128]
        for n in range(1, cols // 128):
            folded = folded + total[:, n * 128 : (n + 1) * 128]
        squares[...] = folded

    return call(body, [((rows, cols), F32), ((rows, 128), F32)])(base, *parts)


def last_norm(mixed, near, far, gain):
    rows, cols = mixed.shape

    def body(mixed_ref, near_ref, far_ref, gain_ref, out):
        squares = jnp.sum(near_ref[...] + far_ref[...], axis=1, keepdims=True)
        out[...] = (
            mixed_ref[...] * lax.rsqrt(squares / (2 * cols) + EPSILON) * gain_ref[...]
        ).astype(BF16)

    return call(body, [((rows, cols), BF16)])(mixed, near, far, gain.reshape(1, -1))[0]


def line_pg(x, n_pg):
    return [x] + [swap_pg(x, 4 * z, n_pg) for z in range(1, n_pg // 4)]


def fast_local(
    residual_in,
    queries,
    prefill_attn,
    kv_cache,
    page_table,
    lengths,
    out_weight,
    norm_gain_in,
    norm_gain_out,
    expert_ids,
    route_weight,
    slot_table,
    w_gate_up,
    w_down,
):
    n_pg = lax.axis_size("pg")
    me = lax.axis_index("pg")
    me_kv = lax.axis_index("kv").reshape(1).astype(jnp.int32)
    me_pg = me.reshape(1).astype(jnp.int32)
    rows, cols = residual_in.shape
    own_req = queries.shape[0]
    slots = w_gate_up.shape[0]
    pages, _, page_len, wide = kv_cache.shape
    head_dim = wide // 2
    max_pages = page_table.shape[1]
    top = expert_ids.shape[1]
    zs = n_pg // 4
    first = 2 * own_req * cols // 128

    packed = pack(queries, residual_in, expert_ids, route_weight, n_pg)
    sent = lax.all_to_all(packed, "pg", split_axis=0, concat_axis=0, tiled=True)
    send, near, base = project_prefill(
        after(prefill_attn, packed), out_weight, residual_in, me_kv
    )

    mine = me * slots + jnp.arange(slots, dtype=jnp.int32)
    expert = jnp.arange(slot_table.shape[0], dtype=jnp.int32)
    experts = jnp.max(
        jnp.where(slot_table[:, :, None] == mine[None, None, :], expert[:, None, None], -1), axis=0
    )
    page_ids = me * pages + jnp.arange(pages, dtype=jnp.int32)
    flat_table = page_table.reshape(-1)
    entry_index = jnp.arange(flat_table.shape[0], dtype=jnp.int32)
    found = jnp.sum(
        jnp.where(flat_table[None, :] == page_ids[:, None], entry_index[None, :], 0), axis=1
    )
    owner = found // max_pages
    owner_len = jnp.sum(
        jnp.where(
            owner[:, None] == jnp.arange(lengths.shape[0], dtype=jnp.int32)[None, :],
            lengths[None, :],
            0,
        ),
        axis=1,
    )
    live = owner_len - found % max_pages * page_len
    partial = page_attention(sent, kv_cache, owner, live, own_req, cols)
    got, far = after([swap_kv(send), swap_kv(near)], partial)
    middle, payload = norm_and_pages(base, send, got, far, norm_gain_in, partial)
    line = [swap_pg(payload, 4 * z, n_pg) for z in reversed(range(1, zs))][::-1]
    picks, gates, dec_gates = plan(
        after(sent, payload), first, top, experts, me_pg, slots, rows, own_req, zs
    )
    w_units, w_rows = load(after([w_gate_up, w_down], picks))

    def swap_each(arrays, mask):
        return [swap_pg(x, mask, n_pg) for x in arrays]

    def swap_units(arrays):
        return [swap_kv(x) for x in arrays]

    def gathered(which, groups, parts, decode=None):
        return gather(groups, which, picks, w_units, me_kv, me_pg, rows, own_req, parts, decode)

    *near, near_pages = join([payload] + after(line, w_units), cols, pages)
    across_pages = swap_pg(near_pages, 2, n_pg)
    across = swap_each(near, 2)
    near_pages_core = swap_pg(near_pages, 1, n_pg)
    xs0, *out0 = gathered([0, 2], [near, swap_each(near, 1)], (slots,))
    got0 = swap_units(out0)
    own0 = own_products(xs0, w_units, me_kv)
    across_pages = after(across_pages, own0)
    pieces = [near_pages, across_pages, near_pages_core, swap_pg(across_pages, 1, n_pg)]
    dec_send, dec_near, dec_base = project_decode(
        pieces, page_table, pages, sent, out_weight, me_kv, me_pg, own_req, head_dim
    )
    dec_got, dec_far = swap_kv(dec_send), swap_kv(dec_near)
    near0 = activate(own0, after(got0, dec_send))
    far0 = swap_units(near0)
    across = after(across, near0)
    across_core = swap_each(across, 1)
    dec_got, dec_far = after([dec_got, dec_far], across)
    dec_middle, dec_normed = first_norm(dec_base, dec_send, dec_got, dec_far, norm_gain_in)
    dec_own, dec_units = pick_decode(dec_normed, w_units, me_pg, own_req, zs)
    dec_got = swap_kv(dec_units)
    xs1, *out1 = gathered([1, 3], after([across, across_core], [dec_units, far0]), (slots,), dec_normed)
    got1 = swap_units(out1)
    own1 = own_products(xs1, w_units, me_kv)
    decode = decode_experts(dec_own, after(dec_got, own1), w_rows, dec_gates)
    keep0, *give0 = down(
        near0, after(far0, decode), w_rows, [0, 2], picks, gates, me_kv, rows, own_req, decode
    )
    parts0 = split_sum(keep0, swap_each(give0, 1), rows, F32, 0)
    lines0 = [swap_pg(parts0[z], 4 * z, n_pg) for z in reversed(range(1, zs))]
    near1 = activate(own1, after(got1, parts0), 2)
    far1 = swap_units(near1)
    base = line_base(middle, dec_middle, parts0[0], after(lines0, near1), me_pg, own_req)
    keep1, *give1 = down(
        near1, after(far1, base), w_rows, [1, 3], picks, gates, me_kv, rows, own_req
    )
    parts1 = split_sum(keep1, swap_each(give1, 1), rows)
    mixed, squares = close(
        base, [swap_pg(parts1[z], 4 * z + 2, n_pg) for z in reversed(range(zs))]
    )
    return last_norm(mixed, squares, swap_kv(squares), norm_gain_out)


def solution(mesh):
    fast = mesh.shape["kv"] == 2 and mesh.shape["pg"] == 16
    local = fast_local if fast else general_local
    in_specs = (
        P("pg", "kv"),
        P("pg", "kv"),
        P("pg", "kv"),
        P("pg", "kv", None, None),
        P(),
        P(),
        P("kv", None),
        P("kv"),
        P("kv"),
        P("pg", None),
        P("pg", None),
        P(),
        P("pg", "kv", None),
        P("pg", None, "kv"),
    )
    out_specs = P("pg", "kv")
    return jax.shard_map(local, mesh=mesh, in_specs=in_specs, out_specs=out_specs, check_vma=False)
```

```python
import functools

import jax
import jax.numpy as jnp
from jax import lax
from jax.experimental import pallas as pl
from jax.experimental.pallas import tpu as pltpu
from jax.sharding import PartitionSpec as P

NEG_FILL = -1e30
EPSILON = 1e-06


def merged_2(array, axis, join):
    gathered = jax.tree.map(
        lambda a, kind: lax.all_gather(a.astype(kind), axis),
        array,
        (jnp.bfloat16, jnp.bfloat16, jnp.bfloat16),
    )

    def take(source):
        return jax.tree.map(
            lambda a, own: lax.dynamic_index_in_dim(a, source, 0, False).astype(own.dtype),
            gathered,
            array,
        )

    return lax.fori_loop(
        1, lax.axis_size(axis), lambda source, state: join(state, take(source)), take(0)
    )


def merge_pair(first, secondary_slot):
    highest = jnp.maximum(first[0], secondary_slot[0])
    scale_a = jnp.exp(first[0] - highest)
    scale_b = jnp.exp(secondary_slot[0] - highest)
    head_count = first[0].shape[1]
    acc_a = first[2].reshape(first[2].shape[0], head_count, -1) * scale_a[:, :, None]
    acc_b = (
        secondary_slot[2].reshape(secondary_slot[2].shape[0], head_count, -1) * scale_b[:, :, None]
    )
    return (
        highest,
        first[1] * scale_a + secondary_slot[1] * scale_b,
        (acc_a + acc_b).reshape(first[2].shape),
    )


def general_local(
    residual_in,
    queries,
    prefill_attn,
    kv_cache,
    page_table,
    lengths,
    out_weight,
    norm_gain_in,
    norm_gain_out,
    expert_ids,
    route_weight,
    slot_table,
    w_gate_up,
    w_down,
):
    head_dim = kv_cache.shape[3] // 2
    page_len = kv_cache.shape[2]
    pages_here = kv_cache.shape[0]
    kv_here = kv_cache.shape[1]
    own_req = queries.shape[0]
    heads_here = queries.shape[1] // head_dim
    head_group = heads_here // kv_here
    total_req = page_table.shape[0]
    max_pages = page_table.shape[1]
    full_gate_up, full_down = (
        lax.all_gather(w_gate_up, "kv", axis=1, tiled=True),
        lax.all_gather(w_down, "kv", axis=2, tiled=True),
    )
    gathered = lax.all_gather(queries, "pg", axis=0, tiled=True)
    page_ids = lax.axis_index("pg") * pages_here + jnp.arange(pages_here, dtype=jnp.int32)
    flat_table = page_table.reshape(-1)
    entry_index = jnp.arange(flat_table.shape[0], dtype=jnp.int32)
    found = jnp.sum(
        jnp.where(flat_table[None, :] == page_ids[:, None], entry_index[None, :], 0), axis=1
    )
    owner = found // max_pages
    page_slot = found % max_pages
    owner_len = lengths[owner]
    query_pages = gathered[owner].reshape(pages_here, kv_here, head_group, head_dim)
    keys = kv_cache[:, :, :, :head_dim]
    values = kv_cache[:, :, :, head_dim:]
    scores = jnp.einsum(
        "pkgd,pktd->pkgt", query_pages, keys, preferred_element_type=jnp.float32
    ) * head_dim ** (-0.5)
    positions = page_slot[:, None] * page_len + jnp.arange(page_len, dtype=jnp.int32)[None, :]
    live = (positions < owner_len[:, None])[:, None, None, :]
    masked = jnp.where(live, scores, NEG_FILL)
    page_top = jnp.max(masked, axis=3)
    probs = jnp.where(live, jnp.exp(masked - page_top[..., None]), 0.0).astype(jnp.bfloat16)
    page_sum = jnp.sum(probs.astype(jnp.float32), axis=3).reshape(pages_here, heads_here)
    page_acc = jnp.einsum(
        "pkgt,pktd->pkgd", probs, values, preferred_element_type=jnp.float32
    ).reshape(pages_here, heads_here, head_dim)
    page_top = page_top.reshape(pages_here, heads_here)
    page_live = page_slot * page_len < owner_len
    member = (owner[:, None] == jnp.arange(total_req, dtype=jnp.int32)[None, :]) & page_live[
        :, None
    ]
    local_max = jnp.max(jnp.where(member[:, :, None], page_top[:, None, :], NEG_FILL), axis=0)
    member_t = member.astype(jnp.float32).T
    weight = jnp.exp(page_top - local_max[owner])
    sums = jnp.dot(member_t, weight * page_sum, precision=lax.Precision.HIGHEST)
    accs = jnp.dot(
        member_t,
        (weight[:, :, None] * page_acc).reshape(pages_here, -1),
        precision=lax.Precision.HIGHEST,
    )
    sums, accs = (sums, accs)
    merged = merged_2((local_max, sums, accs), "pg", merge_pair)
    start = lax.axis_index("pg") * own_req
    own_sum = lax.dynamic_slice_in_dim(merged[1], start, own_req, 0)
    own_acc = lax.dynamic_slice_in_dim(merged[2], start, own_req, 0)
    attn_dec = (own_acc.reshape(own_req, heads_here, head_dim) / own_sum[:, :, None]).reshape(
        own_req, -1
    )
    attn_dec = attn_dec.astype(jnp.bfloat16)
    attn_rows = jnp.concatenate([attn_dec, prefill_attn], axis=0)
    projected = jnp.dot(attn_rows, out_weight, preferred_element_type=jnp.float32)
    mixed_in = lax.psum_scatter(
        projected.astype(jnp.bfloat16), "kv", scatter_dimension=1, tiled=True
    ).astype(jnp.float32)
    middle = residual_in.astype(jnp.float32) + mixed_in
    full_width = residual_in.shape[1] * lax.axis_size("kv")
    in_squares = lax.psum(jnp.sum(middle * middle, axis=1), "kv")
    normed = (middle * lax.rsqrt(in_squares / full_width + EPSILON)[:, None] * norm_gain_in).astype(
        jnp.bfloat16
    )
    token_rows, top = expert_ids.shape
    copies = slot_table.shape[1]
    experts_total = slot_table.shape[0]
    kv_count = lax.axis_size("kv")
    capacity = kv_count * max(
        1,
        (token_rows * top * 5 + 4 * experts_total * kv_count - 1) // (4 * experts_total * kv_count),
    )
    slots_here = w_gate_up.shape[0]
    groups = lax.axis_size("pg")
    all_slots = slots_here * groups
    feature_cols = normed.shape[1]
    row_ids = lax.axis_index("pg") * token_rows + jnp.arange(token_rows, dtype=jnp.int32)
    parity = (row_ids[:, None] + jnp.arange(top, dtype=jnp.int32)[None, :]) % copies
    route_key = (expert_ids * copies + parity).reshape(-1)
    table_flat = slot_table.reshape(-1)
    table_index = jnp.arange(table_flat.shape[0], dtype=jnp.int32)
    target_slot = jnp.sum(
        jnp.where(route_key[:, None] == table_index[None, :], table_flat[None, :], 0), axis=1
    )
    match_count = (target_slot[:, None] == jnp.arange(all_slots, dtype=jnp.int32)[None, :]).astype(
        jnp.int32
    )
    rank = jnp.sum((jnp.cumsum(match_count, axis=0) - match_count) * match_count, axis=1)
    dest = target_slot * capacity + rank
    source_row = jnp.arange(token_rows * top, dtype=jnp.int32) // top
    outgoing = (
        jnp.zeros((all_slots * capacity, feature_cols), jnp.bfloat16)
        .at[dest]
        .set(normed[source_row])
    )
    outgoing = outgoing.reshape(groups, slots_here, capacity, feature_cols)
    arrived = lax.all_to_all(outgoing, "pg", split_axis=0, concat_axis=0, tiled=True)
    widened = lax.all_to_all(arrived, "kv", split_axis=2, concat_axis=3, tiled=True)
    gate_up = jnp.einsum(
        "pscd,sdf->pscf", widened, full_gate_up, preferred_element_type=jnp.float32
    )
    half = gate_up.shape[3] // 2
    hidden = (jax.nn.silu(gate_up[..., :half]) * gate_up[..., half:]).astype(jnp.bfloat16)
    produced = jnp.einsum(
        "pscf,sfd->pscd", hidden, full_down, preferred_element_type=jnp.float32
    ).astype(jnp.bfloat16)
    narrowed = lax.all_to_all(produced, "kv", split_axis=3, concat_axis=2, tiled=True)
    returned = lax.all_to_all(narrowed, "pg", split_axis=0, concat_axis=0, tiled=True)
    returned = returned.reshape(all_slots * capacity, feature_cols)
    picked = returned[dest].astype(jnp.float32).reshape(token_rows, top, feature_cols)
    mixed = middle + jnp.sum(picked * route_weight[:, :, None], axis=1)
    out_squares = lax.psum(jnp.sum(mixed * mixed, axis=1), "kv")
    return (mixed * lax.rsqrt(out_squares / full_width + EPSILON)[:, None] * norm_gain_out).astype(
        jnp.bfloat16
    )


F32 = jnp.float32
BF16 = jnp.bfloat16
CAP = 16
HIGH = lax.Precision.HIGHEST


def call(body, outs, scratch=(), smem=(), hbm=(), vmem=16, flops=10**9):
    def run(*operands):
        kinds = [
            pltpu.SMEM if n in smem else pltpu.HBM if n in hbm else pltpu.VMEM
            for n in range(len(operands))
        ]
        return pl.pallas_call(
            body,
            out_shape=[jax.ShapeDtypeStruct(s, d) for s, d in outs],
            in_specs=[pl.BlockSpec(memory_space=kind) for kind in kinds],
            out_specs=[pl.BlockSpec(memory_space=pltpu.VMEM) for _ in outs],
            scratch_shapes=list(scratch),
            compiler_params=pltpu.CompilerParams(
                vmem_limit_bytes=vmem * 2**20
            ),
            cost_estimate=pl.CostEstimate(flops=flops, bytes_accessed=1, transcendentals=0),
        )(*operands)

    return run


def after(values, *earlier):
    return lax.optimization_barrier((values, earlier))[0]


def iota(shape, dim):
    return lax.broadcasted_iota(jnp.int32, shape, dim)


def dot(a, b, precision=None):
    return jnp.dot(a, b, preferred_element_type=F32, precision=precision)


def dot_t(a, b):
    return lax.dot_general(a, b, (((1,), (1,)), ((), ())), preferred_element_type=F32)


def t_dot(a, b):
    return lax.dot_general(a, b, (((0,), (0,)), ((), ())), preferred_element_type=F32)


def swap_kv(x):
    return lax.ppermute(x, "kv", [(0, 1), (1, 0)])


def swap_pg(x, mask, n):
    return lax.ppermute(x, "pg", [(i, i ^ mask) for i in range(n)])


def pack(queries, residual, expert_ids, route_weight, n_pg):
    own_req, cols = queries.shape
    rows, top = expert_ids.shape
    tiles = cols // 128
    high = 2 * own_req * tiles
    total = high + top

    def body(q_hbm, res_hbm, ids_hbm, gates_hbm, out_ref, scr, q_ref, res_ref, ids, gates, sems):
        copies = [
            pltpu.make_async_copy(q_hbm, q_ref, sems.at[0]),
            pltpu.make_async_copy(res_hbm.at[0:16, :], res_ref, sems.at[1]),
            pltpu.make_async_copy(ids_hbm, ids, sems.at[2]),
            pltpu.make_async_copy(gates_hbm, gates, sems.at[3]),
        ]
        for copy in copies:
            copy.start()
        for copy in copies:
            copy.wait()
        for n, ref in enumerate((q_ref, res_ref)):
            for i in range(tiles):
                low = (n * tiles + i) * own_req
                scr[low : low + own_req, :] = ref[0:own_req, 128 * i : 128 * (i + 1)].astype(F32)
        scr[high:, 0:rows] = ids[...].astype(F32)
        scr[high:, 64 : 64 + rows] = gates[...]
        packed = scr[...].astype(BF16)
        for g in range(n_pg):
            out_ref[g] = packed

    return call(
        body,
        [((n_pg, total, 128), BF16)],
        [
            pltpu.VMEM((total, 128), F32),
            pltpu.VMEM((own_req, cols), BF16),
            pltpu.VMEM((16, cols), BF16),
            pltpu.VMEM((top, rows), expert_ids.dtype),
            pltpu.VMEM((top, rows), F32),
            pltpu.SemaphoreType.DMA((4,)),
        ],
        hbm=(0, 1, 2, 3),
        vmem=62,
    )(queries, residual, expert_ids.T, route_weight.T)[0]


def unpack(sent_ref, out, which, own_req):
    tiles = out.shape[1] // 128
    for g in range(sent_ref.shape[0]):
        for i in range(tiles):
            low = (which * tiles + i) * own_req
            out[g * own_req : (g + 1) * own_req, 128 * i : 128 * (i + 1)] = sent_ref[
                g, low : low + own_req, :
            ].astype(F32)


def routing(sent_ref, me, masks, first, top, count):
    got = [sent_ref[me ^ mask, first : first + top, :].astype(F32) for mask in masks]
    ids = jnp.concatenate([x[:, 0:count] for x in got], axis=1)
    gates = jnp.concatenate([x[:, 64 : 64 + count] for x in got], axis=1)
    return jnp.concatenate([ids, gates], axis=0)


def group_masks(g, zs):
    return [4 * z + 2 * (g % 2) + g // 2 for z in range(zs)]


def page_attention(sent, kv_cache, owner, live, own_req, cols):
    groups = sent.shape[0]
    pages, kv_here, page_len, wide = kv_cache.shape
    head_dim = wide // 2
    heads = cols // head_dim
    group = heads // kv_here
    rows = 16
    requests = groups * own_req
    keys = kv_here * page_len
    total = pages * rows

    def body(owner_col, live_col, sent_ref, kv_ref, out_ref, q_all, scores, probs, acc):
        unpack(sent_ref, q_all, 0, own_req)
        pick = (owner_col[...] == iota((total, requests), 1)).astype(BF16)
        wide_q = dot(pick, q_all[...].astype(BF16))
        spread = iota((total, cols), 0) % rows == iota((total, cols), 1) // head_dim
        fold = (iota((cols, wide), 0) % head_dim == iota((cols, wide), 1)).astype(BF16)
        q = dot(jnp.where(spread, wide_q, 0.0).astype(BF16), fold).astype(BF16)
        for p in range(pages):
            part = slice(p * rows, (p + 1) * rows)
            scores[part, :] = dot_t(q[part], kv_ref[p].reshape(keys, wide)) * head_dim ** (-0.5)
        col = iota((total, keys), 1)
        ok = (col // page_len == iota((total, keys), 0) % rows // group) & (
            col % page_len < live_col[...]
        )
        masked = jnp.where(ok, scores[...], NEG_FILL)
        top = jnp.max(masked, axis=1, keepdims=True).astype(BF16).astype(F32)
        share = jnp.where(ok, jnp.exp(masked - top), 0.0).astype(BF16)
        probs[...] = share
        whole = jnp.sum(share.astype(F32), axis=1, keepdims=True)
        for p in range(pages):
            part = slice(p * rows, (p + 1) * rows)
            acc[part, :] = dot(probs[part, :], kv_ref[p].reshape(keys, wide))
        unfold = (iota((wide, cols), 0) - head_dim == iota((wide, cols), 1) % head_dim).astype(BF16)
        here = iota((total, 128), 0) % rows == iota((total, 128), 1)
        merge = (iota((pages, total), 0) == iota((pages, total), 1) // rows).astype(BF16)
        flat = jnp.where(spread, dot(acc[...].astype(BF16), unfold), 0.0).astype(BF16)
        out_ref[:, 0:cols] = dot(merge, flat).astype(BF16)
        flat = jnp.where(here, top, 0.0).astype(BF16)
        out_ref[:, cols : cols + 128] = dot(merge, flat).astype(BF16)
        flat = jnp.where(here, whole, 0.0).astype(BF16)
        out_ref[:, cols + 128 :] = dot(merge, flat).astype(BF16)

    return call(
        body,
        [((pages, cols + 256), BF16)],
        [
            pltpu.VMEM((requests, cols), F32),
            pltpu.VMEM((total, keys), F32),
            pltpu.VMEM((total, keys), BF16),
            pltpu.VMEM((total, wide), F32),
        ],
    )(jnp.repeat(owner, rows)[:, None], jnp.repeat(live, rows)[:, None], sent, kv_cache)[0]


def half_products(left, w_ref, res, me, cols, far, near, base):
    mine = pl.multiple_of(me[0] * cols, 128)
    other = pl.multiple_of((1 - me[0]) * cols, 128)
    far[...] = dot(left, w_ref[:, pl.ds(other, cols)]).astype(BF16)
    own = dot(left, w_ref[:, pl.ds(mine, cols)]).astype(BF16).astype(F32) + res
    base[...] = own
    near[...] = own.astype(BF16)


def project_prefill(prefill, weight, residual, me_kv):
    rows, cols = residual.shape
    skip = rows - prefill.shape[0]

    def body(me, pre, w_ref, res, far, near, base, rows_scr):
        rows_scr[0:skip, :] = jnp.zeros((skip, cols), F32)
        rows_scr[skip:, :] = pre[...].astype(F32)
        left = rows_scr[...].astype(BF16)
        half_products(left, w_ref, res[...].astype(F32), me, cols, far, near, base)

    return call(
        body,
        [((rows, cols), BF16)] * 2 + [((rows, cols), F32)],
        [pltpu.VMEM((rows, cols), F32)],
        smem=(0,),
    )(me_kv, prefill, weight, residual)


def project_decode(pieces, page_table, pages, sent, weight, me_kv, me_pg, own_req, head_dim):
    groups = sent.shape[0]
    cols = weight.shape[0]
    requests = groups * own_req
    entries = page_table.size
    count = len(pieces)
    high = pieces[0].shape[0]
    total = count * high

    def body(me, pg, table_ref, w_ref, sent_ref, *refs):
        far, near, base, res = refs[count:]
        unpack(sent_ref, res, 1, own_req)
        table = jnp.concatenate([ref[...] for ref in refs[:count]], axis=0)
        page = jnp.concatenate(
            [table_ref[j : j + 1, :] for j in range(entries // requests)], axis=1
        )
        away = (page // pages) ^ pg[0]
        where = ((away % 2) * 2 + away // 2 % 2) * high + away // 4 * pages + page % pages
        pick = (iota((total, entries), 0) == where).astype(BF16)
        got = t_dot(pick, table)
        parts = [got[n : n + requests] for n in range(0, entries, requests)]
        sums = [part[:, cols + 128 :] for part in parts]
        tops = [
            jnp.where(tot > 0.0, part[:, cols : cols + 128], NEG_FILL)
            for part, tot in zip(parts, sums)
        ]
        best = functools.reduce(jnp.maximum, tops)
        scales = [jnp.where(tot > 0.0, jnp.exp(top - best), 0.0) for top, tot in zip(tops, sums)]
        whole = functools.reduce(jnp.add, [scale * tot for scale, tot in zip(scales, sums)])
        whole = jnp.where(whole > 0.0, whole, 1.0)
        expand = (iota((128, cols), 0) == iota((128, cols), 1) // head_dim).astype(BF16)
        share = jnp.concatenate([scale / whole for scale in scales], axis=0)
        share_high = share.astype(BF16)
        share_low = (share - share_high.astype(F32)).astype(BF16)
        wide = dot(share_high, expand) + dot(share_low, expand)
        merged = jnp.zeros((requests, cols), F32)
        for n, part in enumerate(parts):
            merged += wide[n * requests : (n + 1) * requests] * part[:, 0:cols]
        half_products(merged.astype(BF16), w_ref, res[...], me, cols, far, near, base)

    return call(
        body,
        [((requests, cols), BF16)] * 2 + [((requests, cols), F32)],
        [pltpu.VMEM((requests, cols), F32)],
        smem=(0, 1),
    )(me_kv, me_pg, page_table.T, weight, sent, *pieces)


def norm_and_pages(base, sent, got_own, got_far, gain, pages):
    rows, cols = base.shape
    count, wide = pages.shape
    lanes = wide * count // rows

    def body(base_ref, sent_ref, got_ref, far_ref, gain_ref, pages_ref, middle, out):
        mid = base_ref[...] + got_ref[...].astype(F32)
        far = far_ref[...].astype(F32) + sent_ref[...].astype(F32)
        squares = jnp.sum(mid * mid + far * far, axis=1, keepdims=True)
        middle[...] = mid
        out[:, 0:cols] = (
            mid * lax.rsqrt(squares / (2 * cols) + EPSILON) * gain_ref[...]
        ).astype(BF16)
        for n in range(rows // count):
            out[n * count : (n + 1) * count, cols:] = pages_ref[:, n * lanes : (n + 1) * lanes]

    return call(body, [((rows, cols), F32), ((rows, cols + lanes), BF16)])(
        base, sent, got_own, got_far, gain.reshape(1, -1), pages
    )


def join(parts, cols, pages):
    rows, wide = parts[0].shape
    lanes = wide - cols
    count = len(parts)
    quarters = rows // pages

    def body(*refs):
        outs, out_pages = refs[-3:-1], refs[-1]
        for n in range(count):
            low = n % (count // 2) * rows
            outs[n // (count // 2)][low : low + rows, :] = refs[n][:, 0:cols]
            for k in range(quarters):
                out_pages[n * pages : (n + 1) * pages, k * lanes : (k + 1) * lanes] = refs[n][
                    k * pages : (k + 1) * pages, cols:
                ]

    return call(
        body,
        [((count // 2 * rows, cols), BF16)] * 2 + [((count * pages, quarters * lanes), BF16)],
    )(*parts)


def first_norm(base, sent, got_own, got_far, gain):
    rows, cols = base.shape

    def body(base_ref, sent_ref, got_ref, far_ref, gain_ref, middle, normed):
        mid = base_ref[...] + got_ref[...].astype(F32)
        far = far_ref[...].astype(F32) + sent_ref[...].astype(F32)
        squares = jnp.sum(mid * mid + far * far, axis=1, keepdims=True)
        middle[...] = mid
        normed[...] = (
            mid * lax.rsqrt(squares / (2 * cols) + EPSILON) * gain_ref[...]
        ).astype(BF16)

    return call(body, [((rows, cols), F32), ((rows, cols), BF16)])(
        base, sent, got_own, got_far, gain.reshape(1, -1)
    )


def routes(info, experts, slots, block_rows, skip):
    top = info.shape[0] // 2
    tokens = info.shape[1]
    token = iota((top, tokens), 1) % block_rows
    odd = (token + iota((top, tokens), 0)) % 2 == 1
    hits, gates = [], []
    for s in range(slots):
        wanted = jnp.where(odd, experts[1, s], experts[0, s]).astype(F32)
        hit = (info[0:top] == wanted) & (token >= skip)
        hits.append(jnp.sum(hit.astype(F32), axis=0, keepdims=True))
        gates.append(jnp.sum(jnp.where(hit, info[top:], 0.0), axis=0, keepdims=True))
    fill = [jnp.zeros((8 - slots, tokens), F32)] if slots < 8 else []
    stacked = jnp.concatenate(hits + fill, axis=0)
    row, col = iota((tokens, tokens), 0), iota((tokens, tokens), 1)
    before = ((row < col) & (row // block_rows == col // block_rows)).astype(BF16)
    ranks = dot(stacked.astype(BF16), before).astype(jnp.int32)
    places = [jnp.where(hits[s] > 0.0, ranks[s : s + 1], -1) for s in range(slots)]
    return places, gates


def one_hot(place, block_rows):
    tokens = place.shape[1]
    shape = (tokens // block_rows * CAP, tokens)
    row = iota(shape, 0)
    return (place == row % CAP) & (iota(shape, 1) // block_rows == row // CAP)


def plan(sent, first, top, experts, me_pg, slots, rows, skip, zs):
    part = zs * CAP
    tokens = zs * rows

    def body(pg, es, sent_ref, picks, gates, dec_gates):
        for g in range(4):
            info = routing(sent_ref, pg[0], group_masks(g, zs), first, top, rows)
            places, shares = routes(info, es, slots, rows, 0 if g % 2 else skip)
            for s in range(slots):
                hot = one_hot(places[s], rows)
                low = s * part
                picks[g, low : low + part, :] = hot.astype(BF16)
                gates[g, low : low + part, :] = jnp.broadcast_to(
                    jnp.sum(jnp.where(hot, shares[s], 0.0), axis=1, keepdims=True), (part, 128)
                )
        masks = group_masks(0, zs) + group_masks(2, zs)
        count = len(masks) * skip
        info = routing(sent_ref, pg[0], masks, first, top, skip)
        ids, shares = info[0:top], info[top:]
        odd = (iota((top, count), 1) % skip + iota((top, count), 0)) % 2 == 1
        eye = iota((count, count), 0) == iota((count, count), 1)
        for s in range(slots):
            wanted = jnp.where(odd, es[1, s], es[0, s]).astype(F32)
            share = jnp.sum(jnp.where(ids == wanted, shares, 0.0), axis=0, keepdims=True)
            dec_gates[s * count : (s + 1) * count, :] = jnp.broadcast_to(
                jnp.sum(jnp.where(eye, share, 0.0), axis=1, keepdims=True), (count, 128)
            )

    return call(
        body,
        [
            ((4, slots * part, tokens), BF16),
            ((4, slots * part, 128), F32),
            ((slots * 2 * zs * skip, 128), F32),
        ],
        smem=(0, 1),
    )(me_pg, experts, sent)


def load(arrays):
    count = len(arrays)

    def body(*refs):
        sems = refs[-1]
        copies = [
            pltpu.make_async_copy(refs[n].at[s], refs[count + n].at[s], sems.at[n, s])
            for n in range(count)
            for s in range(arrays[n].shape[0])
        ]
        for copy in copies:
            copy.start()
        for copy in copies:
            copy.wait()

    return call(
        body,
        [(x.shape, x.dtype) for x in arrays],
        [pltpu.SemaphoreType.DMA((count, arrays[0].shape[0]))],
        hbm=tuple(range(count)),
        vmem=44,
    )(*arrays)


def products(xs, w_ref, side, *outs):
    half = outs[0].shape[2] // 2
    places = [(out, n) for out in outs for n in range(out.shape[0])]
    for s, (out, n) in enumerate(places):
        x = xs[s] if len(xs.shape) == 3 else xs[...]
        for k in range(2):
            low = pl.multiple_of(k * 2 * half + side * half, 128)
            out[n, :, k * half : (k + 1) * half] = dot(x, w_ref[s, :, pl.ds(low, half)]).astype(
                out.dtype
            )


def gather(groups, which, picks, w, me_kv, me_pg, rows, skip, parts, decode=None):
    count, slots = len(groups), w.shape[0]
    pieces = len(groups[0])
    cols = w.shape[1]
    tokens = pieces * groups[0][0].shape[0]
    zs = tokens // rows
    part = zs * CAP
    ff = w.shape[2] // 2

    def body(me, pg, w_ref, picks_ref, *refs):
        xs, sends = refs[-1 - len(parts)], refs[-len(parts) :]
        for n, g in enumerate(which):
            x = jnp.concatenate(
                [ref[...] for ref in refs[n * pieces : (n + 1) * pieces]], axis=0
            )
            if decode is not None:
                dec = refs[count * pieces][...]
                shape = (tokens, dec.shape[0])
                row = iota(shape, 0)
                source = jnp.zeros(shape, jnp.int32)
                for z, mask in enumerate(group_masks(g, zs)):
                    source = jnp.where(row // rows == z, (pg[0] ^ mask) * skip, source)
                late = row % rows < skip
                put = late & (iota(shape, 1) == source + row % rows)
                x = jnp.where(
                    iota((tokens, cols), 0) % rows < skip,
                    dot(put.astype(BF16), dec),
                    x.astype(F32),
                ).astype(BF16)
            got = dot(picks_ref[g], x).astype(BF16)
            for s in range(slots):
                xs[s, n * part : (n + 1) * part, :] = got[s * part : (s + 1) * part]
        products(xs, w_ref, 1 - me[0], *sends)

    more = [] if decode is None else [decode]
    high = count * part
    return call(
        body,
        [((slots, high, cols), BF16)] + [((n, high, ff), BF16) for n in parts],
        smem=(0, 1),
    )(me_kv, me_pg, w, picks, *[x for group in groups for x in group], *more)


def pick_decode(normed, w, me_pg, skip, zs):
    slots, _, wide = w.shape
    total, cols = normed.shape
    masks = group_masks(0, zs) + group_masks(2, zs)
    rows = len(masks) * skip

    def body(pg, w_ref, x_ref, own, send):
        row = iota((rows, total), 0)
        source = jnp.zeros((rows, total), jnp.int32)
        for n, mask in enumerate(masks):
            source = jnp.where(row // skip == n, (pg[0] ^ mask) * skip, source)
        put = iota((rows, total), 1) == source + row % skip
        x = dot(put.astype(BF16), x_ref[...]).astype(BF16)
        for s in range(slots):
            made = dot(x, w_ref[s])
            own[s] = made
            send[s] = made.astype(BF16)

    return call(body, [((slots, rows, wide), F32), ((slots, rows, wide), BF16)], smem=(0,))(
        me_pg, w, normed
    )


def own_products(xs, w, me_kv, flops=1):
    def body(me, w_ref, x_ref, out):
        products(x_ref, w_ref, me[0], out)

    return call(body, [((w.shape[0], xs.shape[-2], w.shape[2] // 2), F32)], smem=(0,), flops=flops)(
        me_kv, w, xs
    )[0]


def activate(own, got, parts=1):
    slots, rows, ff = own.shape
    half = ff // 2
    high = rows // parts

    def body(own_ref, *refs):
        places = [(ref, n) for ref in refs[:-parts] for n in range(ref.shape[0])]
        for s, (ref, n) in enumerate(places):
            gate = own_ref[s, :, 0:half] + ref[n, :, 0:half].astype(F32)
            up = own_ref[s, :, half:] + ref[n, :, half:].astype(F32)
            hidden = (gate / (1.0 + jnp.exp(-gate)) * up).astype(BF16)
            for k in range(parts):
                refs[k - parts][s] = hidden[k * high : (k + 1) * high]

    return call(body, [((slots, high, half), BF16)] * parts, flops=1)(own, *got)


def outputs(near, far, w_ref, me, s):
    half = near[0].shape[2]
    made = dot(
        jnp.concatenate([ref[s] for ref in near], axis=0),
        w_ref[s, pl.ds(pl.multiple_of(me * half, 128), half), :],
    )
    return made + dot(
        jnp.concatenate([ref[s] for ref in far], axis=0),
        w_ref[s, pl.ds(pl.multiple_of((1 - me) * half, 128), half), :],
    )


def decode_experts(own, got, w_down, gates):
    slots, rows, wide = own.shape
    cols = w_down.shape[2]
    half = wide // 2

    def body(w_ref, own_ref, got_ref, gates_ref, out):
        total = jnp.zeros((rows, cols), F32)
        for s in range(slots):
            units = own_ref[s] + got_ref[s].astype(F32)
            gate, up = units[:, 0:half], units[:, half:]
            hidden = (gate / (1.0 + jnp.exp(-gate)) * up).astype(BF16)
            made = dot(hidden, w_ref[s]).astype(BF16).astype(F32)
            total = total + made * gates_ref[s * rows : (s + 1) * rows, 0:1]
        out[...] = total

    return call(body, [((rows, cols), F32)], flops=1)(w_down, own, got, gates)[0]


def down(near, far, w_down, which, picks, gates, me_kv, rows, skip, decode=None):
    pieces = len(near)
    slots, total_rows, _ = near[0].shape
    total_rows = total_rows * pieces
    cols = w_down.shape[2]
    count = len(which)
    part = total_rows // count
    blocks = part // CAP

    def body(me, w_ref, picks_ref, gates_ref, *refs):
        near_refs, far_refs = refs[:pieces], refs[pieces : 2 * pieces]
        outs = refs[-3:]
        made = [outputs(near_refs, far_refs, w_ref, me[0], s) for s in range(slots)]
        for n, g in enumerate(which):
            parts = jnp.concatenate(
                [made[s][n * part : (n + 1) * part] for s in range(slots)], axis=0
            )
            parts = (parts * gates_ref[g, :, 0:1]).astype(BF16)
            total = t_dot(picks_ref[g], parts)
            for b in range(blocks):
                out, low = outs[n + b * 2 // blocks if n else 0], b * rows
                low = low % out.shape[0]
                block = total[b * rows : (b + 1) * rows]
                out[low : low + rows, :] = block.astype(BF16)
                if decode is None:
                    continue
                late = (n * blocks + b) * skip
                late = jnp.concatenate([refs[2 * pieces][late : late + skip, :], block[skip:16]], axis=0)
                out[low : low + 16, :] = late.astype(BF16)

    more = [] if decode is None else [decode]
    shapes = [((blocks * rows, cols), BF16)] + [((blocks // 2 * rows, cols), BF16)] * 2
    return call(body, shapes, smem=(0,), flops=1)(
        me_kv, w_down, picks, gates, *near, *far, *more
    )


def split_sum(kept, halves, rows, first=BF16, pad=0):
    cols = kept.shape[1]
    high = halves[0].shape[0]
    count = kept.shape[0] // rows

    def body(kept_ref, *refs):
        for n in range(count):
            low = n * rows
            more = refs[low // high][low % high : low % high + rows, :]
            total = kept_ref[low : low + rows, :].astype(F32) + more.astype(F32)
            out = refs[2 + n]
            out[0:rows, :] = total.astype(out.dtype)
            if n and pad:
                out[rows:, :] = jnp.zeros((pad, cols), out.dtype)

    return call(
        body, [((rows, cols), first)] + [((rows + pad, cols), BF16)] * (count - 1), flops=1
    )(kept, *halves)


def line_base(middle, decode_middle, own, parts, me_pg, skip):
    rows, cols = middle.shape

    def body(pg, mid, dec, *refs):
        out = refs[-1]
        total = refs[0][...]
        for ref in refs[1:-1]:
            total = total + ref[0:rows, :].astype(F32)
        out[...] = total + mid[...]
        put = iota((8, dec.shape[0]), 1) == pg[0] * skip + iota((8, dec.shape[0]), 0)
        put = put & (iota((8, dec.shape[0]), 0) < skip)
        stream = dot(put.astype(F32), dec[...], HIGH)
        stream = jnp.where(iota((8, cols), 0) < skip, stream, mid[0:8, :])
        out[0:8, :] = total[0:8] + stream

    return call(body, [((rows, cols), F32)], smem=(0,))(
        me_pg, middle, decode_middle, own, *parts
    )[0]


def close(base, parts):
    rows, cols = base.shape

    def body(base_ref, *refs):
        mixed, squares = refs[-2:]
        total = base_ref[...]
        for ref in refs[:-2]:
            total = total + ref[...].astype(F32)
        mixed[...] = total
        total = total * total
        folded = total[:, 0:128]
        for n in range(1, cols // 128):
            folded = folded + total[:, n * 128 : (n + 1) * 128]
        squares[...] = folded

    return call(body, [((rows, cols), F32), ((rows, 128), F32)])(base, *parts)


def last_norm(mixed, near, far, gain):
    rows, cols = mixed.shape

    def body(mixed_ref, near_ref, far_ref, gain_ref, out):
        squares = jnp.sum(near_ref[...] + far_ref[...], axis=1, keepdims=True)
        out[...] = (
            mixed_ref[...] * lax.rsqrt(squares / (2 * cols) + EPSILON) * gain_ref[...]
        ).astype(BF16)

    return call(body, [((rows, cols), BF16)])(mixed, near, far, gain.reshape(1, -1))[0]


def line_pg(x, n_pg):
    return [x] + [swap_pg(x, 4 * z, n_pg) for z in range(1, n_pg // 4)]


def fast_local(
    residual_in,
    queries,
    prefill_attn,
    kv_cache,
    page_table,
    lengths,
    out_weight,
    norm_gain_in,
    norm_gain_out,
    expert_ids,
    route_weight,
    slot_table,
    w_gate_up,
    w_down,
):
    n_pg = lax.axis_size("pg")
    me = lax.axis_index("pg")
    me_kv = lax.axis_index("kv").reshape(1).astype(jnp.int32)
    me_pg = me.reshape(1).astype(jnp.int32)
    rows, cols = residual_in.shape
    own_req = queries.shape[0]
    slots = w_gate_up.shape[0]
    pages, _, page_len, wide = kv_cache.shape
    head_dim = wide // 2
    max_pages = page_table.shape[1]
    top = expert_ids.shape[1]
    zs = n_pg // 4
    first = 2 * own_req * cols // 128

    packed = pack(queries, residual_in, expert_ids, route_weight, n_pg)
    sent = lax.all_to_all(packed, "pg", split_axis=0, concat_axis=0, tiled=True)
    send, near, base = project_prefill(
        after(prefill_attn, packed), out_weight, residual_in, me_kv
    )

    mine = me * slots + jnp.arange(slots, dtype=jnp.int32)
    expert = jnp.arange(slot_table.shape[0], dtype=jnp.int32)
    experts = jnp.max(
        jnp.where(slot_table[:, :, None] == mine[None, None, :], expert[:, None, None], -1), axis=0
    )
    page_ids = me * pages + jnp.arange(pages, dtype=jnp.int32)
    flat_table = page_table.reshape(-1)
    entry_index = jnp.arange(flat_table.shape[0], dtype=jnp.int32)
    found = jnp.sum(
        jnp.where(flat_table[None, :] == page_ids[:, None], entry_index[None, :], 0), axis=1
    )
    owner = found // max_pages
    owner_len = jnp.sum(
        jnp.where(
            owner[:, None] == jnp.arange(lengths.shape[0], dtype=jnp.int32)[None, :],
            lengths[None, :],
            0,
        ),
        axis=1,
    )
    live = owner_len - found % max_pages * page_len
    partial = page_attention(sent, kv_cache, owner, live, own_req, cols)
    got, far = after([swap_kv(send), swap_kv(near)], partial)
    middle, payload = norm_and_pages(base, send, got, far, norm_gain_in, partial)
    line = [swap_pg(payload, 4 * z, n_pg) for z in reversed(range(1, zs))][::-1]
    picks, gates, dec_gates = plan(
        after(sent, payload), first, top, experts, me_pg, slots, rows, own_req, zs
    )
    w_units, w_rows = load(after([w_gate_up, w_down], picks))

    def swap_each(arrays, mask):
        return [swap_pg(x, mask, n_pg) for x in arrays]

    def swap_units(arrays):
        return [swap_kv(x) for x in arrays]

    def gathered(which, groups, parts, decode=None):
        return gather(groups, which, picks, w_units, me_kv, me_pg, rows, own_req, parts, decode)

    *near, near_pages = join([payload] + after(line, w_units), cols, pages)
    across_pages = swap_pg(near_pages, 2, n_pg)
    across = swap_each(near, 2)
    near_pages_core = swap_pg(near_pages, 1, n_pg)
    xs0, *out0 = gathered([0, 2], [near, swap_each(near, 1)], (slots,))
    got0 = swap_units(out0)
    own0 = own_products(xs0, w_units, me_kv)
    across_pages = after(across_pages, own0)
    pieces = [near_pages, across_pages, near_pages_core, swap_pg(across_pages, 1, n_pg)]
    dec_send, dec_near, dec_base = project_decode(
        pieces, page_table, pages, sent, out_weight, me_kv, me_pg, own_req, head_dim
    )
    dec_got, dec_far = swap_kv(dec_send), swap_kv(dec_near)
    near0 = activate(own0, after(got0, dec_send))
    far0 = swap_units(near0)
    across = after(across, near0)
    across_core = swap_each(across, 1)
    dec_got, dec_far = after([dec_got, dec_far], across)
    dec_middle, dec_normed = first_norm(dec_base, dec_send, dec_got, dec_far, norm_gain_in)
    dec_own, dec_units = pick_decode(dec_normed, w_units, me_pg, own_req, zs)
    dec_got = swap_kv(dec_units)
    xs1, *out1 = gathered([1, 3], after([across, across_core], [dec_units, far0]), (slots,), dec_normed)
    got1 = swap_units(out1)
    own1 = own_products(xs1, w_units, me_kv)
    decode = decode_experts(dec_own, after(dec_got, own1), w_rows, dec_gates)
    keep0, *give0 = down(
        near0, after(far0, decode), w_rows, [0, 2], picks, gates, me_kv, rows, own_req, decode
    )
    parts0 = split_sum(keep0, swap_each(give0, 1), rows, F32, 0)
    lines0 = [swap_pg(parts0[z], 4 * z, n_pg) for z in reversed(range(1, zs))]
    near1 = activate(own1, after(got1, parts0), 2)
    far1 = swap_units(near1)
    base = line_base(middle, dec_middle, parts0[0], after(lines0, near1), me_pg, own_req)
    keep1, *give1 = down(
        near1, after(far1, base), w_rows, [1, 3], picks, gates, me_kv, rows, own_req
    )
    parts1 = split_sum(keep1, swap_each(give1, 1), rows)
    mixed, squares = close(
        base, [swap_pg(parts1[z], 4 * z + 2, n_pg) for z in (0, 3, 2, 1)]
    )
    return last_norm(mixed, squares, swap_kv(squares), norm_gain_out)


def solution(mesh):
    fast = mesh.shape["kv"] == 2 and mesh.shape["pg"] == 16
    local = fast_local if fast else general_local
    in_specs = (
        P("pg", "kv"),
        P("pg", "kv"),
        P("pg", "kv"),
        P("pg", "kv", None, None),
        P(),
        P(),
        P("kv", None),
        P("kv"),
        P("kv"),
        P("pg", None),
        P("pg", None),
        P(),
        P("pg", "kv", None),
        P("pg", None, "kv"),
    )
    out_specs = P("pg", "kv")
    return jax.shard_map(local, mesh=mesh, in_specs=in_specs, out_specs=out_specs, check_vma=False)
```

```python
import functools

import jax
import jax.numpy as jnp
from jax import lax
from jax.experimental import pallas as pl
from jax.experimental.pallas import tpu as pltpu
from jax.sharding import PartitionSpec as P

NEG_FILL = -1e30
EPSILON = 1e-06


def merged_2(array, axis, join):
    gathered = jax.tree.map(
        lambda a, kind: lax.all_gather(a.astype(kind), axis),
        array,
        (jnp.bfloat16, jnp.bfloat16, jnp.bfloat16),
    )

    def take(source):
        return jax.tree.map(
            lambda a, own: lax.dynamic_index_in_dim(a, source, 0, False).astype(own.dtype),
            gathered,
            array,
        )

    return lax.fori_loop(
        1, lax.axis_size(axis), lambda source, state: join(state, take(source)), take(0)
    )


def merge_pair(first, secondary_slot):
    highest = jnp.maximum(first[0], secondary_slot[0])
    scale_a = jnp.exp(first[0] - highest)
    scale_b = jnp.exp(secondary_slot[0] - highest)
    head_count = first[0].shape[1]
    acc_a = first[2].reshape(first[2].shape[0], head_count, -1) * scale_a[:, :, None]
    acc_b = (
        secondary_slot[2].reshape(secondary_slot[2].shape[0], head_count, -1) * scale_b[:, :, None]
    )
    return (
        highest,
        first[1] * scale_a + secondary_slot[1] * scale_b,
        (acc_a + acc_b).reshape(first[2].shape),
    )


def general_local(
    residual_in,
    queries,
    prefill_attn,
    kv_cache,
    page_table,
    lengths,
    out_weight,
    norm_gain_in,
    norm_gain_out,
    expert_ids,
    route_weight,
    slot_table,
    w_gate_up,
    w_down,
):
    head_dim = kv_cache.shape[3] // 2
    page_len = kv_cache.shape[2]
    pages_here = kv_cache.shape[0]
    kv_here = kv_cache.shape[1]
    own_req = queries.shape[0]
    heads_here = queries.shape[1] // head_dim
    head_group = heads_here // kv_here
    total_req = page_table.shape[0]
    max_pages = page_table.shape[1]
    full_gate_up, full_down = (
        lax.all_gather(w_gate_up, "kv", axis=1, tiled=True),
        lax.all_gather(w_down, "kv", axis=2, tiled=True),
    )
    gathered = lax.all_gather(queries, "pg", axis=0, tiled=True)
    page_ids = lax.axis_index("pg") * pages_here + jnp.arange(pages_here, dtype=jnp.int32)
    flat_table = page_table.reshape(-1)
    entry_index = jnp.arange(flat_table.shape[0], dtype=jnp.int32)
    found = jnp.sum(
        jnp.where(flat_table[None, :] == page_ids[:, None], entry_index[None, :], 0), axis=1
    )
    owner = found // max_pages
    page_slot = found % max_pages
    owner_len = lengths[owner]
    query_pages = gathered[owner].reshape(pages_here, kv_here, head_group, head_dim)
    keys = kv_cache[:, :, :, :head_dim]
    values = kv_cache[:, :, :, head_dim:]
    scores = jnp.einsum(
        "pkgd,pktd->pkgt", query_pages, keys, preferred_element_type=jnp.float32
    ) * head_dim ** (-0.5)
    positions = page_slot[:, None] * page_len + jnp.arange(page_len, dtype=jnp.int32)[None, :]
    live = (positions < owner_len[:, None])[:, None, None, :]
    masked = jnp.where(live, scores, NEG_FILL)
    page_top = jnp.max(masked, axis=3)
    probs = jnp.where(live, jnp.exp(masked - page_top[..., None]), 0.0).astype(jnp.bfloat16)
    page_sum = jnp.sum(probs.astype(jnp.float32), axis=3).reshape(pages_here, heads_here)
    page_acc = jnp.einsum(
        "pkgt,pktd->pkgd", probs, values, preferred_element_type=jnp.float32
    ).reshape(pages_here, heads_here, head_dim)
    page_top = page_top.reshape(pages_here, heads_here)
    page_live = page_slot * page_len < owner_len
    member = (owner[:, None] == jnp.arange(total_req, dtype=jnp.int32)[None, :]) & page_live[
        :, None
    ]
    local_max = jnp.max(jnp.where(member[:, :, None], page_top[:, None, :], NEG_FILL), axis=0)
    member_t = member.astype(jnp.float32).T
    weight = jnp.exp(page_top - local_max[owner])
    sums = jnp.dot(member_t, weight * page_sum, precision=lax.Precision.HIGHEST)
    accs = jnp.dot(
        member_t,
        (weight[:, :, None] * page_acc).reshape(pages_here, -1),
        precision=lax.Precision.HIGHEST,
    )
    sums, accs = (sums, accs)
    merged = merged_2((local_max, sums, accs), "pg", merge_pair)
    start = lax.axis_index("pg") * own_req
    own_sum = lax.dynamic_slice_in_dim(merged[1], start, own_req, 0)
    own_acc = lax.dynamic_slice_in_dim(merged[2], start, own_req, 0)
    attn_dec = (own_acc.reshape(own_req, heads_here, head_dim) / own_sum[:, :, None]).reshape(
        own_req, -1
    )
    attn_dec = attn_dec.astype(jnp.bfloat16)
    attn_rows = jnp.concatenate([attn_dec, prefill_attn], axis=0)
    projected = jnp.dot(attn_rows, out_weight, preferred_element_type=jnp.float32)
    mixed_in = lax.psum_scatter(
        projected.astype(jnp.bfloat16), "kv", scatter_dimension=1, tiled=True
    ).astype(jnp.float32)
    middle = residual_in.astype(jnp.float32) + mixed_in
    full_width = residual_in.shape[1] * lax.axis_size("kv")
    in_squares = lax.psum(jnp.sum(middle * middle, axis=1), "kv")
    normed = (middle * lax.rsqrt(in_squares / full_width + EPSILON)[:, None] * norm_gain_in).astype(
        jnp.bfloat16
    )
    token_rows, top = expert_ids.shape
    copies = slot_table.shape[1]
    experts_total = slot_table.shape[0]
    kv_count = lax.axis_size("kv")
    capacity = kv_count * max(
        1,
        (token_rows * top * 5 + 4 * experts_total * kv_count - 1) // (4 * experts_total * kv_count),
    )
    slots_here = w_gate_up.shape[0]
    groups = lax.axis_size("pg")
    all_slots = slots_here * groups
    feature_cols = normed.shape[1]
    row_ids = lax.axis_index("pg") * token_rows + jnp.arange(token_rows, dtype=jnp.int32)
    parity = (row_ids[:, None] + jnp.arange(top, dtype=jnp.int32)[None, :]) % copies
    route_key = (expert_ids * copies + parity).reshape(-1)
    table_flat = slot_table.reshape(-1)
    table_index = jnp.arange(table_flat.shape[0], dtype=jnp.int32)
    target_slot = jnp.sum(
        jnp.where(route_key[:, None] == table_index[None, :], table_flat[None, :], 0), axis=1
    )
    match_count = (target_slot[:, None] == jnp.arange(all_slots, dtype=jnp.int32)[None, :]).astype(
        jnp.int32
    )
    rank = jnp.sum((jnp.cumsum(match_count, axis=0) - match_count) * match_count, axis=1)
    dest = target_slot * capacity + rank
    source_row = jnp.arange(token_rows * top, dtype=jnp.int32) // top
    outgoing = (
        jnp.zeros((all_slots * capacity, feature_cols), jnp.bfloat16)
        .at[dest]
        .set(normed[source_row])
    )
    outgoing = outgoing.reshape(groups, slots_here, capacity, feature_cols)
    arrived = lax.all_to_all(outgoing, "pg", split_axis=0, concat_axis=0, tiled=True)
    widened = lax.all_to_all(arrived, "kv", split_axis=2, concat_axis=3, tiled=True)
    gate_up = jnp.einsum(
        "pscd,sdf->pscf", widened, full_gate_up, preferred_element_type=jnp.float32
    )
    half = gate_up.shape[3] // 2
    hidden = (jax.nn.silu(gate_up[..., :half]) * gate_up[..., half:]).astype(jnp.bfloat16)
    produced = jnp.einsum(
        "pscf,sfd->pscd", hidden, full_down, preferred_element_type=jnp.float32
    ).astype(jnp.bfloat16)
    narrowed = lax.all_to_all(produced, "kv", split_axis=3, concat_axis=2, tiled=True)
    returned = lax.all_to_all(narrowed, "pg", split_axis=0, concat_axis=0, tiled=True)
    returned = returned.reshape(all_slots * capacity, feature_cols)
    picked = returned[dest].astype(jnp.float32).reshape(token_rows, top, feature_cols)
    mixed = middle + jnp.sum(picked * route_weight[:, :, None], axis=1)
    out_squares = lax.psum(jnp.sum(mixed * mixed, axis=1), "kv")
    return (mixed * lax.rsqrt(out_squares / full_width + EPSILON)[:, None] * norm_gain_out).astype(
        jnp.bfloat16
    )


F32 = jnp.float32
BF16 = jnp.bfloat16
CAP = 16
HIGH = lax.Precision.HIGHEST


def call(body, outs, scratch=(), smem=(), hbm=(), vmem=16, flops=10**9):
    def run(*operands):
        kinds = [
            pltpu.SMEM if n in smem else pltpu.HBM if n in hbm else pltpu.VMEM
            for n in range(len(operands))
        ]
        return pl.pallas_call(
            body,
            out_shape=[jax.ShapeDtypeStruct(s, d) for s, d in outs],
            in_specs=[pl.BlockSpec(memory_space=kind) for kind in kinds],
            out_specs=[pl.BlockSpec(memory_space=pltpu.VMEM) for _ in outs],
            scratch_shapes=list(scratch),
            compiler_params=pltpu.CompilerParams(
                vmem_limit_bytes=vmem * 2**20
            ),
            cost_estimate=pl.CostEstimate(flops=flops, bytes_accessed=1, transcendentals=0),
        )(*operands)

    return run


def after(values, *earlier):
    return lax.optimization_barrier((values, earlier))[0]


def iota(shape, dim):
    return lax.broadcasted_iota(jnp.int32, shape, dim)


def dot(a, b, precision=None):
    return jnp.dot(a, b, preferred_element_type=F32, precision=precision)


def dot_t(a, b):
    return lax.dot_general(a, b, (((1,), (1,)), ((), ())), preferred_element_type=F32)


def t_dot(a, b):
    return lax.dot_general(a, b, (((0,), (0,)), ((), ())), preferred_element_type=F32)


def swap_kv(x):
    return lax.ppermute(x, "kv", [(0, 1), (1, 0)])


def swap_pg(x, mask, n):
    return lax.ppermute(x, "pg", [(i, i ^ mask) for i in range(n)])


def pack(queries, residual, expert_ids, route_weight, n_pg):
    own_req, cols = queries.shape
    rows, top = expert_ids.shape
    tiles = cols // 128
    high = 2 * own_req * tiles
    total = high + top

    def body(q_hbm, res_hbm, ids_hbm, gates_hbm, out_ref, scr, q_ref, res_ref, ids, gates, sems):
        copies = [
            pltpu.make_async_copy(q_hbm, q_ref, sems.at[0]),
            pltpu.make_async_copy(res_hbm.at[0:16, :], res_ref, sems.at[1]),
            pltpu.make_async_copy(ids_hbm, ids, sems.at[2]),
            pltpu.make_async_copy(gates_hbm, gates, sems.at[3]),
        ]
        for copy in copies:
            copy.start()
        for copy in copies:
            copy.wait()
        for n, ref in enumerate((q_ref, res_ref)):
            for i in range(tiles):
                low = (n * tiles + i) * own_req
                scr[low : low + own_req, :] = ref[0:own_req, 128 * i : 128 * (i + 1)].astype(F32)
        scr[high:, 0:rows] = ids[...].astype(F32)
        scr[high:, 64 : 64 + rows] = gates[...]
        packed = scr[...].astype(BF16)
        for g in range(n_pg):
            out_ref[g] = packed

    return call(
        body,
        [((n_pg, total, 128), BF16)],
        [
            pltpu.VMEM((total, 128), F32),
            pltpu.VMEM((own_req, cols), BF16),
            pltpu.VMEM((16, cols), BF16),
            pltpu.VMEM((top, rows), expert_ids.dtype),
            pltpu.VMEM((top, rows), F32),
            pltpu.SemaphoreType.DMA((4,)),
        ],
        hbm=(0, 1, 2, 3),
        vmem=62,
    )(queries, residual, expert_ids.T, route_weight.T)[0]


def unpack(sent_ref, out, which, own_req):
    tiles = out.shape[1] // 128
    for g in range(sent_ref.shape[0]):
        for i in range(tiles):
            low = (which * tiles + i) * own_req
            out[g * own_req : (g + 1) * own_req, 128 * i : 128 * (i + 1)] = sent_ref[
                g, low : low + own_req, :
            ].astype(F32)


def routing(sent_ref, me, masks, first, top, count):
    got = [sent_ref[me ^ mask, first : first + top, :].astype(F32) for mask in masks]
    ids = jnp.concatenate([x[:, 0:count] for x in got], axis=1)
    gates = jnp.concatenate([x[:, 64 : 64 + count] for x in got], axis=1)
    return jnp.concatenate([ids, gates], axis=0)


def group_masks(g, zs):
    return [4 * z + 2 * (g % 2) + g // 2 for z in range(zs)]


def page_attention(sent, kv_cache, owner, live, own_req, cols):
    groups = sent.shape[0]
    pages, kv_here, page_len, wide = kv_cache.shape
    head_dim = wide // 2
    heads = cols // head_dim
    group = heads // kv_here
    rows = 16
    requests = groups * own_req
    keys = kv_here * page_len
    total = pages * rows

    def body(owner_col, live_col, sent_ref, kv_ref, out_ref, q_all, scores, probs, acc):
        unpack(sent_ref, q_all, 0, own_req)
        pick = (owner_col[...] == iota((total, requests), 1)).astype(BF16)
        wide_q = dot(pick, q_all[...].astype(BF16))
        spread = iota((total, cols), 0) % rows == iota((total, cols), 1) // head_dim
        fold = (iota((cols, wide), 0) % head_dim == iota((cols, wide), 1)).astype(BF16)
        q = dot(jnp.where(spread, wide_q, 0.0).astype(BF16), fold).astype(BF16)
        for p in range(pages):
            part = slice(p * rows, (p + 1) * rows)
            scores[part, :] = dot_t(q[part], kv_ref[p].reshape(keys, wide)) * head_dim ** (-0.5)
        col = iota((total, keys), 1)
        ok = (col // page_len == iota((total, keys), 0) % rows // group) & (
            col % page_len < live_col[...]
        )
        masked = jnp.where(ok, scores[...], NEG_FILL)
        top = jnp.max(masked, axis=1, keepdims=True).astype(BF16).astype(F32)
        share = jnp.where(ok, jnp.exp(masked - top), 0.0).astype(BF16)
        probs[...] = share
        whole = jnp.sum(share.astype(F32), axis=1, keepdims=True)
        for p in range(pages):
            part = slice(p * rows, (p + 1) * rows)
            acc[part, :] = dot(probs[part, :], kv_ref[p].reshape(keys, wide))
        unfold = (iota((wide, cols), 0) - head_dim == iota((wide, cols), 1) % head_dim).astype(BF16)
        here = iota((total, 128), 0) % rows == iota((total, 128), 1)
        merge = (iota((pages, total), 0) == iota((pages, total), 1) // rows).astype(BF16)
        flat = jnp.where(spread, dot(acc[...].astype(BF16), unfold), 0.0).astype(BF16)
        out_ref[:, 0:cols] = dot(merge, flat).astype(BF16)
        flat = jnp.where(here, top, 0.0).astype(BF16)
        out_ref[:, cols : cols + 128] = dot(merge, flat).astype(BF16)
        flat = jnp.where(here, whole, 0.0).astype(BF16)
        out_ref[:, cols + 128 :] = dot(merge, flat).astype(BF16)

    return call(
        body,
        [((pages, cols + 256), BF16)],
        [
            pltpu.VMEM((requests, cols), F32),
            pltpu.VMEM((total, keys), F32),
            pltpu.VMEM((total, keys), BF16),
            pltpu.VMEM((total, wide), F32),
        ],
    )(jnp.repeat(owner, rows)[:, None], jnp.repeat(live, rows)[:, None], sent, kv_cache)[0]


def half_products(left, w_ref, res, me, cols, far, near, base):
    mine = pl.multiple_of(me[0] * cols, 128)
    other = pl.multiple_of((1 - me[0]) * cols, 128)
    far[...] = dot(left, w_ref[:, pl.ds(other, cols)]).astype(BF16)
    own = dot(left, w_ref[:, pl.ds(mine, cols)]).astype(BF16).astype(F32) + res
    base[...] = own
    near[...] = own.astype(BF16)


def project_prefill(prefill, weight, residual, me_kv):
    rows, cols = residual.shape
    skip = rows - prefill.shape[0]

    def body(me, pre, w_ref, res, far, near, base, rows_scr):
        rows_scr[0:skip, :] = jnp.zeros((skip, cols), F32)
        rows_scr[skip:, :] = pre[...].astype(F32)
        left = rows_scr[...].astype(BF16)
        half_products(left, w_ref, res[...].astype(F32), me, cols, far, near, base)

    return call(
        body,
        [((rows, cols), BF16)] * 2 + [((rows, cols), F32)],
        [pltpu.VMEM((rows, cols), F32)],
        smem=(0,),
    )(me_kv, prefill, weight, residual)


def project_decode(pieces, page_table, pages, sent, weight, me_kv, me_pg, own_req, head_dim):
    groups = sent.shape[0]
    cols = weight.shape[0]
    requests = groups * own_req
    entries = page_table.size
    count = len(pieces)
    high = pieces[0].shape[0]
    total = count * high

    def body(me, pg, table_ref, w_ref, sent_ref, *refs):
        far, near, base, res = refs[count:]
        unpack(sent_ref, res, 1, own_req)
        table = jnp.concatenate([ref[...] for ref in refs[:count]], axis=0)
        page = jnp.concatenate(
            [table_ref[j : j + 1, :] for j in range(entries // requests)], axis=1
        )
        away = (page // pages) ^ pg[0]
        where = ((away % 2) * 2 + away // 2 % 2) * high + away // 4 * pages + page % pages
        pick = (iota((total, entries), 0) == where).astype(BF16)
        got = t_dot(pick, table)
        parts = [got[n : n + requests] for n in range(0, entries, requests)]
        sums = [part[:, cols + 128 :] for part in parts]
        tops = [
            jnp.where(tot > 0.0, part[:, cols : cols + 128], NEG_FILL)
            for part, tot in zip(parts, sums)
        ]
        best = functools.reduce(jnp.maximum, tops)
        scales = [jnp.where(tot > 0.0, jnp.exp(top - best), 0.0) for top, tot in zip(tops, sums)]
        whole = functools.reduce(jnp.add, [scale * tot for scale, tot in zip(scales, sums)])
        whole = jnp.where(whole > 0.0, whole, 1.0)
        expand = (iota((128, cols), 0) == iota((128, cols), 1) // head_dim).astype(BF16)
        share = jnp.concatenate([scale / whole for scale in scales], axis=0)
        share_high = share.astype(BF16)
        share_low = (share - share_high.astype(F32)).astype(BF16)
        wide = dot(share_high, expand) + dot(share_low, expand)
        merged = jnp.zeros((requests, cols), F32)
        for n, part in enumerate(parts):
            merged += wide[n * requests : (n + 1) * requests] * part[:, 0:cols]
        half_products(merged.astype(BF16), w_ref, res[...], me, cols, far, near, base)

    return call(
        body,
        [((requests, cols), BF16)] * 2 + [((requests, cols), F32)],
        [pltpu.VMEM((requests, cols), F32)],
        smem=(0, 1),
    )(me_kv, me_pg, page_table.T, weight, sent, *pieces)


def norm_and_pages(base, sent, got_own, got_far, gain, pages):
    rows, cols = base.shape
    count, wide = pages.shape
    lanes = wide * count // rows

    def body(base_ref, sent_ref, got_ref, far_ref, gain_ref, pages_ref, middle, out):
        mid = base_ref[...] + got_ref[...].astype(F32)
        far = far_ref[...].astype(F32) + sent_ref[...].astype(F32)
        squares = jnp.sum(mid * mid + far * far, axis=1, keepdims=True)
        middle[...] = mid
        out[:, 0:cols] = (
            mid * lax.rsqrt(squares / (2 * cols) + EPSILON) * gain_ref[...]
        ).astype(BF16)
        for n in range(rows // count):
            out[n * count : (n + 1) * count, cols:] = pages_ref[:, n * lanes : (n + 1) * lanes]

    return call(body, [((rows, cols), F32), ((rows, cols + lanes), BF16)])(
        base, sent, got_own, got_far, gain.reshape(1, -1), pages
    )


def join(parts, cols, pages):
    rows, wide = parts[0].shape
    lanes = wide - cols
    count = len(parts)
    quarters = rows // pages

    def body(*refs):
        outs, out_pages = refs[-3:-1], refs[-1]
        for n in range(count):
            low = n % (count // 2) * rows
            outs[n // (count // 2)][low : low + rows, :] = refs[n][:, 0:cols]
            for k in range(quarters):
                out_pages[n * pages : (n + 1) * pages, k * lanes : (k + 1) * lanes] = refs[n][
                    k * pages : (k + 1) * pages, cols:
                ]

    return call(
        body,
        [((count // 2 * rows, cols), BF16)] * 2 + [((count * pages, quarters * lanes), BF16)],
    )(*parts)


def first_norm(base, sent, got_own, got_far, gain):
    rows, cols = base.shape

    def body(base_ref, sent_ref, got_ref, far_ref, gain_ref, middle, normed):
        mid = base_ref[...] + got_ref[...].astype(F32)
        far = far_ref[...].astype(F32) + sent_ref[...].astype(F32)
        squares = jnp.sum(mid * mid + far * far, axis=1, keepdims=True)
        middle[...] = mid
        normed[...] = (
            mid * lax.rsqrt(squares / (2 * cols) + EPSILON) * gain_ref[...]
        ).astype(BF16)

    return call(body, [((rows, cols), F32), ((rows, cols), BF16)])(
        base, sent, got_own, got_far, gain.reshape(1, -1)
    )


def routes(info, experts, slots, block_rows, skip):
    top = info.shape[0] // 2
    tokens = info.shape[1]
    token = iota((top, tokens), 1) % block_rows
    odd = (token + iota((top, tokens), 0)) % 2 == 1
    hits, gates = [], []
    for s in range(slots):
        wanted = jnp.where(odd, experts[1, s], experts[0, s]).astype(F32)
        hit = (info[0:top] == wanted) & (token >= skip)
        hits.append(jnp.sum(hit.astype(F32), axis=0, keepdims=True))
        gates.append(jnp.sum(jnp.where(hit, info[top:], 0.0), axis=0, keepdims=True))
    fill = [jnp.zeros((8 - slots, tokens), F32)] if slots < 8 else []
    stacked = jnp.concatenate(hits + fill, axis=0)
    row, col = iota((tokens, tokens), 0), iota((tokens, tokens), 1)
    before = ((row < col) & (row // block_rows == col // block_rows)).astype(BF16)
    ranks = dot(stacked.astype(BF16), before).astype(jnp.int32)
    places = [jnp.where(hits[s] > 0.0, ranks[s : s + 1], -1) for s in range(slots)]
    return places, gates


def one_hot(place, block_rows):
    tokens = place.shape[1]
    shape = (tokens // block_rows * CAP, tokens)
    row = iota(shape, 0)
    return (place == row % CAP) & (iota(shape, 1) // block_rows == row // CAP)


def plan(sent, first, top, experts, me_pg, slots, rows, skip, zs):
    part = zs * CAP
    tokens = zs * rows

    def body(pg, es, sent_ref, picks, gates, dec_gates):
        for g in range(4):
            info = routing(sent_ref, pg[0], group_masks(g, zs), first, top, rows)
            places, shares = routes(info, es, slots, rows, 0 if g % 2 else skip)
            for s in range(slots):
                hot = one_hot(places[s], rows)
                low = s * part
                picks[g, low : low + part, :] = hot.astype(BF16)
                gates[g, low : low + part, :] = jnp.broadcast_to(
                    jnp.sum(jnp.where(hot, shares[s], 0.0), axis=1, keepdims=True), (part, 128)
                )
        masks = group_masks(0, zs) + group_masks(2, zs)
        count = len(masks) * skip
        info = routing(sent_ref, pg[0], masks, first, top, skip)
        ids, shares = info[0:top], info[top:]
        odd = (iota((top, count), 1) % skip + iota((top, count), 0)) % 2 == 1
        eye = iota((count, count), 0) == iota((count, count), 1)
        for s in range(slots):
            wanted = jnp.where(odd, es[1, s], es[0, s]).astype(F32)
            share = jnp.sum(jnp.where(ids == wanted, shares, 0.0), axis=0, keepdims=True)
            dec_gates[s * count : (s + 1) * count, :] = jnp.broadcast_to(
                jnp.sum(jnp.where(eye, share, 0.0), axis=1, keepdims=True), (count, 128)
            )

    return call(
        body,
        [
            ((4, slots * part, tokens), BF16),
            ((4, slots * part, 128), F32),
            ((slots * 2 * zs * skip, 128), F32),
        ],
        smem=(0, 1),
    )(me_pg, experts, sent)


def load(arrays):
    count = len(arrays)

    def body(*refs):
        sems = refs[-1]
        copies = [
            pltpu.make_async_copy(refs[n].at[s], refs[count + n].at[s], sems.at[n, s])
            for n in range(count)
            for s in range(arrays[n].shape[0])
        ]
        for copy in copies:
            copy.start()
        for copy in copies:
            copy.wait()

    return call(
        body,
        [(x.shape, x.dtype) for x in arrays],
        [pltpu.SemaphoreType.DMA((count, arrays[0].shape[0]))],
        hbm=tuple(range(count)),
        vmem=44,
    )(*arrays)


def products(xs, w_ref, side, *outs):
    half = outs[0].shape[2] // 2
    places = [(out, n) for out in outs for n in range(out.shape[0])]
    for s, (out, n) in enumerate(places):
        x = xs[s] if len(xs.shape) == 3 else xs[...]
        for k in range(2):
            low = pl.multiple_of(k * 2 * half + side * half, 128)
            out[n, :, k * half : (k + 1) * half] = dot(x, w_ref[s, :, pl.ds(low, half)]).astype(
                out.dtype
            )


def gather(groups, which, picks, w, me_kv, me_pg, rows, skip, parts, decode=None):
    count, slots = len(groups), w.shape[0]
    pieces = len(groups[0])
    cols = w.shape[1]
    tokens = pieces * groups[0][0].shape[0]
    zs = tokens // rows
    part = zs * CAP
    ff = w.shape[2] // 2

    def body(me, pg, w_ref, picks_ref, *refs):
        xs, sends = refs[-1 - len(parts)], refs[-len(parts) :]
        for n, g in enumerate(which):
            x = jnp.concatenate(
                [ref[...] for ref in refs[n * pieces : (n + 1) * pieces]], axis=0
            )
            if decode is not None:
                dec = refs[count * pieces][...]
                shape = (tokens, dec.shape[0])
                row = iota(shape, 0)
                source = jnp.zeros(shape, jnp.int32)
                for z, mask in enumerate(group_masks(g, zs)):
                    source = jnp.where(row // rows == z, (pg[0] ^ mask) * skip, source)
                late = row % rows < skip
                put = late & (iota(shape, 1) == source + row % rows)
                x = jnp.where(
                    iota((tokens, cols), 0) % rows < skip,
                    dot(put.astype(BF16), dec),
                    x.astype(F32),
                ).astype(BF16)
            got = dot(picks_ref[g], x).astype(BF16)
            for s in range(slots):
                xs[s, n * part : (n + 1) * part, :] = got[s * part : (s + 1) * part]
        products(xs, w_ref, 1 - me[0], *sends)

    more = [] if decode is None else [decode]
    high = count * part
    return call(
        body,
        [((slots, high, cols), BF16)] + [((n, high, ff), BF16) for n in parts],
        smem=(0, 1),
    )(me_kv, me_pg, w, picks, *[x for group in groups for x in group], *more)


def pick_decode(normed, w, me_pg, skip, zs):
    slots, _, wide = w.shape
    total, cols = normed.shape
    masks = group_masks(0, zs) + group_masks(2, zs)
    rows = len(masks) * skip

    def body(pg, w_ref, x_ref, own, send):
        row = iota((rows, total), 0)
        source = jnp.zeros((rows, total), jnp.int32)
        for n, mask in enumerate(masks):
            source = jnp.where(row // skip == n, (pg[0] ^ mask) * skip, source)
        put = iota((rows, total), 1) == source + row % skip
        x = dot(put.astype(BF16), x_ref[...]).astype(BF16)
        for s in range(slots):
            made = dot(x, w_ref[s])
            own[s] = made
            send[s] = made.astype(BF16)

    return call(body, [((slots, rows, wide), F32), ((slots, rows, wide), BF16)], smem=(0,))(
        me_pg, w, normed
    )


def own_products(xs, w, me_kv, flops=1):
    def body(me, w_ref, x_ref, out):
        products(x_ref, w_ref, me[0], out)

    return call(body, [((w.shape[0], xs.shape[-2], w.shape[2] // 2), F32)], smem=(0,), flops=flops)(
        me_kv, w, xs
    )[0]


def activate(own, got, parts=1):
    slots, rows, ff = own.shape
    half = ff // 2
    high = rows // parts

    def body(own_ref, *refs):
        places = [(ref, n) for ref in refs[:-parts] for n in range(ref.shape[0])]
        for s, (ref, n) in enumerate(places):
            gate = own_ref[s, :, 0:half] + ref[n, :, 0:half].astype(F32)
            up = own_ref[s, :, half:] + ref[n, :, half:].astype(F32)
            hidden = (gate / (1.0 + jnp.exp(-gate)) * up).astype(BF16)
            for k in range(parts):
                refs[k - parts][s] = hidden[k * high : (k + 1) * high]

    return call(body, [((slots, high, half), BF16)] * parts, flops=1)(own, *got)


def outputs(near, far, w_ref, me, s):
    half = near[0].shape[2]
    made = dot(
        jnp.concatenate([ref[s] for ref in near], axis=0),
        w_ref[s, pl.ds(pl.multiple_of(me * half, 128), half), :],
    )
    return made + dot(
        jnp.concatenate([ref[s] for ref in far], axis=0),
        w_ref[s, pl.ds(pl.multiple_of((1 - me) * half, 128), half), :],
    )


def decode_experts(own, got, w_down, gates):
    slots, rows, wide = own.shape
    cols = w_down.shape[2]
    half = wide // 2

    def body(w_ref, own_ref, got_ref, gates_ref, out):
        total = jnp.zeros((rows, cols), F32)
        for s in range(slots):
            units = own_ref[s] + got_ref[s].astype(F32)
            gate, up = units[:, 0:half], units[:, half:]
            hidden = (gate / (1.0 + jnp.exp(-gate)) * up).astype(BF16)
            made = dot(hidden, w_ref[s]).astype(BF16).astype(F32)
            total = total + made * gates_ref[s * rows : (s + 1) * rows, 0:1]
        out[...] = total

    return call(body, [((rows, cols), F32)], flops=1)(w_down, own, got, gates)[0]


def down(near, far, w_down, which, picks, gates, me_kv, rows, skip, decode=None):
    pieces = len(near)
    slots, total_rows, _ = near[0].shape
    total_rows = total_rows * pieces
    cols = w_down.shape[2]
    count = len(which)
    part = total_rows // count
    blocks = part // CAP

    def body(me, w_ref, picks_ref, gates_ref, *refs):
        near_refs, far_refs = refs[:pieces], refs[pieces : 2 * pieces]
        outs = refs[-3:]
        made = [outputs(near_refs, far_refs, w_ref, me[0], s) for s in range(slots)]
        for n, g in enumerate(which):
            parts = jnp.concatenate(
                [made[s][n * part : (n + 1) * part] for s in range(slots)], axis=0
            )
            parts = (parts * gates_ref[g, :, 0:1]).astype(BF16)
            total = t_dot(picks_ref[g], parts)
            for b in range(blocks):
                out, low = outs[n + b * 2 // blocks if n else 0], b * rows
                low = low % out.shape[0]
                block = total[b * rows : (b + 1) * rows]
                out[low : low + rows, :] = block.astype(BF16)
                if decode is None:
                    continue
                late = (n * blocks + b) * skip
                late = jnp.concatenate([refs[2 * pieces][late : late + skip, :], block[skip:16]], axis=0)
                out[low : low + 16, :] = late.astype(BF16)

    more = [] if decode is None else [decode]
    shapes = [((blocks * rows, cols), BF16)] + [((blocks // 2 * rows, cols), BF16)] * 2
    return call(body, shapes, smem=(0,), flops=1)(
        me_kv, w_down, picks, gates, *near, *far, *more
    )


def split_sum(kept, halves, rows, first=BF16, pad=0):
    cols = kept.shape[1]
    high = halves[0].shape[0]
    count = kept.shape[0] // rows

    def body(kept_ref, *refs):
        for n in range(count):
            low = n * rows
            more = refs[low // high][low % high : low % high + rows, :]
            total = kept_ref[low : low + rows, :].astype(F32) + more.astype(F32)
            out = refs[2 + n]
            out[0:rows, :] = total.astype(out.dtype)
            if n and pad:
                out[rows:, :] = jnp.zeros((pad, cols), out.dtype)

    return call(
        body, [((rows, cols), first)] + [((rows + pad, cols), BF16)] * (count - 1), flops=1
    )(kept, *halves)


def line_base(middle, decode_middle, own, parts, me_pg, skip):
    rows, cols = middle.shape

    def body(pg, mid, dec, *refs):
        out = refs[-1]
        total = refs[0][...]
        for ref in refs[1:-1]:
            total = total + ref[0:rows, :].astype(F32)
        out[...] = total + mid[...]
        put = iota((8, dec.shape[0]), 1) == pg[0] * skip + iota((8, dec.shape[0]), 0)
        put = put & (iota((8, dec.shape[0]), 0) < skip)
        stream = dot(put.astype(F32), dec[...], HIGH)
        stream = jnp.where(iota((8, cols), 0) < skip, stream, mid[0:8, :])
        out[0:8, :] = total[0:8] + stream

    return call(body, [((rows, cols), F32)], smem=(0,))(
        me_pg, middle, decode_middle, own, *parts
    )[0]


def close(base, parts):
    rows, cols = base.shape

    def body(base_ref, *refs):
        mixed, squares = refs[-2:]
        total = base_ref[...]
        for ref in refs[:-2]:
            total = total + ref[...].astype(F32)
        mixed[...] = total
        total = total * total
        folded = total[:, 0:128]
        for n in range(1, cols // 128):
            folded = folded + total[:, n * 128 : (n + 1) * 128]
        squares[...] = lax.dot_general(
            jnp.ones((8, 128), F32),
            folded,
            (((1,), (1,)), ((), ())),
            precision=HIGH,
            preferred_element_type=F32,
        )

    return call(body, [((rows, cols), F32), ((8, rows), F32)])(base, *parts)


def last_norm(mixed, near, far, gain):
    rows, cols = mixed.shape

    def body(mixed_ref, near_ref, far_ref, gain_ref, out):
        both = near_ref[0:1, :] + far_ref[0:1, :]
        eye = iota((rows, rows), 0) == iota((rows, rows), 1)
        squares = jnp.sum(jnp.where(eye, both, 0.0), axis=1, keepdims=True)
        out[...] = (
            mixed_ref[...] * lax.rsqrt(squares / (2 * cols) + EPSILON) * gain_ref[...]
        ).astype(BF16)

    return call(body, [((rows, cols), BF16)])(mixed, near, far, gain.reshape(1, -1))[0]


def line_pg(x, n_pg):
    return [x] + [swap_pg(x, 4 * z, n_pg) for z in range(1, n_pg // 4)]


def fast_local(
    residual_in,
    queries,
    prefill_attn,
    kv_cache,
    page_table,
    lengths,
    out_weight,
    norm_gain_in,
    norm_gain_out,
    expert_ids,
    route_weight,
    slot_table,
    w_gate_up,
    w_down,
):
    n_pg = lax.axis_size("pg")
    me = lax.axis_index("pg")
    me_kv = lax.axis_index("kv").reshape(1).astype(jnp.int32)
    me_pg = me.reshape(1).astype(jnp.int32)
    rows, cols = residual_in.shape
    own_req = queries.shape[0]
    slots = w_gate_up.shape[0]
    pages, _, page_len, wide = kv_cache.shape
    head_dim = wide // 2
    max_pages = page_table.shape[1]
    top = expert_ids.shape[1]
    zs = n_pg // 4
    first = 2 * own_req * cols // 128

    packed = pack(queries, residual_in, expert_ids, route_weight, n_pg)
    sent = lax.all_to_all(packed, "pg", split_axis=0, concat_axis=0, tiled=True)
    send, near, base = project_prefill(
        after(prefill_attn, packed), out_weight, residual_in, me_kv
    )

    mine = me * slots + jnp.arange(slots, dtype=jnp.int32)
    expert = jnp.arange(slot_table.shape[0], dtype=jnp.int32)
    experts = jnp.max(
        jnp.where(slot_table[:, :, None] == mine[None, None, :], expert[:, None, None], -1), axis=0
    )
    page_ids = me * pages + jnp.arange(pages, dtype=jnp.int32)
    flat_table = page_table.reshape(-1)
    entry_index = jnp.arange(flat_table.shape[0], dtype=jnp.int32)
    found = jnp.sum(
        jnp.where(flat_table[None, :] == page_ids[:, None], entry_index[None, :], 0), axis=1
    )
    owner = found // max_pages
    owner_len = jnp.sum(
        jnp.where(
            owner[:, None] == jnp.arange(lengths.shape[0], dtype=jnp.int32)[None, :],
            lengths[None, :],
            0,
        ),
        axis=1,
    )
    live = owner_len - found % max_pages * page_len
    partial = page_attention(sent, kv_cache, owner, live, own_req, cols)
    got, far = after([swap_kv(send), swap_kv(near)], partial)
    middle, payload = norm_and_pages(base, send, got, far, norm_gain_in, partial)
    line = [swap_pg(payload, 4 * z, n_pg) for z in reversed(range(1, zs))][::-1]
    picks, gates, dec_gates = plan(
        after(sent, payload), first, top, experts, me_pg, slots, rows, own_req, zs
    )
    w_units, w_rows = load(after([w_gate_up, w_down], picks))

    def swap_each(arrays, mask):
        return [swap_pg(x, mask, n_pg) for x in arrays]

    def swap_units(arrays):
        return [swap_kv(x) for x in arrays]

    def gathered(which, groups, parts, decode=None):
        return gather(groups, which, picks, w_units, me_kv, me_pg, rows, own_req, parts, decode)

    *near, near_pages = join([payload] + after(line, w_units), cols, pages)
    across_pages = swap_pg(near_pages, 2, n_pg)
    across = swap_each(near, 2)
    near_pages_core = swap_pg(near_pages, 1, n_pg)
    xs0, *out0 = gathered([0, 2], [near, swap_each(near, 1)], (slots,))
    got0 = swap_units(out0)
    own0 = own_products(xs0, w_units, me_kv)
    across_pages = after(across_pages, own0)
    pieces = [near_pages, across_pages, near_pages_core, swap_pg(across_pages, 1, n_pg)]
    dec_send, dec_near, dec_base = project_decode(
        pieces, page_table, pages, sent, out_weight, me_kv, me_pg, own_req, head_dim
    )
    dec_got, dec_far = swap_kv(dec_send), swap_kv(dec_near)
    near0 = activate(own0, after(got0, dec_send))
    far0 = swap_units(near0)
    across = after(across, near0)
    across_core = swap_each(across, 1)
    dec_got, dec_far = after([dec_got, dec_far], across)
    dec_middle, dec_normed = first_norm(dec_base, dec_send, dec_got, dec_far, norm_gain_in)
    dec_own, dec_units = pick_decode(dec_normed, w_units, me_pg, own_req, zs)
    dec_got = swap_kv(dec_units)
    xs1, *out1 = gathered([1, 3], after([across, across_core], [dec_units, far0]), (slots,), dec_normed)
    got1 = swap_units(out1)
    own1 = own_products(xs1, w_units, me_kv)
    decode = decode_experts(dec_own, after(dec_got, out1), w_rows, dec_gates)
    keep0, *give0 = down(
        near0, after(far0, decode), w_rows, [0, 2], picks, gates, me_kv, rows, own_req, decode
    )
    parts0 = split_sum(keep0, swap_each(give0, 1), rows, F32, 0)
    lines0 = [swap_pg(parts0[z], 4 * z, n_pg) for z in reversed(range(1, zs))]
    near1 = activate(own1, after(got1, parts0), 2)
    far1 = swap_units(near1)
    base = line_base(middle, dec_middle, parts0[0], after(lines0, near1), me_pg, own_req)
    keep1, *give1 = down(
        near1, after(far1, base), w_rows, [1, 3], picks, gates, me_kv, rows, own_req
    )
    parts1 = split_sum(keep1, swap_each(give1, 1), rows)
    mixed, squares = close(
        base, [swap_pg(parts1[z], 4 * z + 2, n_pg) for z in (0, 3, 2, 1)]
    )
    return last_norm(mixed, squares, swap_kv(squares), norm_gain_out)


def solution(mesh):
    fast = mesh.shape["kv"] == 2 and mesh.shape["pg"] == 16
    local = fast_local if fast else general_local
    in_specs = (
        P("pg", "kv"),
        P("pg", "kv"),
        P("pg", "kv"),
        P("pg", "kv", None, None),
        P(),
        P(),
        P("kv", None),
        P("kv"),
        P("kv"),
        P("pg", None),
        P("pg", None),
        P(),
        P("pg", "kv", None),
        P("pg", None, "kv"),
    )
    out_specs = P("pg", "kv")
    return jax.shard_map(local, mesh=mesh, in_specs=in_specs, out_specs=out_specs, check_vma=False)
```
